32 devices in a mesh: dp: 4 (over x, core), ctx: 8 (over z, y).
Axes of the slice: x: 2, y: 2, z: 4, core: 2. Of those that a mesh axis runs over, the one named last changes fastest.
Arguments:
- tokens: bfloat16 [16384, 1536], P(('dp', 'ctx')), may hold values from -6 to 6
- out_grad: bfloat16 [16384, 1536], P(('dp', 'ctx')), may hold values from -6 to 6
- seq_lengths: int32 [4, 3], P('dp'), may hold values from 1 to 4094, as said below
- norm_gain: bfloat16 [1536], P(('dp', 'ctx')), may hold values from 0.5 to 1.5
- in_weight: bfloat16 [1536, 6448], P(('dp', 'ctx')), may hold values from -0.15625 to 0.15625
- conv_weight: bfloat16 [4, 3328], P(None, ('dp', 'ctx')), may hold values from -3 to 3
- conv_bias: bfloat16 [3328], P(('dp', 'ctx')), may hold values from -3 to 3
- dt_bias: float32 [48], replicated, may hold values from -1 to 1
- a_log: float32 [48], replicated, as said below
- skip_gain: float32 [48], replicated, may hold values from 0.5 to 1.5
- gated_gain: bfloat16 [3072], P(('dp', 'ctx')), may hold values from 0.5 to 1.5
- out_weight: bfloat16 [3072, 1536], P(('dp', 'ctx')), may hold values from -0.109375 to 0.109375
Outputs:
- layer_out: bfloat16 [16384, 1536], P(('dp', 'ctx'))
- grad_tokens: float32 [16384, 1536], P(('dp', 'ctx'))
- grad_norm_gain: float32 [1536], P(('dp', 'ctx'))
- grad_in_weight: float32 [1536, 6448], P(('dp', 'ctx'))
- grad_conv_weight: float32 [4, 3328], P(None, ('dp', 'ctx'))
- grad_conv_bias: float32 [3328], P(('dp', 'ctx'))
- grad_dt_bias: float32 [48], replicated
- grad_a_log: float32 [48], replicated
- grad_skip_gain: float32 [48], replicated
- grad_gated_gain: float32 [3072], P(('dp', 'ctx'))
- grad_out_weight: float32 [3072, 1536], P(('dp', 'ctx'))
The draws below stay inside these ranges and needn't reach their ends.
Inputs may be any that keep to these rules, and one draw needn't show every extreme that they name: `seq_lengths`: row g holds three document lengths that sum to 4096 (4096 here); the first and the last are 1 to 511, so the middle document of every group starts on the group's first device and ends on its last; in one group, drawn from the seed, the first and the last are both 1. `a_log`: one value a head.
All inputs are finite; a program needn't handle non-finite values.
Results may differ from the reference program's by a relative error of at most 0.0021.
The reference program's roundings to bfloat16 on the way count: a program that leaves them out, or rounds other values in their place, can miss the bound.
Values may be sent and summed in bfloat16 or wider, within the bound.
No kernel may reach another device: no remote copies, remote signals or barrier semaphores. Data moves between devices by JAX's collectives and lax.ppermute only.
A program may use at most 256 MiB of HBM per device.

```python
import math
import jax
import jax.numpy as jnp
from jax import lax

D = 1536
HEADS = 48
HEAD_DIM = 64
STATE = 128
CONV_K = 4
SPAN = 256
TOK_DEV = 512
INNER = 3072
CONVW = 3328
PROJ = 6448
PACK = 4096
TOKENS = 16384
N_DP = 4
N_CTX = 8


def draw_seq_lengths(key, part):
    key = jax.random.fold_in(key, 11)
    first_key, last_key, pick_key = jax.random.split(key, 3)
    heads_len = jax.random.randint(first_key, (N_DP, 1), 1, TOK_DEV)
    tails_len = jax.random.randint(last_key, (N_DP, 1), 1, TOK_DEV)
    chosen = jax.random.randint(pick_key, (), 0, N_DP)
    marked = (jnp.arange(N_DP, dtype=jnp.int32) == chosen)[:, None]
    heads_len = jnp.where(marked, 1, heads_len)
    tails_len = jnp.where(marked, 1, tails_len)
    middle_len = PACK - heads_len - tails_len
    return jnp.concatenate([heads_len, middle_len, tails_len], axis=1).astype(jnp.int32)


def draw_a_log(key, part):
    key = jax.random.fold_in(key, 23)
    spots = jax.random.uniform(key, (HEADS,), jnp.float32)
    bottom = math.log(0.02 / PACK)
    summit = math.log(0.05)
    return (bottom + spots * (summit - bottom)).astype(jnp.float32)


def levels(key, dims, cuts, least, largest):
    loudness, own = 1.0, jax.random.fold_in(key, 6)
    for position, blocks in cuts:
        steps = jnp.exp(jax.random.uniform(jax.random.fold_in(own, position), (blocks,), jnp.float32, least / len(cuts), largest / len(cuts)))
        loudness = loudness * jnp.repeat(steps, dims[position] // blocks).reshape([-1 if axis == position else 1 for axis in range(len(dims))])
    return loudness


def gaussian(key, extent, width, bound, cuts=(), kind=jnp.bfloat16):
    loudness = levels(key, extent, cuts, -0.22, 0.18) if cuts else 1.0
    values = jax.random.normal(key, extent, jnp.float32) * width * loudness
    return jnp.minimum(jnp.maximum(values, -bound), bound).astype(kind)


def setup_inputs(seed: int = 0) -> dict:
    streams_of = jax.random.split(jax.random.key(seed), 13)
    tokens = gaussian(streams_of[0], (TOKENS, D), 1.0, 6.0, ((0, 32),))
    out_grad = gaussian(streams_of[1], (TOKENS, D), 1.0, 6.0, ((0, 32),))
    seq_lengths = draw_seq_lengths(jax.random.fold_in(streams_of[12], 71), 0)
    norm_gain = jnp.clip(1.0 + 0.1 * jax.random.normal(streams_of[3], (D,), jnp.float32), 0.5, 1.5).astype(jnp.bfloat16)
    in_weight = gaussian(streams_of[4], (D, PROJ), D ** -0.5, 0.15625, ((0, 32),))
    conv_weight = gaussian(streams_of[5], (CONV_K, CONVW), CONV_K ** -0.5, 3.0, ((1, 32),))
    conv_bias = gaussian(streams_of[6], (CONVW,), 0.5, 3.0, ((0, 32),))
    dt_bias = jnp.clip(jax.random.uniform(streams_of[7], (HEADS,), jnp.float32, -1.0, 1.0), -1.0, 1.0)
    a_log = draw_a_log(jax.random.fold_in(streams_of[12], 71), 0)
    skip_gain = jnp.clip(jax.random.uniform(streams_of[9], (HEADS,), jnp.float32, 0.5, 1.5), 0.5, 1.5)
    gated_gain = jnp.clip(1.0 + 0.1 * jax.random.normal(streams_of[10], (INNER,), jnp.float32), 0.5, 1.5).astype(jnp.bfloat16)
    out_weight = gaussian(streams_of[11], (INNER, D), INNER ** -0.5, 0.109375, ((0, 32),))
    return dict(tokens=tokens, out_grad=out_grad, seq_lengths=seq_lengths, norm_gain=norm_gain, in_weight=in_weight, conv_weight=conv_weight, conv_bias=conv_bias, dt_bias=dt_bias, a_log=a_log, skip_gain=skip_gain, gated_gain=gated_gain, out_weight=out_weight)


@jax.custom_vjp
def low(v):
    return lax.optimization_barrier(v.astype(jnp.bfloat16)).astype(jnp.float32)

@jax.custom_vjp
def low_back(v):
    return v

def low_keep(v):
    return (low(v), None)

def low_pass(kept, grad):
    return (grad,)

def back_keep(v):
    return (v, None)

def back_low(kept, grad):
    return (low(grad),)
low.defvjp(low_keep, low_pass)
low_back.defvjp(back_keep, back_low)
epsilon = 1e-05
highest = lax.Precision.HIGHEST

def rms_scale(values):
    return lax.rsqrt(lax.optimization_barrier(jnp.mean(values * values, axis=-1, keepdims=True)) + epsilon)

def span_step(carry_state, pieces):
    x_heads, b_rows, c_rows, steps_dt, log_decay, doc_ids, before = pieces
    row_total = doc_ids.shape[0]
    cumulative = jnp.cumsum(log_decay, axis=0).T
    ordinal = jnp.arange(row_total)
    allowed = (doc_ids[:, None] == doc_ids[None, :]) & (ordinal[:, None] >= ordinal[None, :])
    log_gaps = jnp.where(allowed[None], cumulative[:, :, None] - cumulative[:, None, :], 0.0)
    decays = jnp.where(allowed[None], jnp.exp(log_gaps), 0.0)
    scores = jnp.dot(c_rows, b_rows.T, precision=highest)
    mixing = scores[None] * decays * steps_dt.T[:, None, :]
    inside = jnp.einsum('hij,jhp->ihp', mixing, x_heads, precision=highest)
    alive_rows = (doc_ids == before).astype(jnp.float32)
    entering = jnp.exp(cumulative.T) * alive_rows[:, None]
    carry_term = jnp.einsum('hpn,in->ihp', carry_state, c_rows, precision=highest) * entering[:, :, None]
    tail_same = (doc_ids == doc_ids[-1]).astype(jnp.float32)
    weight_last = jnp.exp(cumulative[:, -1][None, :] - cumulative.T) * tail_same[:, None] * steps_dt
    fresh_state = jnp.einsum('jhp,jn->hpn', weight_last[:, :, None] * x_heads, b_rows, precision=highest)
    fading = jnp.exp(cumulative[:, -1]) * alive_rows[-1]
    return (fading[:, None, None] * carry_state + fresh_state, inside + carry_term)

def causal_conv(inputs, lead_rows, weight, bias_value, doc_ids, lead_docs):
    row_total = doc_ids.shape[0]
    padded = jnp.concatenate([lead_rows, inputs], axis=0)
    padded_docs = jnp.concatenate([lead_docs, doc_ids], axis=0)
    running = jnp.zeros_like(inputs) + bias_value[None, :]
    for offset in range(CONV_K):
        shifted = padded[offset:offset + row_total]
        same_doc = (padded_docs[offset:offset + row_total] == doc_ids).astype(jnp.float32)
        running = running + shifted * weight[offset][None, :] * same_doc[:, None]
    return running

def document_ids(lengths, positions):
    first_end = lengths[0]
    second_end = lengths[0] + lengths[1]
    return (positions >= first_end).astype(jnp.int32) + (positions >= second_end).astype(jnp.int32)

def pack_layer(rows_in, weights, doc_ids, span_before):
    gain_one, in_weight, conv_weight, conv_bias, dt_bias, a_log, skip_gain, gain_two, out_weight = weights
    row_total = rows_in.shape[0]
    normed = low(rows_in * rms_scale(rows_in) * gain_one[None, :])
    mixed = low_back(low(jnp.dot(normed, in_weight, precision=highest)))
    z_part = mixed[:, :INNER]
    x_part = mixed[:, INNER:INNER + CONVW]
    dt_part = mixed[:, INNER + CONVW:]
    lead_rows = jnp.zeros((CONV_K - 1, CONVW), mixed.dtype)
    lead_docs = jnp.full((CONV_K - 1,), -1, jnp.int32)
    active = jax.nn.silu(causal_conv(x_part, lead_rows, conv_weight, conv_bias, doc_ids, lead_docs))
    x_heads = active[:, :INNER].reshape(row_total, HEADS, HEAD_DIM)
    b_rows = active[:, INNER:INNER + STATE]
    c_rows = active[:, INNER + STATE:]
    steps_dt = jax.nn.softplus(dt_part + dt_bias[None, :])
    log_decay = -steps_dt * jnp.exp(a_log)[None, :]
    blocks = row_total // SPAN
    pieces = (x_heads.reshape(blocks, SPAN, HEADS, HEAD_DIM), b_rows.reshape(blocks, SPAN, STATE), c_rows.reshape(blocks, SPAN, STATE), steps_dt.reshape(blocks, SPAN, HEADS), log_decay.reshape(blocks, SPAN, HEADS), doc_ids.reshape(blocks, SPAN), span_before)
    start_state = jnp.zeros((HEADS, HEAD_DIM, STATE), mixed.dtype)
    last_state, outputs = lax.scan(jax.checkpoint(span_step), start_state, pieces)
    y_heads = outputs.reshape(row_total, HEADS, HEAD_DIM) + skip_gain[None, :, None] * x_heads
    gated = y_heads.reshape(row_total, INNER) * jax.nn.silu(z_part)
    final = low(gated * rms_scale(gated) * gain_two[None, :])
    return rows_in + jnp.dot(final, out_weight, precision=highest)

def reference(tokens, out_grad, seq_lengths, norm_gain, in_weight, conv_weight, conv_bias, dt_bias, a_log, skip_gain, gated_gain, out_weight):
    params = (norm_gain.astype(jnp.float32), in_weight.astype(jnp.float32), conv_weight.astype(jnp.float32), conv_bias.astype(jnp.float32), dt_bias.astype(jnp.float32), a_log.astype(jnp.float32), skip_gain.astype(jnp.float32), gated_gain.astype(jnp.float32), out_weight.astype(jnp.float32))
    pack_rows = TOK_DEV * N_CTX
    positions = jnp.arange(pack_rows, dtype=jnp.int32)

    def per_group(totals, element):
        rows_in, grad_rows, lengths = element
        doc_ids = document_ids(lengths, positions)
        span_before = jnp.concatenate([jnp.full((1,), -1, jnp.int32), doc_ids[SPAN - 1:-1:SPAN]])

        def forward(rows_value, weights):
            return pack_layer(rows_value, weights, doc_ids, span_before)
        result, back = jax.vjp(forward, rows_in.astype(jnp.float32), params)
        grad_rows_in, grad_params = back(grad_rows.astype(jnp.float32))
        totals = jax.tree.map(lambda left, right: left + right, totals, grad_params)
        return (totals, (result.astype(jnp.bfloat16), grad_rows_in))
    start_totals = jax.tree.map(jnp.zeros_like, params)
    totals, results = lax.scan(per_group, start_totals, (tokens.reshape(N_DP, pack_rows, D), out_grad.reshape(N_DP, pack_rows, D), seq_lengths))
    layer_out = results[0].reshape(-1, D)
    grad_tokens = results[1].reshape(-1, D)
    return (layer_out, grad_tokens, totals[0], totals[1], totals[2], totals[3], totals[4], totals[5], totals[6], totals[7], totals[8])
```

```python
import functools

import jax
import jax.numpy as jnp
from jax import lax
from jax.experimental import pallas as pl
from jax.experimental.pallas import tpu as pltpu
from jax.sharding import Mesh, PartitionSpec as P

HEADS = 48
HEAD_DIM = 64
STATE = 128
CONV_K = 4
INNER = 3072
CONVW = 3328
LEAD = 16
BLOCK = 512
BLOCK_HEADS = BLOCK // HEAD_DIM
PAIRS = 2
PAIR_LANES = 128 * PAIRS
VMEM = 56 * 1024 * 1024
F32 = jnp.float32
BF = jnp.bfloat16
EPS = 1e-05
highest = lax.Precision.HIGHEST
EVERY = ("x", "core", "z", "y")
CTX = ("z", "y")


def params():
    return pltpu.CompilerParams(vmem_limit_bytes=VMEM, dimension_semantics=("arbitrary",))


def call(body, grid, ins, outs, scratch=()):
    in_specs = [spec for _, spec in ins]
    return pl.pallas_call(
        body,
        grid=(grid,),
        in_specs=in_specs,
        out_specs=[spec for _, spec in outs],
        out_shape=[shape for shape, _ in outs],
        scratch_shapes=list(scratch),
        compiler_params=params(),
    )(*[array for array, _ in ins])


def whole(*shape):
    return pl.BlockSpec(shape, lambda g: (0,) * len(shape))


def lanes(rows, width):
    return pl.BlockSpec((rows, width), lambda g: (0, g))


def rows_of(count, width):
    return pl.BlockSpec((count, width), lambda g: (g, 0))


def group(rows, width):
    return pl.BlockSpec((1, rows, width), lambda g: (g, 0, 0))


def out(shape, dtype=F32):
    return jax.ShapeDtypeStruct(shape, dtype)


def split(value):
    high = value.astype(BF)
    return high, (value - high.astype(F32)).astype(BF)


def mm(left, right):
    return jnp.dot(left, right, preferred_element_type=F32)


def mm_nt(left, right):
    return lax.dot_general(left, right, (((1,), (1,)), ((), ())), preferred_element_type=F32)


def mm_tn(left, right):
    return lax.dot_general(left, right, (((0,), (0,)), ((), ())), preferred_element_type=F32)


def three(product, left, right):
    left_high, left_low = left
    right_high, right_low = right
    return (
        product(left_high, right_high)
        + product(left_high, right_low)
        + product(left_low, right_high)
    )


def head_of_lane(first, count):
    lane = lax.broadcasted_iota(jnp.int32, (STATE, count), 1) // HEAD_DIM + first
    row = lax.broadcasted_iota(jnp.int32, (STATE, count), 0)
    return (lane == row).astype(BF)


def expand(value, places):
    high, low = split(value)
    return mm(high, places) + mm(low, places)


def fold(value, places):
    high, low = split(value)
    return mm_nt(high, places) + mm_nt(low, places)


def sigmoid(value):
    return 1.0 / (1.0 + jnp.exp(-value))


def conv_pre(extended, weight, bias, masks):
    running = jnp.zeros((masks.shape[0], extended.shape[1]), F32) + bias
    for tap in range(CONV_K):
        shifted = extended if tap == CONV_K - 1 else pltpu.roll(extended, CONV_K - 1 - tap, 0)
        running = running + shifted[LEAD:] * weight[tap : tap + 1] * masks[:, tap : tap + 1]
    return running


def conv_back(d_pre, extended, weight, masks):
    zeros = jnp.zeros((LEAD, d_pre.shape[1]), F32)
    total = LEAD + d_pre.shape[0]
    d_ext = jnp.zeros((total, d_pre.shape[1]), F32)
    weight_rows = []
    for tap in range(CONV_K):
        by = CONV_K - 1 - tap
        part = d_pre * masks[:, tap : tap + 1]
        padded = jnp.concatenate([zeros, part], axis=0)
        shifted = extended
        if by:
            padded = pltpu.roll(padded, total - by, 0)
            shifted = pltpu.roll(extended, by, 0)
        d_ext = d_ext + padded * weight[tap : tap + 1]
        weight_rows.append(jnp.sum(shifted[LEAD:] * part, axis=0, keepdims=True))
    weight_rows.append(jnp.sum(d_pre, axis=0, keepdims=True))
    weight_rows.append(jnp.zeros((8 - len(weight_rows), d_pre.shape[1]), F32))
    return d_ext, jnp.concatenate(weight_rows, axis=0)


def same_mask(doc_row, doc_col, transposed):
    count = doc_row.shape[1]
    rows = lax.broadcasted_iota(jnp.int32, (count, count), 0)
    cols = lax.broadcasted_iota(jnp.int32, (count, count), 1)
    order = rows <= cols if transposed else rows >= cols
    return jnp.where((doc_row == doc_col) & order, 1.0, 0.0)


def prep_bc_body(x_ref, w_ref, b_ref, m_ref, doc_ref, pre_ref, act_ref, t_ref, s_ref, st_ref):
    masks = m_ref[...]
    pre = conv_pre(x_ref[...].astype(F32), w_ref[...], b_ref[...], masks)
    act = pre * sigmoid(pre)
    pre_ref[...] = pre
    act_ref[...] = act
    t_ref[...] = act.T
    b_rows, c_rows = split(act[:, :STATE]), split(act[:, STATE:])
    doc_row, doc_col = doc_ref[0:1], masks[:, CONV_K : CONV_K + 1]
    s_ref[...] = three(mm_nt, c_rows, b_rows) * same_mask(doc_row, doc_col, False)
    st_ref[...] = three(mm_nt, b_rows, c_rows) * same_mask(doc_row, doc_col, True)


def prep_x_body(x_ref, w_ref, b_ref, m_ref, wl_ref, t_ref, pre_ref, act_ref, state_ref):
    pre = conv_pre(x_ref[...].astype(F32), w_ref[...], b_ref[...], m_ref[...])
    act = pre * sigmoid(pre)
    pre_ref[...] = pre
    act_ref[...] = act
    places = head_of_lane(pl.program_id(0) * BLOCK_HEADS, BLOCK)
    weighted = split(act * expand(wl_ref[...], places))
    state_ref[...] = three(mm, split(t_ref[:STATE]), weighted)


def intra_body(x_ref, dt_ref, skip_ref, s_ref, col_ref, row_ref, y_ref):
    half = s_ref.shape[0] // 2
    places = head_of_lane(pl.program_id(0) * 2 * PAIRS, PAIR_LANES)
    scaled = x_ref[...] * expand(dt_ref[...], places)
    lane = lax.broadcasted_iota(jnp.int32, (2 * half, 128), 1)
    for pair in range(PAIRS):
        here = slice(pair * 128, pair * 128 + 128)
        high, low = split(scaled[:, here])
        right = jnp.concatenate([high, low], axis=1)
        both = []
        for side in range(2):
            head = 2 * pair + side
            col = col_ref[0, :, head : head + 1]
            row = row_ref[0, head : head + 1, :]
            top = s_ref[:half, :half] * jnp.exp(jnp.minimum(col[:half] - row[:, :half], 0.0))
            low_part = s_ref[half:, :] * jnp.exp(jnp.minimum(col[half:] - row, 0.0))
            done = []
            for part, count in ((top, half), (low_part, 2 * half)):
                p_high, p_low = split(part)
                first = mm(p_high, right[:count])
                done.append(first[:, :128] + first[:, 128:] + mm(p_low, high[:count]))
            both.append(jnp.concatenate(done, axis=0))
        y_ref[:, here] = (
            jnp.where(lane < HEAD_DIM, both[0], both[1]) + skip_ref[:, here] * x_ref[:, here]
        )


def gate_body(
    y_ref, z_ref, df_ref, x_ref, c_ref, ct_ref, state_ref, e_ref, gain_ref, skip_ref,
    final_ref, dz_ref, dy_ref, r_ref, dc_ref, q_ref, sums_ref, carry, scaled,
):
    @pl.when(pl.program_id(0) == 0)
    def _():
        r_ref[...] = jnp.zeros_like(r_ref)
        sums_ref[...] = jnp.zeros_like(sums_ref)

    e_high, e_low = split(e_ref[...])
    c_rows = split(c_ref[...])
    for block in range(INNER // BLOCK):
        here = slice(block * BLOCK, block * BLOCK + BLOCK)
        places = head_of_lane(block * BLOCK_HEADS, BLOCK)
        spread = mm(e_high, places) + mm(e_low, places)
        carry[:, here] = three(mm, c_rows, split(state_ref[:, here])) * spread
        scaled[:, here] = spread
    gain, skip = gain_ref[...], skip_ref[...]

    def some(lap, sums):
        at = pl.ds(pl.multiple_of(lap * 16, 16), 16)
        y = y_ref[at, :] + carry[at, :]
        z = z_ref[at, :].astype(F32)
        sig = sigmoid(z)
        gate = z * sig
        gated = y * gate
        scale = lax.rsqrt(jnp.mean(gated * gated, axis=-1, keepdims=True) + EPS)
        unit = gated * scale
        final_ref[at, :] = (unit * gain).astype(BF)
        d_final = df_ref[at, :]
        q = d_final * gain
        inner = jnp.mean(q * unit, axis=-1, keepdims=True)
        d_gated = scale * (q - unit * inner)
        d_y = d_gated * gate
        dz_ref[at, :] = (d_gated * y * (sig * (1.0 + z * (1.0 - sig)))).astype(BF)
        dy_ref[at, :] = d_y
        x = x_ref[at, :]
        scaled[at, :] = scaled[at, :] * d_y
        carry[at, :] = d_y * (y - skip * x)
        d_gain, d_skip = d_final * unit, d_y * x
        return (
            sums[0] + d_gain[:8] + d_gain[8:],
            sums[1] + d_skip[:8] + d_skip[8:],
        )

    zero = jnp.zeros((8, INNER), F32)
    d_gain, d_skip = lax.fori_loop(0, y_ref.shape[0] // 16, some, (zero, zero))
    sums_ref[0:8] += d_gain
    sums_ref[8:16] += d_skip
    ct_rows = split(ct_ref[...])
    d_c = jnp.zeros(dc_ref.shape, F32)
    q_sum = jnp.zeros(q_ref.shape, F32)
    for block in range(INNER // BLOCK):
        here = slice(block * BLOCK, block * BLOCK + BLOCK)
        piece = split(scaled[:, here])
        r_ref[:, here] += three(mm, ct_rows, piece)
        d_c = d_c + three(mm_nt, piece, split(state_ref[:, here]))
        q_sum = q_sum + fold(carry[:, here], head_of_lane(block * BLOCK_HEADS, BLOCK))
    dc_ref[...] = d_c
    q_ref[...] = q_sum


def back_body(x_ref, dy_ref, dt_ref, st_ref, col_ref, row_ref, bc_ref, doc_ref, m_ref, dx_ref, dbc_ref, acc):
    step = pl.program_id(0)
    half = st_ref.shape[0] // 2

    @pl.when(step == 0)
    def _():
        acc[...] = jnp.zeros_like(acc)

    places = head_of_lane(step * 2 * PAIRS, PAIR_LANES)
    scaled = x_ref[...] * expand(dt_ref[...], places)
    lane = lax.broadcasted_iota(jnp.int32, (2 * half, 128), 1)
    for pair in range(PAIRS):
        here = slice(pair * 128, pair * 128 + 128)
        dy_high, dy_low = split(dy_ref[:, here])
        right = jnp.concatenate([dy_high, dy_low], axis=1)
        twice = jnp.concatenate([dy_high, dy_high], axis=1)
        both = []
        for side in range(2):
            head = 2 * pair + side
            mine = (lane < HEAD_DIM) if side == 0 else (lane >= HEAD_DIM)
            x_high, x_low = split(jnp.where(mine, scaled[:, here], 0.0))
            x_both = jnp.concatenate([x_high, x_low], axis=1)
            col = col_ref[0, :, head : head + 1]
            row = row_ref[0, head : head + 1, :]
            done = []
            for at, over in ((slice(0, half), slice(0, 2 * half)), (slice(half, 2 * half), slice(half, 2 * half))):
                decay = jnp.exp(jnp.minimum(row[:, over] - col[at], 0.0))
                p_high, p_low = split(st_ref[at, over] * decay)
                first = mm(p_high, right[over])
                done.append(first[:, :128] + first[:, 128:] + mm(p_low, dy_high[over]))
                outer = mm_nt(x_both[at], twice[over]) + mm_nt(x_high[at], dy_low[over])
                acc[at, over] += outer * decay
            both.append(jnp.concatenate(done, axis=0))
        dx_ref[:, here] = jnp.where(lane < HEAD_DIM, both[0], both[1])

    @pl.when(step == pl.num_programs(0) - 1)
    def _():
        doc_col = m_ref[:, CONV_K : CONV_K + 1]
        ds = split(acc[...] * same_mask(doc_ref[0:1], doc_col, True))
        dbc_ref[:, :STATE] = three(mm, ds, split(bc_ref[:, STATE:]))
        dbc_ref[:, STATE:] = three(mm_tn, ds, split(bc_ref[:, :STATE]))


def carry_body(
    dx_ref, x_ref, dy_ref, pre_ref, in_ref, w_ref, m_ref, bc_ref, r_ref, end_ref, wl_ref, dt_ref, skip_ref,
    d_ref, edge_ref, conv_ref, db_ref, g_ref,
):
    step = pl.program_id(0)

    @pl.when(step == 0)
    def _():
        db_ref[...] = jnp.zeros_like(db_ref)
        g_ref[...] = jnp.zeros_like(g_ref)

    places = head_of_lane(step * BLOCK_HEADS, BLOCK)
    returned = r_ref[...]
    r_parts = split(returned)
    to_end = expand(wl_ref[...], places)
    steps = expand(dt_ref[...], places)
    x = x_ref[...]
    d_scaled = dx_ref[...] + to_end * three(mm, split(bc_ref[:, :STATE]), r_parts)
    g_ref[...] += fold(x * d_scaled, places)
    db_ref[...] += three(mm_nt, split(to_end * steps * x), r_parts)
    d_x = steps * d_scaled + skip_ref[...] * dy_ref[...]
    pre = pre_ref[...]
    sig = sigmoid(pre)
    d_pre = d_x * (sig * (1.0 + pre * (1.0 - sig)))
    d_ext, sums = conv_back(d_pre, in_ref[...].astype(F32), w_ref[...], m_ref[...])
    d_ref[...] = d_ext[LEAD:].astype(BF)
    edge_ref[:LEAD] = d_ext[:LEAD]
    edge_ref[LEAD:] = d_ext[d_ext.shape[0] - LEAD :]
    flow = jnp.sum(returned * end_ref[...], axis=0, keepdims=True)
    row = lax.broadcasted_iota(jnp.int32, sums.shape, 0)
    conv_ref[...] = jnp.where(row == CONV_K + 1, flow, sums)


def carry_bc_body(d_ref, pre_ref, in_ref, w_ref, m_ref, o_ref, edge_ref, conv_ref):
    pre = pre_ref[...]
    sig = sigmoid(pre)
    d_pre = d_ref[...] * (sig * (1.0 + pre * (1.0 - sig)))
    d_ext, sums = conv_back(d_pre, in_ref[...].astype(F32), w_ref[...], m_ref[...])
    o_ref[...] = d_ext[LEAD:].astype(BF)
    edge_ref[:LEAD] = d_ext[:LEAD]
    edge_ref[LEAD:] = d_ext[d_ext.shape[0] - LEAD :]
    conv_ref[...] = sums


def swap(array, axis):
    return lax.ppermute(array, axis, [(0, 1), (1, 0)])


def from_behind(array, by):
    peers = lax.axis_size(CTX[0]) * lax.axis_size(CTX[1])
    pairs = [(i, i + by) for i in range(peers) if 0 <= i + by < peers]
    return lax.ppermute(array, CTX, pairs)


def entering(state, decay, reverse):
    depth, width = lax.axis_size("z"), lax.axis_size("y")
    place_z, place_y = lax.axis_index("z"), lax.axis_index("y")
    if width != 2:
        both = jnp.concatenate([state, jnp.broadcast_to(decay, (8, decay.shape[1]))], axis=0)
        gathered = lax.all_gather(both, CTX)
        count = depth * width
        place = place_z * width + place_y
        ahead = count - 1 - place if reverse else place

        def one(lap, running):
            source = count - 1 - lap if reverse else lap
            item = lax.dynamic_index_in_dim(gathered, source, 0, False)
            return item[STATE : STATE + 1] * running + item[:STATE]

        return lax.fori_loop(0, ahead, one, jnp.zeros_like(state))
    half = state.shape[1] // 2
    second = place_y == (0 if reverse else 1)
    own = lax.dynamic_slice_in_dim(state, place_y * half, half, 1)
    other = lax.dynamic_slice_in_dim(state, (1 - place_y) * half, half, 1)
    got = swap(other, "y")
    decay_own = lax.dynamic_slice_in_dim(decay, place_y * half, half, 1)
    decay_got = swap(lax.dynamic_slice_in_dim(decay, (1 - place_y) * half, half, 1), "y")
    early = jnp.where(second, got, own)
    late = jnp.where(second, own, got)
    decay_early = jnp.where(second, decay_got, decay_own)
    decay_late = jnp.where(second, decay_own, decay_got)
    total = decay_late * early + late
    decay_total = decay_early * decay_late
    before = jnp.zeros_like(total)
    sent = total
    for hop in range(1, depth):
        pair = (depth - hop, depth - 1 - hop) if reverse else (hop - 1, hop)
        before = before + lax.ppermute(sent, "z", [pair])
        sent = decay_total * before + total
    middle = decay_early * before + early
    mine = jnp.where(second, middle, before)
    theirs = swap(jnp.where(second, before, middle), "y")
    return jnp.where(
        place_y == 0,
        jnp.concatenate([mine, theirs], axis=1),
        jnp.concatenate([theirs, mine], axis=1),
    )


def line_sum(parts, axis):
    count, place = lax.axis_size(axis), lax.axis_index(axis)

    def pick(i):
        return lax.dynamic_index_in_dim(parts, jnp.clip(i, 0, count - 1), 0, False)

    up, down = pick(count - 1), pick(0)
    for step in range(1, count):
        got_up = lax.ppermute(up, axis, [(i, i + 1) for i in range(step)])
        got_down = lax.ppermute(down, axis, [(count - 1 - i, count - 2 - i) for i in range(step)])
        if step < count - 1:
            up = pick(count - step - 1 + place) + got_up
            down = pick(place - (count - step - 1)) + got_down
    return pick(place) + got_up + got_down


def pair_sum(parts, axis):
    if lax.axis_size(axis) != 2:
        return line_sum(parts, axis)
    place = lax.axis_index(axis)
    sent = lax.dynamic_index_in_dim(parts, 1 - place, 0, False).astype(BF)
    kept = lax.dynamic_index_in_dim(parts, place, 0, False)
    return kept + swap(sent, axis).astype(F32)


def scatter_sum(partial, x_first):
    sizes = [lax.axis_size(a) for a in ("x", "z", "y")]
    count = partial.shape[0] // (sizes[0] * sizes[1] * sizes[2])
    parts = partial.reshape(*sizes, count, partial.shape[1])
    if x_first:
        parts = pair_sum(parts, "x")
        parts = pair_sum(jnp.moveaxis(parts, 1, 0), "y")
    else:
        parts = pair_sum(jnp.moveaxis(parts, 2, 0), "y")
        parts = pair_sum(parts, "x")
    return line_sum(parts, "z")


def own_rows(array, core):
    sizes = lax.axis_size("x")
    view = array.reshape(array.shape[0], sizes, 2, -1)
    return lax.dynamic_index_in_dim(view, core, 2, False).reshape(array.shape[0], -1)


def document_ids(lengths, positions):
    first_end = lengths[0]
    second_end = lengths[0] + lengths[1]
    inside = (positions >= first_end).astype(jnp.int32) + (positions >= second_end).astype(jnp.int32)
    return jnp.where(positions < 0, -1, inside)


def gather_small(pieces, count):
    flat = jnp.concatenate([piece.reshape(-1) for piece in pieces])
    spread = jnp.broadcast_to(flat[None], (count, flat.shape[0]))
    return lax.all_to_all(spread, EVERY, 0, 0, tiled=True)


def columns(array, width):
    return jnp.pad(array, ((0, 0), (0, width - array.shape[1])))


def shards(
    tokens, out_grad, seq_lengths, norm_gain, in_weight, conv_weight, conv_bias,
    dt_bias, a_log, skip_gain, gated_gain, out_weight,
):
    count = 1
    for axis in EVERY:
        count *= lax.axis_size(axis)
    core = lax.axis_index("core")
    place = lax.axis_index("z") * lax.axis_size("y") + lax.axis_index("y")
    row_count = tokens.shape[0]
    width = tokens.shape[1]
    first_row = place * row_count

    lengths = seq_lengths[0]
    ordinal = jnp.arange(row_count, dtype=jnp.int32)
    doc_ids = document_ids(lengths, first_row + ordinal)
    doc_before = document_ids(lengths, first_row - 1 + jnp.zeros((1,), jnp.int32))
    marks = [
        (document_ids(lengths, first_row + ordinal - (CONV_K - 1 - tap)) == doc_ids).astype(F32)
        for tap in range(CONV_K)
    ]
    keep = marks[CONV_K - 2]
    masks = columns(jnp.stack(marks + [doc_ids.astype(F32)], axis=1), 128)
    doc_rows = jnp.broadcast_to(doc_ids.astype(F32)[None], (8, row_count))
    alive = (doc_ids == doc_before[0]).astype(F32)
    tail = (doc_ids == doc_ids[row_count - 1]).astype(F32)

    lead_tokens = from_behind(tokens[row_count - LEAD :], 1)
    small = gather_small([norm_gain, conv_weight, conv_bias, gated_gain], count)
    cuts = [norm_gain.size, conv_weight.size, conv_bias.size]
    cuts = [sum(cuts[: i + 1]) for i in range(3)]
    gain_piece, conv_piece, bias_piece, gated_piece = jnp.split(small, cuts, axis=1)
    full_gain = gain_piece.reshape(1, -1).astype(F32)
    full_conv = jnp.moveaxis(conv_piece.reshape(count, CONV_K, -1), 1, 0).reshape(CONV_K, -1)
    full_conv = jnp.pad(full_conv.astype(F32), ((0, 4), (0, 0)))
    full_bias = bias_piece.reshape(1, -1).astype(F32)
    full_gated = gated_piece.reshape(1, -1).astype(F32)
    weight_x = lax.all_gather(in_weight[:, INNER:], EVERY, axis=0, tiled=True)
    weight_z = lax.all_gather(in_weight[:, :INNER], EVERY, axis=0, tiled=True)
    weight_o = lax.all_gather(out_weight, EVERY, axis=0, tiled=True)

    extended = jnp.concatenate([lead_tokens, tokens], axis=0).astype(F32)
    rms = lax.rsqrt(jnp.mean(extended * extended, axis=-1, keepdims=True) + EPS)
    normed_ext = (extended * rms * full_gain).astype(BF)
    normed = normed_ext[LEAD:]
    mixed_x = mm(normed_ext, weight_x).astype(BF)
    mixed_xs = mixed_x[:, :INNER]
    mixed_bc = mixed_x[:, INNER:CONVW]
    shifted_dt = mixed_x[LEAD:, CONVW:].astype(F32) + dt_bias[None]

    steps = jax.nn.softplus(shifted_dt)
    rate = jnp.exp(a_log)[None]
    log_decay = -steps * rate
    lower = (ordinal[:, None] >= ordinal[None, :]).astype(F32)
    cumulative = jnp.dot(lower, log_decay, precision=highest)
    last = cumulative[row_count - 1 :]
    enter = jnp.exp(cumulative) * alive[:, None]
    to_end = jnp.exp(last - cumulative) * tail[:, None]
    device_decay = jnp.repeat(enter[row_count - 1 :], HEAD_DIM, axis=1)
    steps_wide = columns(steps, 128)
    enter_wide = columns(enter, 128)
    to_end_wide = columns(to_end, 128)
    weights_wide = columns(to_end * steps, 128)
    heads_block = 2 * PAIRS
    groups = HEADS // heads_block
    cum_cols = jnp.moveaxis(cumulative.reshape(row_count, groups, heads_block), 1, 0)
    cum_rows = cumulative.T.reshape(groups, heads_block, row_count)
    skip_wide = jnp.repeat(skip_gain, HEAD_DIM)[None]

    bc_width = CONVW - INNER
    full_rows = LEAD + row_count
    square = (row_count, row_count)
    pre_bc, act_bc, act_t, scores, scores_t = call(
        prep_bc_body, 1,
        [
            (mixed_bc, whole(full_rows, bc_width)),
            (full_conv[:, INNER:], whole(8, bc_width)),
            (full_bias[:, INNER:], whole(1, bc_width)),
            (masks, whole(row_count, 128)),
            (doc_rows, whole(8, row_count)),
        ],
        [
            (out((row_count, bc_width)), whole(row_count, bc_width)),
            (out((row_count, bc_width)), whole(row_count, bc_width)),
            (out((bc_width, row_count)), whole(bc_width, row_count)),
            (out(square), whole(*square)),
            (out(square), whole(*square)),
        ],
    )
    pre_x, act_x, state_local = call(
        prep_x_body, INNER // BLOCK,
        [
            (mixed_xs, lanes(full_rows, BLOCK)),
            (full_conv[:, :INNER], lanes(8, BLOCK)),
            (full_bias[:, :INNER], lanes(1, BLOCK)),
            (masks, whole(row_count, 128)),
            (weights_wide, whole(row_count, 128)),
            (act_t, whole(bc_width, row_count)),
        ],
        [
            (out((row_count, INNER)), lanes(row_count, BLOCK)),
            (out((row_count, INNER)), lanes(row_count, BLOCK)),
            (out((STATE, INNER)), lanes(STATE, BLOCK)),
        ],
    )
    state_in = entering(state_local, device_decay, False)
    state_end = device_decay * state_in + state_local

    y_local = call(
        intra_body, groups,
        [
            (act_x, lanes(row_count, PAIR_LANES)),
            (steps_wide, whole(row_count, 128)),
            (skip_wide, lanes(1, PAIR_LANES)),
            (scores, whole(*square)),
            (cum_cols, group(row_count, heads_block)),
            (cum_rows, group(heads_block, row_count)),
        ],
        [(out((row_count, INNER)), lanes(row_count, PAIR_LANES))],
    )[0]
    mixed_z = mm(normed, weight_z).astype(BF)
    d_final = mm_nt(out_grad, weight_o)

    tile = 128
    c_rows = act_bc[:, STATE:]
    c_cols = act_t[STATE:]
    final, d_z, d_y, returned_local, d_c_carry, dy_y, sums = call(
        gate_body, row_count // tile,
        [
            (y_local, rows_of(tile, INNER)),
            (mixed_z, rows_of(tile, INNER)),
            (d_final, rows_of(tile, INNER)),
            (act_x, rows_of(tile, INNER)),
            (c_rows, rows_of(tile, STATE)),
            (c_cols, lanes(STATE, tile)),
            (state_in, whole(STATE, INNER)),
            (enter_wide, rows_of(tile, 128)),
            (full_gated, whole(1, INNER)),
            (skip_wide, whole(1, INNER)),
        ],
        [
            (out((row_count, INNER), BF), rows_of(tile, INNER)),
            (out((row_count, INNER), BF), rows_of(tile, INNER)),
            (out((row_count, INNER)), rows_of(tile, INNER)),
            (out((STATE, INNER)), whole(STATE, INNER)),
            (out((row_count, STATE)), rows_of(tile, STATE)),
            (out((row_count, 128)), rows_of(tile, 128)),
            (out((16, INNER)), whole(16, INNER)),
        ],
        [pltpu.VMEM((tile, INNER), F32), pltpu.VMEM((tile, INNER), F32)],
    )
    returned = entering(returned_local, device_decay, True)

    layer_out = (tokens.astype(F32) + mm(final, weight_o)).astype(BF)
    final_mine = jnp.concatenate([own_rows(final, core), swap(own_rows(final, 1 - core), "core")], axis=0)
    out_grad_both = jnp.concatenate([out_grad, swap(out_grad, "core")], axis=0)
    normed_mine = jnp.concatenate([own_rows(normed, core), swap(own_rows(normed, 1 - core), "core")], axis=0)

    def reduce_columns(left, right):
        middle = right.shape[1] // 256 * 128
        return jnp.concatenate(
            [
                scatter_sum(mm_tn(left, right[:, :middle]), True),
                scatter_sum(mm_tn(left, right[:, middle:]), False),
            ],
            axis=1,
        )

    sum_out = reduce_columns(final_mine, out_grad_both)
    d_z_both = jnp.concatenate([d_z, swap(d_z, "core")], axis=0)
    sum_in_z = reduce_columns(normed_mine, d_z_both)

    d_scaled, d_bc = call(
        back_body, groups,
        [
            (act_x, lanes(row_count, PAIR_LANES)),
            (d_y, lanes(row_count, PAIR_LANES)),
            (steps_wide, whole(row_count, 128)),
            (scores_t, whole(*square)),
            (cum_cols, group(row_count, heads_block)),
            (cum_rows, group(heads_block, row_count)),
            (act_bc, whole(row_count, bc_width)),
            (doc_rows, whole(8, row_count)),
            (masks, whole(row_count, 128)),
        ],
        [
            (out((row_count, INNER)), lanes(row_count, PAIR_LANES)),
            (out((row_count, bc_width)), whole(row_count, bc_width)),
        ],
        [pltpu.VMEM(square, F32)],
    )

    d_xs, edge_x, conv_x, d_b_carry, x_dx = call(
        carry_body, INNER // BLOCK,
        [
            (d_scaled, lanes(row_count, BLOCK)),
            (act_x, lanes(row_count, BLOCK)),
            (d_y, lanes(row_count, BLOCK)),
            (pre_x, lanes(row_count, BLOCK)),
            (mixed_xs, lanes(full_rows, BLOCK)),
            (full_conv[:, :INNER], lanes(8, BLOCK)),
            (masks, whole(row_count, 128)),
            (act_bc, whole(row_count, bc_width)),
            (returned, lanes(STATE, BLOCK)),
            (state_end, lanes(STATE, BLOCK)),
            (to_end_wide, whole(row_count, 128)),
            (steps_wide, whole(row_count, 128)),
            (skip_wide, lanes(1, BLOCK)),
        ],
        [
            (out((row_count, INNER), BF), lanes(row_count, BLOCK)),
            (out((2 * LEAD, INNER)), lanes(2 * LEAD, BLOCK)),
            (out((8, INNER)), lanes(8, BLOCK)),
            (out((row_count, STATE)), whole(row_count, STATE)),
            (out((row_count, 128)), whole(row_count, 128)),
        ],
    )
    d_bc = d_bc + jnp.concatenate([d_b_carry, d_c_carry], axis=1)
    d_bc_low, edge_bc, conv_bc = call(
        carry_bc_body, 1,
        [
            (d_bc, whole(row_count, bc_width)),
            (pre_bc, whole(row_count, bc_width)),
            (mixed_bc, whole(full_rows, bc_width)),
            (full_conv[:, INNER:], whole(8, bc_width)),
            (masks, whole(row_count, 128)),
        ],
        [
            (out((row_count, bc_width), BF), whole(row_count, bc_width)),
            (out((2 * LEAD, bc_width)), whole(2 * LEAD, bc_width)),
            (out((8, bc_width)), whole(8, bc_width)),
        ],
    )
    conv_sums = jnp.concatenate([conv_x, conv_bc], axis=1)
    edges = jnp.concatenate([edge_x, edge_bc], axis=1)
    d_last = edges[LEAD:] + from_behind(edges[:LEAD], -1)

    x_dx = x_dx[:, :HEADS]
    flow = jnp.sum(conv_x[CONV_K + 1].reshape(HEADS, HEAD_DIM), axis=1)
    difference = dy_y[:, :HEADS] - steps * x_dx
    upper = (ordinal[:, None] <= ordinal[None, :]).astype(F32)
    d_log_decay = (flow[None] + jnp.dot(upper, difference, precision=highest)) * keep[:, None]
    d_steps = x_dx - rate * d_log_decay
    d_dt = d_steps * jax.nn.sigmoid(shifted_dt)
    grad_a_log = -jnp.sum(steps * rate * d_log_decay, axis=0)
    grad_dt_bias = jnp.sum(d_dt, axis=0)
    grad_skip = jnp.sum(jnp.sum(sums[8:], axis=0).reshape(HEADS, HEAD_DIM), axis=1)
    grad_gated = jnp.sum(sums[:8], axis=0)

    d_xr = jnp.concatenate([d_xs, d_bc_low], axis=1)
    d_xr = lax.dynamic_update_slice_in_dim(d_xr, d_last.astype(BF), row_count - LEAD, 0)
    d_x = jnp.concatenate([d_xr, d_dt.astype(BF)], axis=1)
    d_x_both = jnp.concatenate([d_x, swap(d_x, "core")], axis=0)
    sum_in_x = reduce_columns(normed_mine, d_x_both)
    d_normed = mm_nt(d_z, weight_z) + mm_nt(d_x, weight_x)

    rows_value, scale = extended[LEAD:], rms[LEAD:]
    unit = rows_value * scale
    pulled = d_normed * full_gain
    d_rows = scale * (pulled - unit * jnp.mean(pulled * unit, axis=-1, keepdims=True))
    grad_tokens = out_grad.astype(F32) + d_rows
    grad_gain = jnp.sum(d_normed * unit, axis=0)

    per_device = jnp.concatenate(
        [
            grad_gain.reshape(count, -1),
            jnp.moveaxis(conv_sums[:CONV_K].reshape(CONV_K, count, -1), 1, 0).reshape(count, -1),
            conv_sums[CONV_K].reshape(count, -1),
            grad_gated.reshape(count, -1),
            jnp.broadcast_to(
                jnp.concatenate([grad_dt_bias, grad_a_log, grad_skip])[None], (count, 3 * HEADS)
            ),
        ],
        axis=1,
    )
    small_sums = jnp.sum(lax.all_to_all(per_device, EVERY, 0, 0, tiled=True), axis=0)
    cuts = [norm_gain.size, conv_weight.size, conv_bias.size, gated_gain.size, HEADS, HEADS]
    cuts = [sum(cuts[: i + 1]) for i in range(6)]
    sum_gain, sum_conv, sum_bias, sum_gated, sum_dt, sum_log, sum_skip = jnp.split(small_sums, cuts)
    return (
        layer_out,
        grad_tokens,
        sum_gain,
        jnp.concatenate([sum_in_z, sum_in_x], axis=1),
        sum_conv.reshape(conv_weight.shape),
        sum_bias,
        sum_dt,
        sum_log,
        sum_skip,
        sum_gated,
        sum_out,
    )


def solution(mesh):
    x = mesh.shape["dp"] // 2
    y = x
    z = mesh.shape["ctx"] // y
    fine = Mesh(mesh.devices.reshape(x, 2, z, y), EVERY)
    rows = P(EVERY, None)
    flat = P(EVERY)
    in_specs = (
        rows, rows, P(("x", "core"), None), flat, rows, P(None, EVERY), flat,
        P(), P(), P(), flat, rows,
    )
    out_specs = (rows, rows, flat, rows, P(None, EVERY), flat, P(), P(), P(), flat, rows)
    return jax.shard_map(shards, mesh=fine, in_specs=in_specs, out_specs=out_specs, check_vma=False)
```

```python
import functools

import jax
import jax.numpy as jnp
from jax import lax
from jax.experimental import pallas as pl
from jax.experimental.pallas import tpu as pltpu
from jax.sharding import Mesh, PartitionSpec as P

HEADS = 48
HEAD_DIM = 64
STATE = 128
CONV_K = 4
INNER = 3072
CONVW = 3328
LEAD = 16
BLOCK = 512
BLOCK_HEADS = BLOCK // HEAD_DIM
PAIRS = 2
PAIR_LANES = 128 * PAIRS
VMEM = 56 * 1024 * 1024
F32 = jnp.float32
BF = jnp.bfloat16
EPS = 1e-05
highest = lax.Precision.HIGHEST
EVERY = ("x", "core", "z", "y")
CTX = ("z", "y")


def params():
    return pltpu.CompilerParams(vmem_limit_bytes=VMEM, dimension_semantics=("arbitrary",))


def call(body, grid, micros, ins, outs, scratch=(), waits=(), places=None):
    first = (places is not None) + len(ins)
    anywhere = pl.BlockSpec(memory_space=pl.ANY)

    def run(*refs):
        body(*refs[:first], *refs[first + len(waits) :])

    scalars = [] if places is None else [places]
    return pl.pallas_call(
        run,
        grid_spec=pltpu.PrefetchScalarGridSpec(
            num_scalar_prefetch=len(scalars),
            grid=(grid,),
            in_specs=[spec for _, spec in ins] + [anywhere] * len(waits),
            out_specs=[spec for _, spec in outs],
            scratch_shapes=list(scratch),
        ),
        out_shape=[shape for shape, _ in outs],
        compiler_params=params(),
        cost_estimate=pl.CostEstimate(
            flops=int(micros * 1e9), bytes_accessed=int(micros * 3e6), transcendentals=0
        ),
    )(*scalars, *[array for array, _ in ins], *waits)


def tie(value, *others):
    def body(*refs):
        pass

    anywhere = pl.BlockSpec(memory_space=pl.ANY)
    return pl.pallas_call(
        body,
        in_specs=[anywhere] * (1 + len(others)),
        out_specs=anywhere,
        out_shape=jax.ShapeDtypeStruct(value.shape, value.dtype),
        input_output_aliases={0: 0},
    )(value, *others)


def whole(*shape):
    return pl.BlockSpec(shape, lambda g: (0,) * len(shape))


def lanes(rows, width):
    return pl.BlockSpec((rows, width), lambda g: (0, g))


def rows_of(count, width):
    return pl.BlockSpec((count, width), lambda g: (g, 0))


def halves(rows, width):
    count = INNER // 2 // width
    return pl.BlockSpec((1, rows, width), lambda g: (g // count, 0, g % count))


def group(rows, width):
    return pl.BlockSpec((1, rows, width), lambda g: (g, 0, 0))


def out(shape, dtype=F32):
    return jax.ShapeDtypeStruct(shape, dtype)


def split(value):
    high = value.astype(BF)
    return high, (value - high.astype(F32)).astype(BF)


def mm(left, right):
    return jnp.dot(left, right, preferred_element_type=F32)


def mm_nt(left, right):
    return lax.dot_general(left, right, (((1,), (1,)), ((), ())), preferred_element_type=F32)


def mm_tn(left, right):
    return lax.dot_general(left, right, (((0,), (0,)), ((), ())), preferred_element_type=F32)


def three(product, left, right):
    left_high, left_low = left
    right_high, right_low = right
    return (
        product(left_high, right_high)
        + product(left_high, right_low)
        + product(left_low, right_high)
    )


def head_of_lane(first, count):
    lane = lax.broadcasted_iota(jnp.int32, (STATE, count), 1) // HEAD_DIM + first
    row = lax.broadcasted_iota(jnp.int32, (STATE, count), 0)
    return (lane == row).astype(BF)


def expand(value, places):
    high, low = split(value)
    return mm(high, places) + mm(low, places)


def fold(value, places):
    high, low = split(value)
    return mm_nt(high, places) + mm_nt(low, places)


def sigmoid(value):
    return 1.0 / (1.0 + jnp.exp(-value))


def conv_pre(extended, weight, bias, masks):
    running = jnp.zeros((masks.shape[0], extended.shape[1]), F32) + bias
    for tap in range(CONV_K):
        shifted = extended if tap == CONV_K - 1 else pltpu.roll(extended, CONV_K - 1 - tap, 0)
        running = running + shifted[LEAD:] * weight[tap : tap + 1] * masks[:, tap : tap + 1]
    return running


def conv_back(d_pre, extended, weight, masks):
    zeros = jnp.zeros((LEAD, d_pre.shape[1]), F32)
    total = LEAD + d_pre.shape[0]
    d_ext = jnp.zeros((total, d_pre.shape[1]), F32)
    weight_rows = []
    for tap in range(CONV_K):
        by = CONV_K - 1 - tap
        part = d_pre * masks[:, tap : tap + 1]
        padded = jnp.concatenate([zeros, part], axis=0)
        shifted = extended
        if by:
            padded = pltpu.roll(padded, total - by, 0)
            shifted = pltpu.roll(extended, by, 0)
        d_ext = d_ext + padded * weight[tap : tap + 1]
        weight_rows.append(jnp.sum(shifted[LEAD:] * part, axis=0, keepdims=True))
    weight_rows.append(jnp.sum(d_pre, axis=0, keepdims=True))
    weight_rows.append(jnp.zeros((8 - len(weight_rows), d_pre.shape[1]), F32))
    return d_ext, jnp.concatenate(weight_rows, axis=0)


def same_mask(doc_row, doc_col, transposed):
    count = doc_row.shape[1]
    rows = lax.broadcasted_iota(jnp.int32, (count, count), 0)
    cols = lax.broadcasted_iota(jnp.int32, (count, count), 1)
    order = rows <= cols if transposed else rows >= cols
    return jnp.where((doc_row == doc_col) & order, 1.0, 0.0)


def prep_bc_body(x_ref, w_ref, b_ref, m_ref, doc_ref, pre_ref, act_ref, t_ref, s_ref, st_ref):
    masks = m_ref[...]
    pre = conv_pre(x_ref[...].astype(F32), w_ref[...], b_ref[...], masks)
    act = pre * sigmoid(pre)
    pre_ref[...] = pre
    act_ref[...] = act
    t_ref[...] = act.T
    b_rows, c_rows = split(act[:, :STATE]), split(act[:, STATE:])
    doc_row, doc_col = doc_ref[0:1], masks[:, CONV_K : CONV_K + 1]
    s_ref[...] = three(mm_nt, c_rows, b_rows) * same_mask(doc_row, doc_col, False)
    st_ref[...] = three(mm_nt, b_rows, c_rows) * same_mask(doc_row, doc_col, True)


def either(first_ref, second_ref):
    first = pl.program_id(0) < INNER // 2 // BLOCK
    return jnp.where(first, first_ref[...].astype(F32), second_ref[...].astype(F32))


def prep_x_body(x_ref, w_ref, b_ref, m_ref, wl_ref, t_ref, pre_ref, act_ref, state_ref):
    pre = conv_pre(x_ref[...].astype(F32), w_ref[...], b_ref[...], m_ref[...])
    act = pre * sigmoid(pre)
    pre_ref[...] = pre
    act_ref[...] = act
    places = head_of_lane(pl.program_id(0) * BLOCK_HEADS, BLOCK)
    weighted = split(act * expand(wl_ref[...], places))
    state_ref[0] = three(mm, split(t_ref[:STATE]), weighted)


def intra_body(first, x_ref, dt_ref, skip_ref, s_ref, col_ref, row_ref, y_ref):
    half = s_ref.shape[0] // 2
    places = head_of_lane((pl.program_id(0) + first) * 2 * PAIRS, PAIR_LANES)
    scaled = x_ref[...] * expand(dt_ref[...], places)
    lane = lax.broadcasted_iota(jnp.int32, (2 * half, 128), 1)
    for pair in range(PAIRS):
        here = slice(pair * 128, pair * 128 + 128)
        high, low = split(scaled[:, here])
        right = jnp.concatenate([high, low], axis=1)
        both = []
        for side in range(2):
            head = 2 * pair + side
            col = col_ref[0, :, head : head + 1]
            row = row_ref[0, head : head + 1, :]
            top = s_ref[:half, :half] * jnp.exp(jnp.minimum(col[:half] - row[:, :half], 0.0))
            low_part = s_ref[half:, :] * jnp.exp(jnp.minimum(col[half:] - row, 0.0))
            done = []
            for part, count in ((top, half), (low_part, 2 * half)):
                p_high, p_low = split(part)
                first = mm(p_high, right[:count])
                done.append(first[:, :128] + first[:, 128:] + mm(p_low, high[:count]))
            both.append(jnp.concatenate(done, axis=0))
        y_ref[:, here] = (
            jnp.where(lane < HEAD_DIM, both[0], both[1]) + skip_ref[:, here] * x_ref[:, here]
        )


def gate_body(
    ya_ref, yb_ref, z_ref, df_ref, x_ref, c_ref, ct_ref, state_ref, e_ref, gain_ref, skip_ref,
    final_ref, turned_ref, dz_ref, dy_ref, r_ref, dc_ref, q_ref, sums_ref, carry, scaled,
):
    @pl.when(pl.program_id(0) == 0)
    def _():
        r_ref[...] = jnp.zeros_like(r_ref)
        sums_ref[...] = jnp.zeros_like(sums_ref)

    e_high, e_low = split(e_ref[...])
    c_rows = split(c_ref[...])
    for block in range(INNER // BLOCK):
        here = slice(block * BLOCK, block * BLOCK + BLOCK)
        places = head_of_lane(block * BLOCK_HEADS, BLOCK)
        spread = mm(e_high, places) + mm(e_low, places)
        there = slice(block % 3 * BLOCK, block % 3 * BLOCK + BLOCK)
        carry[:, here] = three(mm, c_rows, split(state_ref[block // 3, :, there])) * spread
        scaled[:, here] = spread
    gain, skip = gain_ref[...], skip_ref[...]

    def some(lap, sums):
        at = pl.ds(pl.multiple_of(lap * 16, 16), 16)
        y = jnp.concatenate([ya_ref[at, :], yb_ref[at, :]], axis=1) + carry[at, :]
        z = z_ref[at, :].astype(F32)
        sig = sigmoid(z)
        gate = z * sig
        gated = y * gate
        scale = lax.rsqrt(jnp.mean(gated * gated, axis=-1, keepdims=True) + EPS)
        unit = gated * scale
        final_ref[at, :] = (unit * gain).astype(BF)
        d_final = df_ref[at, :]
        q = d_final * gain
        inner = jnp.mean(q * unit, axis=-1, keepdims=True)
        d_gated = scale * (q - unit * inner)
        d_y = d_gated * gate
        dz_ref[at, :] = (d_gated * y * (sig * (1.0 + z * (1.0 - sig)))).astype(BF)
        dy_ref[at, :] = d_y
        x = x_ref[at, :]
        scaled[at, :] = scaled[at, :] * d_y
        carry[at, :] = d_y * (y - skip * x)
        d_gain, d_skip = d_final * unit, d_y * x
        return (
            sums[0] + d_gain[:8] + d_gain[8:],
            sums[1] + d_skip[:8] + d_skip[8:],
        )

    zero = jnp.zeros((8, INNER), F32)
    d_gain, d_skip = lax.fori_loop(0, z_ref.shape[0] // 16, some, (zero, zero))
    sums_ref[0:8] += d_gain
    sums_ref[8:16] += d_skip
    ct_rows = split(ct_ref[...])
    d_c = jnp.zeros(dc_ref.shape, F32)
    q_sum = jnp.zeros(q_ref.shape, F32)
    for block in range(INNER // BLOCK):
        here = slice(block * BLOCK, block * BLOCK + BLOCK)
        there = slice(block % 3 * BLOCK, block % 3 * BLOCK + BLOCK)
        piece = split(scaled[:, here])
        r_ref[block // 3, :, there] += three(mm, ct_rows, piece)
        d_c = d_c + three(mm_nt, piece, split(state_ref[block // 3, :, there]))
        turned_ref[here, :] = final_ref[:, here].T
        q_sum = q_sum + fold(carry[:, here], head_of_lane(block * BLOCK_HEADS, BLOCK))
    dc_ref[...] = d_c
    q_ref[...] = q_sum


def back_body(first, x_ref, dy_ref, dt_ref, st_ref, col_ref, row_ref, bc_ref, doc_ref, m_ref, in_ref, dx_ref, acc, *ends):
    step = pl.program_id(0)
    half = st_ref.shape[0] // 2

    @pl.when(step == 0)
    def _():
        acc[...] = in_ref[...]

    places = head_of_lane((step + first) * 2 * PAIRS, PAIR_LANES)
    scaled = x_ref[...] * expand(dt_ref[...], places)
    lane = lax.broadcasted_iota(jnp.int32, (2 * half, 128), 1)
    for pair in range(PAIRS):
        here = slice(pair * 128, pair * 128 + 128)
        dy_high, dy_low = split(dy_ref[:, here])
        right = jnp.concatenate([dy_high, dy_low], axis=1)
        twice = jnp.concatenate([dy_high, dy_high], axis=1)
        both = []
        for side in range(2):
            head = 2 * pair + side
            mine = (lane < HEAD_DIM) if side == 0 else (lane >= HEAD_DIM)
            x_high, x_low = split(jnp.where(mine, scaled[:, here], 0.0))
            x_both = jnp.concatenate([x_high, x_low], axis=1)
            col = col_ref[0, :, head : head + 1]
            row = row_ref[0, head : head + 1, :]
            done = []
            for at, over in ((slice(0, half), slice(0, 2 * half)), (slice(half, 2 * half), slice(half, 2 * half))):
                decay = jnp.exp(jnp.minimum(row[:, over] - col[at], 0.0))
                p_high, p_low = split(st_ref[at, over] * decay)
                first = mm(p_high, right[over])
                done.append(first[:, :128] + first[:, 128:] + mm(p_low, dy_high[over]))
                outer = mm_nt(x_both[at], twice[over]) + mm_nt(x_high[at], dy_low[over])
                acc[at, over] += outer * decay
            both.append(jnp.concatenate(done, axis=0))
        dx_ref[:, here] = jnp.where(lane < HEAD_DIM, both[0], both[1])

    if not ends:
        return

    @pl.when(step == pl.num_programs(0) - 1)
    def _():
        dbc_ref = ends[0]
        doc_col = m_ref[:, CONV_K : CONV_K + 1]
        ds = split(acc[...] * same_mask(doc_ref[0:1], doc_col, True))
        dbc_ref[:, :STATE] = three(mm, ds, split(bc_ref[:, STATE:]))
        dbc_ref[:, STATE:] = three(mm_tn, ds, split(bc_ref[:, :STATE]))


def carry_body(
    dxa_ref, dxb_ref, x_ref, dy_ref, pre_ref, in_ref, w_ref, m_ref, bc_ref, r_ref, end_ref, wl_ref, dt_ref,
    skip_ref,
    d_ref, edge_ref, conv_ref, db_ref, g_ref,
):
    step = pl.program_id(0)

    @pl.when(step == 0)
    def _():
        db_ref[...] = jnp.zeros_like(db_ref)
        g_ref[...] = jnp.zeros_like(g_ref)

    places = head_of_lane(step * BLOCK_HEADS, BLOCK)
    returned = r_ref[0]
    r_parts = split(returned)
    to_end = expand(wl_ref[...], places)
    steps = expand(dt_ref[...], places)
    x = x_ref[...]
    d_scaled = either(dxa_ref, dxb_ref) + to_end * three(mm, split(bc_ref[:, :STATE]), r_parts)
    g_ref[...] += fold(x * d_scaled, places)
    db_ref[...] += three(mm_nt, split(to_end * steps * x), r_parts)
    d_x = steps * d_scaled + skip_ref[...] * dy_ref[...]
    pre = pre_ref[...]
    sig = sigmoid(pre)
    d_pre = d_x * (sig * (1.0 + pre * (1.0 - sig)))
    d_ext, sums = conv_back(d_pre, in_ref[...].astype(F32), w_ref[...], m_ref[...])
    d_ref[...] = d_ext[LEAD:].astype(BF)
    edge_ref[:LEAD] = d_ext[:LEAD]
    edge_ref[LEAD:] = d_ext[d_ext.shape[0] - LEAD :]
    flow = jnp.sum(returned * end_ref[0], axis=0, keepdims=True)
    row = lax.broadcasted_iota(jnp.int32, sums.shape, 0)
    conv_ref[...] = jnp.where(row == CONV_K + 1, flow, sums)


def carry_bc_body(d_ref, pre_ref, in_ref, w_ref, m_ref, o_ref, edge_ref, conv_ref):
    pre = pre_ref[...]
    sig = sigmoid(pre)
    d_pre = d_ref[...] * (sig * (1.0 + pre * (1.0 - sig)))
    d_ext, sums = conv_back(d_pre, in_ref[...].astype(F32), w_ref[...], m_ref[...])
    o_ref[...] = d_ext[LEAD:].astype(BF)
    edge_ref[:LEAD] = d_ext[:LEAD]
    edge_ref[LEAD:] = d_ext[d_ext.shape[0] - LEAD :]
    conv_ref[...] = sums


def swap(array, axis):
    return lax.ppermute(array, axis, [(0, 1), (1, 0)])


def from_behind(array, by):
    peers = lax.axis_size(CTX[0]) * lax.axis_size(CTX[1])
    pairs = [(i, i + by) for i in range(peers) if 0 <= i + by < peers]
    return lax.ppermute(array, CTX, pairs)


def entering(state, decay, reverse, fills):
    fills = list(fills)

    def meanwhile(sent, arrived):
        return tie(arrived, *fills.pop(0)(sent)) if fills else arrived

    depth, width = lax.axis_size("z"), lax.axis_size("y")
    place_z, place_y = lax.axis_index("z"), lax.axis_index("y")
    if width != 2:
        wide = jnp.broadcast_to(decay, (2, 8, decay.shape[2]))
        gathered = lax.all_gather(jnp.concatenate([state, wide], axis=1), CTX)
        while fills:
            gathered = meanwhile(state, gathered)
        count = depth * width
        place = place_z * width + place_y
        ahead = count - 1 - place if reverse else place

        def one(lap, running):
            source = count - 1 - lap if reverse else lap
            item = lax.dynamic_index_in_dim(gathered, source, 0, False)
            return item[:, STATE : STATE + 1] * running + item[:, :STATE]

        return lax.fori_loop(0, ahead, one, jnp.zeros_like(state))
    second = place_y == (0 if reverse else 1)
    sent = pick(state, 1 - place_y)
    got = meanwhile(sent, swap(sent, "y"))
    own = pick(state, place_y)
    decay_own = pick(decay, place_y)
    decay_got = swap(pick(decay, 1 - place_y), "y")
    early = jnp.where(second, got, own)
    late = jnp.where(second, own, got)
    decay_early = jnp.where(second, decay_got, decay_own)
    decay_late = jnp.where(second, decay_own, decay_got)
    total = decay_late * early + late
    decay_total = decay_early * decay_late
    before = jnp.zeros_like(total)
    sent = total
    turn = depth - 1 - place_z if reverse else place_z
    for hop in range(1, depth):
        pairs = [(depth - hop, depth - 1 - hop)] if reverse else [(hop - 1, hop)]
        arrived = meanwhile(sent, lax.ppermute(sent, "z", pairs))
        before = jnp.where(turn == hop, arrived, before)
        sent = decay_total * before + total
    middle = decay_early * before + early
    mine = jnp.where(second, middle, before)
    sent = jnp.where(second, before, middle)
    theirs = swap(sent, "y")
    while fills:
        theirs = meanwhile(sent, theirs)
    return in_order(mine, theirs, "y")


def pick(parts, index, dim=0):
    return lax.dynamic_index_in_dim(parts, index, dim, False)


def in_order(mine, theirs, axis):
    first = lax.axis_index(axis) == 0
    return jnp.where(first, jnp.stack([mine, theirs]), jnp.stack([theirs, mine]))


def across(array, axis, by):
    return lax.ppermute(array, axis, [(i, i ^ by) for i in range(lax.axis_size(axis))])


def xor_sum(parts, axis, kind):
    count, place = lax.axis_size(axis), lax.axis_index(axis)
    total = pick(parts, place)
    for by in range(1, count):
        total = total + across(pick(parts, place ^ by).astype(kind), axis, by).astype(F32)
    return total


def products_body(
    place_ref, sent_own, kept_own, sent_other, kept_other, own_ref, other_ref, sent_ref, kept_ref
):
    def product(first, second):
        first, second = first[...], second[...]
        first = first.reshape(-1, first.shape[-1])
        second = second.reshape(-1, second.shape[-1])
        return mm(first, own_ref[...]) + mm(second, other_ref[...])

    sent_ref[...] = product(sent_own, sent_other).astype(BF)
    kept_ref[...] = product(kept_own, kept_other)


def products(left, right, start, count, axis, waits):
    own, other = left
    sizes = [lax.axis_size(a) for a in ("x", "z", "y")]
    tokens = own.shape[1]
    rows = other.shape[0] // sizes[0] // sizes[1] // sizes[2]
    out_rows = other.shape[0] // 2
    places = jnp.stack([lax.axis_index(a) for a in ("core", "x", "y")])
    if axis == "x":
        own = own.reshape(2, 2, out_rows, tokens)
        other = other.reshape(2, out_rows, tokens)
        own_block, other_block = (1, 1, out_rows, tokens), (1, out_rows, tokens)

        def spec(mine, flip):
            if mine:
                return pl.BlockSpec(own_block, lambda g, p: (p[1] ^ flip, p[0], 0, 0))
            return pl.BlockSpec(other_block, lambda g, p: (p[1] ^ flip, 0, 0))
    else:
        own = own.reshape(2, 2, sizes[1], 2, rows, tokens)
        other = other.reshape(2 * sizes[1], 2, rows, tokens)
        own_block = (2, 1, sizes[1], 1, rows, tokens)
        other_block = (2 * sizes[1], 1, rows, tokens)

        def spec(mine, flip):
            if mine:
                return pl.BlockSpec(own_block, lambda g, p: (0, p[0], 0, p[2] ^ flip, 0, 0))
            return pl.BlockSpec(other_block, lambda g, p: (0, p[2] ^ flip, 0, 0))

    block = 512 if count % 512 == 0 or count > 1024 else 384
    first = start // block
    columns_of = pl.BlockSpec((tokens, block), lambda g, p: (0, g + first))
    result = pl.BlockSpec((out_rows, block), lambda g, p: (0, g))
    return call(
        products_body, -(-count // block), count * out_rows / 2.0e5,
        [
            (own, spec(True, 1)), (own, spec(True, 0)), (other, spec(False, 1)), (other, spec(False, 0)),
            (right[0], columns_of), (right[1], columns_of),
        ],
        [(out((out_rows, count), BF), result), (out((out_rows, count)), result)],
        waits=waits,
        places=places,
    )


def products_any(left, right, start, count, axis):
    core, place = lax.axis_index("core"), lax.axis_index(axis)
    sizes = [lax.axis_size(a) for a in ("x", "z", "y")]
    own = core_rows(left[0], core).reshape(left[1].shape)
    both = jnp.concatenate([own, left[1]], axis=1)
    view = both.reshape(*sizes, -1, both.shape[1])
    if axis == "y":
        view = jnp.moveaxis(view, 2, 0)
    view = view.reshape(view.shape[0], -1, both.shape[1])
    right = jnp.concatenate(right, axis=0)[:, start : start + count]
    sent = [mm(pick(view, place ^ by), right).astype(BF) for by in range(1, view.shape[0])]
    return sent, mm(pick(view, place), right)


def total_of(kept, got):
    for piece in got:
        kept = kept + piece.astype(F32)
    return kept


class Reduction:
    def __init__(self, left, right, start, middle, end, waits=()):
        if lax.axis_size("x") == 2 and lax.axis_size("y") == 2:
            sent_x, self.kept_x = products(left, right, start, middle - start, "x", waits)
            sent_y, self.kept_y = products(left, right, middle, end - middle, "y", waits)
            self.sent_x, self.sent_y = [sent_x], [sent_y]
        else:
            self.sent_x, self.kept_x = products_any(left, right, start, middle - start, "x")
            self.sent_y, self.kept_y = products_any(left, right, middle, end - middle, "y")
        self.got_x = [across(piece, "x", by + 1) for by, piece in enumerate(self.sent_x)]
        self.got_y = [across(piece, "y", by + 1) for by, piece in enumerate(self.sent_y)]

    def made(self):
        return [self.kept_x, self.kept_y, *self.sent_x, *self.sent_y]

    def second(self, *others):
        sizes = [lax.axis_size(a) for a in ("x", "z", "y")]
        kept_x, kept_y = self.kept_x, self.kept_y
        if others:
            kept_x, kept_y = tie(kept_x, *others), tie(kept_y, *others)
        part_x = total_of(kept_x, self.got_x)
        part_y = total_of(kept_y, self.got_y)
        view_x = part_x.reshape(sizes[1], sizes[2], -1, part_x.shape[1])
        view_y = part_y.reshape(sizes[0], sizes[1], -1, part_y.shape[1])
        done_x = xor_sum(jnp.moveaxis(view_x, 1, 0), "y", BF)
        done_y = xor_sum(view_y, "x", BF)
        self.parts = jnp.concatenate([done_x, done_y], axis=2)

    def third(self, *others):
        parts = tie(self.parts, *others) if others else self.parts
        count, place = lax.axis_size("z"), lax.axis_index("z")
        self.got_z = [across(pick(parts, place ^ by), "z", by) for by in range(1, count)]
        self.kept_z = pick(parts, place)

    def last(self, *others):
        total = tie(self.kept_z, *others) if others else self.kept_z
        for piece in self.got_z:
            total = total + piece
        return total


def core_rows(turned, core):
    view = turned.reshape(lax.axis_size("x"), 2, -1, turned.shape[1])
    return pick(view, core, 1)


def both_cores(turned, core):
    theirs = core_rows(turned, 1 - core)
    return turned, swap(theirs.reshape(-1, turned.shape[1]), "core")


def document_ids(lengths, positions):
    first_end = lengths[0]
    second_end = lengths[0] + lengths[1]
    inside = (positions >= first_end).astype(jnp.int32) + (positions >= second_end).astype(jnp.int32)
    return jnp.where(positions < 0, -1, inside)


def gather_small(pieces, count):
    flat = jnp.concatenate([piece.reshape(-1) for piece in pieces])
    spread = jnp.broadcast_to(flat[None], (count, flat.shape[0]))
    return lax.all_to_all(spread, EVERY, 0, 0, tiled=True)


def columns(array, width):
    return jnp.pad(array, ((0, 0), (0, width - array.shape[1])))


def shards(
    tokens, out_grad, seq_lengths, norm_gain, in_weight, conv_weight, conv_bias,
    dt_bias, a_log, skip_gain, gated_gain, out_weight,
):
    count = 1
    for axis in EVERY:
        count *= lax.axis_size(axis)
    core = lax.axis_index("core")
    place = lax.axis_index("z") * lax.axis_size("y") + lax.axis_index("y")
    row_count = tokens.shape[0]
    width = tokens.shape[1]
    first_row = place * row_count

    lengths = seq_lengths[0]
    ordinal = jnp.arange(row_count, dtype=jnp.int32)
    doc_ids = document_ids(lengths, first_row + ordinal)
    doc_before = document_ids(lengths, first_row - 1 + jnp.zeros((1,), jnp.int32))
    marks = [
        (document_ids(lengths, first_row + ordinal - (CONV_K - 1 - tap)) == doc_ids).astype(F32)
        for tap in range(CONV_K)
    ]
    keep = marks[CONV_K - 2]
    masks = columns(jnp.stack(marks + [doc_ids.astype(F32)], axis=1), 128)
    doc_rows = jnp.broadcast_to(doc_ids.astype(F32)[None], (8, row_count))
    alive = (doc_ids == doc_before[0]).astype(F32)
    tail = (doc_ids == doc_ids[row_count - 1]).astype(F32)

    lead_tokens = from_behind(tokens[row_count - LEAD :], 1)
    small = gather_small([norm_gain, conv_weight, conv_bias, gated_gain], count)
    cuts = [norm_gain.size, conv_weight.size, conv_bias.size]
    cuts = [sum(cuts[: i + 1]) for i in range(3)]
    gain_piece, conv_piece, bias_piece, gated_piece = jnp.split(small, cuts, axis=1)
    full_gain = gain_piece.reshape(1, -1).astype(F32)
    full_conv = jnp.moveaxis(conv_piece.reshape(count, CONV_K, -1), 1, 0).reshape(CONV_K, -1)
    full_conv = jnp.pad(full_conv.astype(F32), ((0, 4), (0, 0)))
    full_bias = bias_piece.reshape(1, -1).astype(F32)
    full_gated = gated_piece.reshape(1, -1).astype(F32)
    weight_x = lax.all_gather(in_weight[:, INNER:], EVERY, axis=0, tiled=True)
    half = INNER // 2
    count_out = out_weight.shape[0] // 2
    stacked = jnp.stack(
        [in_weight[:, :half], in_weight[:, half:INNER], out_weight[:count_out], out_weight[count_out:]]
    )
    stacked = lax.all_gather(stacked, EVERY, axis=1, tiled=True)

    extended = jnp.concatenate([lead_tokens, tokens], axis=0).astype(F32)
    rms = lax.rsqrt(jnp.mean(extended * extended, axis=-1, keepdims=True) + EPS)
    normed_ext = (extended * rms * full_gain).astype(BF)
    normed = normed_ext[LEAD:]
    mixed_x = mm(normed_ext, weight_x).astype(BF)
    bc_width = CONVW - INNER
    shifted_dt = mixed_x[LEAD:, CONVW:].astype(F32) + dt_bias[None]
    turned = normed.T
    normed_left = both_cores(turned, core)

    steps = jax.nn.softplus(shifted_dt)
    rate = jnp.exp(a_log)[None]
    log_decay = -steps * rate
    lower = (ordinal[:, None] >= ordinal[None, :]).astype(F32)
    cumulative = jnp.dot(lower, log_decay, precision=highest)
    last = cumulative[row_count - 1 :]
    enter = jnp.exp(cumulative) * alive[:, None]
    to_end = jnp.exp(last - cumulative) * tail[:, None]
    device_decay = jnp.repeat(enter[row_count - 1 :], HEAD_DIM, axis=1).reshape(2, 1, -1)
    steps_wide = columns(steps, 128)
    enter_wide = columns(enter, 128)
    to_end_wide = columns(to_end, 128)
    weights_wide = columns(to_end * steps, 128)
    heads_block = 2 * PAIRS
    groups = HEADS // heads_block
    cum_cols = jnp.moveaxis(cumulative.reshape(row_count, groups, heads_block), 1, 0)
    cum_rows = cumulative.T.reshape(groups, heads_block, row_count)
    skip_wide = jnp.repeat(skip_gain, HEAD_DIM)[None]

    full_rows = LEAD + row_count
    block_bc = pl.BlockSpec((full_rows, bc_width), lambda g: (0, INNER // bc_width))
    square = (row_count, row_count)
    pre_bc, act_bc, act_t, scores, scores_t = call(
        prep_bc_body, 1, 3.6,
        [
            (mixed_x, block_bc),
            (full_conv[:, INNER:], whole(8, bc_width)),
            (full_bias[:, INNER:], whole(1, bc_width)),
            (masks, whole(row_count, 128)),
            (doc_rows, whole(8, row_count)),
        ],
        [
            (out((row_count, bc_width)), whole(row_count, bc_width)),
            (out((row_count, bc_width)), whole(row_count, bc_width)),
            (out((bc_width, row_count)), whole(bc_width, row_count)),
            (out(square), whole(*square)),
            (out(square), whole(*square)),
        ],
    )
    pre_x, act_x, state_local = call(
        prep_x_body, INNER // BLOCK, 12,
        [
            (mixed_x, lanes(full_rows, BLOCK)),
            (full_conv[:, :INNER], lanes(8, BLOCK)),
            (full_bias[:, :INNER], lanes(1, BLOCK)),
            (masks, whole(row_count, 128)),
            (weights_wide, whole(row_count, 128)),
            (act_t, whole(bc_width, row_count)),
        ],
        [
            (out((row_count, INNER)), lanes(row_count, BLOCK)),
            (out((row_count, INNER)), lanes(row_count, BLOCK)),
            (out((2, STATE, INNER // 2)), halves(STATE, BLOCK)),
        ],
    )
    half_groups = groups // 2
    kept = {}

    def intra(index, wait):
        kept[index] = call(
            functools.partial(intra_body, index * half_groups), half_groups, 12,
            [
                (act_x, pl.BlockSpec((row_count, PAIR_LANES), lambda g: (0, g + index * half_groups))),
                (steps_wide, whole(row_count, 128)),
                (skip_wide[:, index * half :][:, :half], lanes(1, PAIR_LANES)),
                (scores, whole(*square)),
                (cum_cols[index * half_groups :][:half_groups], group(row_count, heads_block)),
                (cum_rows[index * half_groups :][:half_groups], group(heads_block, row_count)),
            ],
            [(out((row_count, half)), lanes(row_count, PAIR_LANES))],
            waits=[wait],
        )[0]
        return [kept[index]]

    def project(wait):
        weight_z = [stacked[0], stacked[1]]
        weight_o = stacked[2:].reshape(2, count, count_out, width)
        weight_o = jnp.moveaxis(weight_o, 0, 1).reshape(-1, width)
        kept["z"], kept["o"] = weight_z, weight_o
        mixed_z = [mm(normed, weight).astype(BF) for weight in weight_z]
        kept["mixed_z"] = jnp.concatenate(mixed_z, axis=1)
        kept["d_final"] = mm_nt(out_grad, weight_o)
        return [kept["mixed_z"], kept["d_final"]]

    state_in = entering(
        state_local, device_decay, False,
        [lambda wait: [], lambda wait: intra(0, wait), lambda wait: intra(1, wait), project],
    )
    state_end = device_decay * state_in + state_local
    weight_z, weight_o = kept["z"], kept["o"]
    mixed_z, d_final = kept["mixed_z"], kept["d_final"]

    tile = 128
    c_rows = act_bc[:, STATE:]
    c_cols = act_t[STATE:]
    final, final_turned, d_z, d_y, returned_local, d_c_carry, dy_y, sums = call(
        gate_body, row_count // tile, 31,
        [
            (kept[0], rows_of(tile, half)),
            (kept[1], rows_of(tile, half)),
            (mixed_z, rows_of(tile, INNER)),
            (d_final, rows_of(tile, INNER)),
            (act_x, rows_of(tile, INNER)),
            (c_rows, rows_of(tile, STATE)),
            (c_cols, lanes(STATE, tile)),
            (state_in, whole(2, STATE, INNER // 2)),
            (enter_wide, rows_of(tile, 128)),
            (full_gated, whole(1, INNER)),
            (skip_wide, whole(1, INNER)),
        ],
        [
            (out((row_count, INNER), BF), rows_of(tile, INNER)),
            (out((INNER, row_count), BF), lanes(INNER, tile)),
            (out((row_count, INNER), BF), rows_of(tile, INNER)),
            (out((row_count, INNER)), rows_of(tile, INNER)),
            (out((2, STATE, INNER // 2)), whole(2, STATE, INNER // 2)),
            (out((row_count, STATE)), rows_of(tile, STATE)),
            (out((row_count, 128)), rows_of(tile, 128)),
            (out((16, INNER)), whole(16, INNER)),
        ],
        [pltpu.VMEM((tile, INNER), F32), pltpu.VMEM((tile, INNER), F32)],
    )

    out_grad_theirs = swap(out_grad, "core")
    final_left = both_cores(final_turned, core)
    d_z_theirs = swap(d_z, "core")
    back = {"acc": jnp.zeros(square, F32)}

    def out_sums(wait):
        back["out"] = Reduction(final_left, [out_grad, out_grad_theirs], 0, width // 2, width, [wait])
        return back["out"].made()

    def z_sums(wait):
        back["z"] = Reduction(normed_left, [d_z, d_z_theirs], 0, half, INNER, [wait])
        return back["z"].made()

    def within(index, wait):
        ends = [(out((row_count, bc_width)), whole(row_count, bc_width))] if index else []
        back[index], back["acc"], *back["bc"] = call(
            functools.partial(back_body, index * half_groups), half_groups, 16,
            [
                (act_x, pl.BlockSpec((row_count, PAIR_LANES), lambda g: (0, g + index * half_groups))),
                (d_y, pl.BlockSpec((row_count, PAIR_LANES), lambda g: (0, g + index * half_groups))),
                (steps_wide, whole(row_count, 128)),
                (scores_t, whole(*square)),
                (cum_cols[index * half_groups :][:half_groups], group(row_count, heads_block)),
                (cum_rows[index * half_groups :][:half_groups], group(heads_block, row_count)),
                (act_bc, whole(row_count, bc_width)),
                (doc_rows, whole(8, row_count)),
                (masks, whole(row_count, 128)),
                (back["acc"], whole(*square)),
            ],
            [
                (out((row_count, half)), lanes(row_count, PAIR_LANES)),
                (out(square), whole(*square)),
                *ends,
            ],
            waits=[wait],
        )
        return [back[index]]

    def rest(wait):
        back["out"].second(wait)
        back["z"].second(wait)
        layer = (tokens.astype(F32) + mm(final, weight_o)).astype(BF)
        back["layer_out"] = layer
        back["d_normed"] = mm_nt(d_z[:, :half], weight_z[0]) + mm_nt(d_z[:, half:], weight_z[1])
        return [layer, back["d_normed"]]

    returned = entering(
        returned_local, device_decay, True,
        [out_sums, z_sums, lambda wait: within(0, wait), lambda wait: within(1, wait), rest],
    )
    layer_out = back["layer_out"]
    d_bc = back["bc"][0]
    back["out"].third(returned)
    back["z"].third(returned)

    d_xs, edge_x, conv_x, d_b_carry, x_dx = call(
        carry_body, INNER // BLOCK, 27,
        [
            (back[0], pl.BlockSpec((row_count, BLOCK), lambda g: (0, jnp.minimum(g, half // BLOCK - 1)))),
            (back[1], pl.BlockSpec((row_count, BLOCK), lambda g: (0, jnp.maximum(g - half // BLOCK, 0)))),
            (act_x, lanes(row_count, BLOCK)),
            (d_y, lanes(row_count, BLOCK)),
            (pre_x, lanes(row_count, BLOCK)),
            (mixed_x, lanes(full_rows, BLOCK)),
            (full_conv[:, :INNER], lanes(8, BLOCK)),
            (masks, whole(row_count, 128)),
            (act_bc, whole(row_count, bc_width)),
            (returned, halves(STATE, BLOCK)),
            (state_end, halves(STATE, BLOCK)),
            (to_end_wide, whole(row_count, 128)),
            (steps_wide, whole(row_count, 128)),
            (skip_wide, lanes(1, BLOCK)),
        ],
        [
            (out((row_count, INNER), BF), lanes(row_count, BLOCK)),
            (out((2 * LEAD, INNER)), lanes(2 * LEAD, BLOCK)),
            (out((8, INNER)), lanes(8, BLOCK)),
            (out((row_count, STATE)), whole(row_count, STATE)),
            (out((row_count, 128)), whole(row_count, 128)),
        ],
    )
    d_bc = d_bc + jnp.concatenate([d_b_carry, d_c_carry], axis=1)
    d_bc_low, edge_bc, conv_bc = call(
        carry_bc_body, 1, 3,
        [
            (d_bc, whole(row_count, bc_width)),
            (pre_bc, whole(row_count, bc_width)),
            (mixed_x, block_bc),
            (full_conv[:, INNER:], whole(8, bc_width)),
            (masks, whole(row_count, 128)),
        ],
        [
            (out((row_count, bc_width), BF), whole(row_count, bc_width)),
            (out((2 * LEAD, bc_width)), whole(2 * LEAD, bc_width)),
            (out((8, bc_width)), whole(8, bc_width)),
        ],
    )
    conv_sums = jnp.concatenate([conv_x, conv_bc], axis=1)
    edges = jnp.concatenate([edge_x, edge_bc], axis=1)
    d_last = edges[LEAD:] + from_behind(edges[:LEAD], -1)

    x_dx = x_dx[:, :HEADS]
    flow = jnp.sum(conv_x[CONV_K + 1].reshape(HEADS, HEAD_DIM), axis=1)
    difference = dy_y[:, :HEADS] - steps * x_dx
    upper = (ordinal[:, None] <= ordinal[None, :]).astype(F32)
    d_log_decay = (flow[None] + jnp.dot(upper, difference, precision=highest)) * keep[:, None]
    d_steps = x_dx - rate * d_log_decay
    d_dt = d_steps * jax.nn.sigmoid(shifted_dt)
    grad_a_log = -jnp.sum(steps * rate * d_log_decay, axis=0)
    grad_dt_bias = jnp.sum(d_dt, axis=0)
    grad_skip = jnp.sum(jnp.sum(sums[8:], axis=0).reshape(HEADS, HEAD_DIM), axis=1)
    grad_gated = jnp.sum(sums[:8], axis=0)

    d_last = d_last.astype(BF)
    d_x = jnp.concatenate([d_xs, d_bc_low, d_dt.astype(BF)], axis=1)
    d_x = lax.dynamic_update_slice(d_x, d_last, (row_count - LEAD, 0))
    d_x_theirs = swap(d_x, "core")
    last_sums = Reduction(normed_left, [d_x, d_x_theirs], 0, half, d_x.shape[1])
    d_normed = back["d_normed"] + mm_nt(tie(d_x, *last_sums.made()), weight_x)
    last_sums.second()
    last_sums.third()

    rows_value, scale = extended[LEAD:], rms[LEAD:]
    unit = rows_value * scale
    pulled = d_normed * full_gain
    d_rows = scale * (pulled - unit * jnp.mean(pulled * unit, axis=-1, keepdims=True))
    grad_tokens = out_grad.astype(F32) + d_rows
    grad_gain = jnp.sum(d_normed * unit, axis=0)

    sum_out = back["out"].last(d_normed, last_sums.parts)
    sum_in_z = back["z"].last(d_normed, last_sums.parts)
    sum_in_x = last_sums.last()

    per_device = jnp.concatenate(
        [
            grad_gain.reshape(count, -1),
            jnp.moveaxis(conv_sums[:CONV_K].reshape(CONV_K, count, -1), 1, 0).reshape(count, -1),
            conv_sums[CONV_K].reshape(count, -1),
            grad_gated.reshape(count, -1),
            jnp.broadcast_to(
                jnp.concatenate([grad_dt_bias, grad_a_log, grad_skip])[None], (count, 3 * HEADS)
            ),
        ],
        axis=1,
    )
    small_sums = jnp.sum(lax.all_to_all(per_device, EVERY, 0, 0, tiled=True), axis=0)
    cuts = [norm_gain.size, conv_weight.size, conv_bias.size, gated_gain.size, HEADS, HEADS]
    cuts = [sum(cuts[: i + 1]) for i in range(6)]
    sum_gain, sum_conv, sum_bias, sum_gated, sum_dt, sum_log, sum_skip = jnp.split(small_sums, cuts)
    return (
        layer_out,
        grad_tokens,
        sum_gain,
        jnp.concatenate([sum_in_z, sum_in_x], axis=1),
        sum_conv.reshape(conv_weight.shape),
        sum_bias,
        sum_dt,
        sum_log,
        sum_skip,
        sum_gated,
        sum_out,
    )


def solution(mesh):
    x = mesh.shape["dp"] // 2
    y = x
    z = mesh.shape["ctx"] // y
    fine = Mesh(mesh.devices.reshape(x, 2, z, y), EVERY)
    rows = P(EVERY, None)
    flat = P(EVERY)
    in_specs = (
        rows, rows, P(("x", "core"), None), flat, rows, P(None, EVERY), flat,
        P(), P(), P(), flat, rows,
    )
    out_specs = (rows, rows, flat, rows, P(None, EVERY), flat, P(), P(), P(), flat, rows)
    return jax.shard_map(shards, mesh=fine, in_specs=in_specs, out_specs=out_specs, check_vma=False)
```

```python
import functools

import jax
import jax.numpy as jnp
from jax import lax
from jax.experimental import pallas as pl
from jax.experimental.pallas import tpu as pltpu
from jax.sharding import Mesh, PartitionSpec as P

HEADS = 48
HEAD_DIM = 64
STATE = 128
CONV_K = 4
INNER = 3072
CONVW = 3328
LEAD = 16
PROJ_X = 3456
BLOCK = 512
BLOCK_HEADS = BLOCK // HEAD_DIM
PAIRS = 2
PAIR_LANES = 128 * PAIRS
VMEM = 56 * 1024 * 1024
F32 = jnp.float32
BF = jnp.bfloat16
EPS = 1e-05
highest = lax.Precision.HIGHEST
EVERY = ("x", "core", "z", "y")
CTX = ("z", "y")


def params():
    return pltpu.CompilerParams(vmem_limit_bytes=VMEM, dimension_semantics=("arbitrary",))


def call(body, grid, micros, ins, outs, scratch=(), waits=(), places=None):
    first = (places is not None) + len(ins)
    anywhere = pl.BlockSpec(memory_space=pl.ANY)

    def run(*refs):
        body(*refs[:first], *refs[first + len(waits) :])

    scalars = [] if places is None else [places]
    return pl.pallas_call(
        run,
        grid_spec=pltpu.PrefetchScalarGridSpec(
            num_scalar_prefetch=len(scalars),
            grid=(grid,),
            in_specs=[spec for _, spec in ins] + [anywhere] * len(waits),
            out_specs=[spec for _, spec in outs],
            scratch_shapes=list(scratch),
        ),
        out_shape=[shape for shape, _ in outs],
        compiler_params=params(),
        cost_estimate=pl.CostEstimate(
            flops=int(micros * 1e9), bytes_accessed=int(micros * 3e6), transcendentals=0
        ),
    )(*scalars, *[array for array, _ in ins], *waits)


def tie(value, *others):
    def body(*refs):
        pass

    anywhere = pl.BlockSpec(memory_space=pl.ANY)
    return pl.pallas_call(
        body,
        in_specs=[anywhere] * (1 + len(others)),
        out_specs=anywhere,
        out_shape=jax.ShapeDtypeStruct(value.shape, value.dtype),
        input_output_aliases={0: 0},
    )(value, *others)


def whole(*shape):
    return pl.BlockSpec(shape, lambda g: (0,) * len(shape))


def lanes(rows, width):
    return pl.BlockSpec((rows, width), lambda g: (0, g))


def rows_of(count, width):
    return pl.BlockSpec((count, width), lambda g: (g, 0))


def halves(rows, width):
    count = INNER // 2 // width
    return pl.BlockSpec((1, rows, width), lambda g: (g // count, 0, g % count))


def group(rows, width):
    return pl.BlockSpec((1, rows, width), lambda g: (g, 0, 0))


def out(shape, dtype=F32):
    return jax.ShapeDtypeStruct(shape, dtype)


def split(value):
    high = value.astype(BF)
    return high, (value - high.astype(F32)).astype(BF)


def mm(left, right):
    return jnp.dot(left, right, preferred_element_type=F32)


def mm_nt(left, right):
    return lax.dot_general(left, right, (((1,), (1,)), ((), ())), preferred_element_type=F32)


def mm_tn(left, right):
    return lax.dot_general(left, right, (((0,), (0,)), ((), ())), preferred_element_type=F32)


def three(product, left, right):
    left_high, left_low = left
    right_high, right_low = right
    return (
        product(left_high, right_high)
        + product(left_high, right_low)
        + product(left_low, right_high)
    )


def head_of_lane(first, count):
    lane = lax.broadcasted_iota(jnp.int32, (STATE, count), 1) // HEAD_DIM + first
    row = lax.broadcasted_iota(jnp.int32, (STATE, count), 0)
    return (lane == row).astype(BF)


def expand(value, places):
    high, low = split(value)
    return mm(high, places) + mm(low, places)


def fold(value, places):
    high, low = split(value)
    return mm_nt(high, places) + mm_nt(low, places)


def sigmoid(value):
    return 1.0 / (1.0 + jnp.exp(-value))


def conv_pre(extended, weight, bias, masks):
    running = jnp.zeros((masks.shape[0], extended.shape[1]), F32) + bias
    for tap in range(CONV_K):
        shifted = extended if tap == CONV_K - 1 else pltpu.roll(extended, CONV_K - 1 - tap, 0)
        running = running + shifted[LEAD:] * weight[tap : tap + 1] * masks[:, tap : tap + 1]
    return running


def conv_back(d_pre, extended, weight, masks):
    zeros = jnp.zeros((LEAD, d_pre.shape[1]), F32)
    total = LEAD + d_pre.shape[0]
    d_ext = jnp.zeros((total, d_pre.shape[1]), F32)
    weight_rows = []
    for tap in range(CONV_K):
        by = CONV_K - 1 - tap
        part = d_pre * masks[:, tap : tap + 1]
        padded = jnp.concatenate([zeros, part], axis=0)
        shifted = extended
        if by:
            padded = pltpu.roll(padded, total - by, 0)
            shifted = pltpu.roll(extended, by, 0)
        d_ext = d_ext + padded * weight[tap : tap + 1]
        weight_rows.append(jnp.sum(shifted[LEAD:] * part, axis=0, keepdims=True))
    weight_rows.append(jnp.sum(d_pre, axis=0, keepdims=True))
    weight_rows.append(jnp.zeros((8 - len(weight_rows), d_pre.shape[1]), F32))
    return d_ext, jnp.concatenate(weight_rows, axis=0)


def same_mask(doc_row, doc_col, transposed):
    count = doc_row.shape[1]
    rows = lax.broadcasted_iota(jnp.int32, (count, count), 0)
    cols = lax.broadcasted_iota(jnp.int32, (count, count), 1)
    order = rows <= cols if transposed else rows >= cols
    return jnp.where((doc_row == doc_col) & order, 1.0, 0.0)


def norm_body(lead_ref, x_ref, gain_ref, normed_ref, turned_ref):
    def normed(value):
        scale = lax.rsqrt(jnp.mean(value * value, axis=-1, keepdims=True) + EPS)
        return value * scale * gain_ref[...]

    normed_ref[:LEAD] = normed(lead_ref[...].astype(F32)).astype(BF)
    for tile in range(x_ref.shape[0] // 128):
        here = slice(tile * 128, tile * 128 + 128)
        value = normed(x_ref[here].astype(F32))
        normed_ref[LEAD + tile * 128 : LEAD + tile * 128 + 128] = value.astype(BF)
        turned_ref[:, here] = value.T.astype(BF)


def parts_of(value):
    high, low = split(value)
    return high, low, (value - high.astype(F32) - low.astype(F32)).astype(BF)


def running_sum(value, transposed):
    count = value.shape[0]
    rows = lax.broadcasted_iota(jnp.int32, (count, count), 0)
    cols = lax.broadcasted_iota(jnp.int32, (count, count), 1)
    side = ((rows <= cols) if transposed else (rows >= cols)).astype(BF)
    high, middle, low = parts_of(value)
    return mm(side, high) + mm(side, middle) + mm(side, low)


def softplus(value):
    return jnp.maximum(value, 0.0) + jnp.log1p(jnp.exp(-jnp.abs(value)))


def prep_bc_body(
    x_ref, dr_ref, w_ref, b_ref, m_ref, doc_ref, shift_ref, rate_ref,
    pre_ref, act_ref, t_ref, s_ref, st_ref, steps_ref, enter_ref, to_end_ref, cum_ref, turned_ref, dt_ref,
):
    masks = m_ref[...]
    pre = conv_pre(x_ref[...].astype(F32), w_ref[...], b_ref[...], masks)
    act = pre * sigmoid(pre)
    pre_ref[...] = pre
    act_ref[...] = act
    t_ref[...] = act.T
    b_rows, c_rows = split(act[:, :STATE]), split(act[:, STATE:])
    doc_row, doc_col = doc_ref[0:1], masks[:, CONV_K : CONV_K + 1]
    s_ref[...] = three(mm_nt, c_rows, b_rows) * same_mask(doc_row, doc_col, False)
    st_ref[...] = three(mm_nt, b_rows, c_rows) * same_mask(doc_row, doc_col, True)
    shifted = dr_ref[LEAD:, :].astype(F32) + shift_ref[...]
    steps = softplus(shifted)
    cumulative = running_sum(-steps * rate_ref[...], False)
    last = cumulative[cumulative.shape[0] - 1 :]
    dt_ref[...] = shifted
    steps_ref[...] = steps
    enter_ref[...] = jnp.exp(cumulative) * masks[:, CONV_K + 1 : CONV_K + 2]
    to_end_ref[...] = jnp.exp(last - cumulative) * masks[:, CONV_K + 2 : CONV_K + 3]
    cum_ref[...] = cumulative
    turned_ref[...] = cumulative.T


def prep_x_body(
    x_ref, w_ref, b_ref, m_ref, wl_ref, dt_ref, e_ref, t_ref, pre_ref, act_ref, state_ref, decay_ref
):
    pre = conv_pre(x_ref[...].astype(F32), w_ref[...], b_ref[...], m_ref[...])
    act = pre * sigmoid(pre)
    pre_ref[...] = pre
    act_ref[...] = act
    places = head_of_lane(pl.program_id(0) * BLOCK_HEADS, BLOCK)
    weighted = split(act * expand(wl_ref[...] * dt_ref[...], places))
    state_ref[0] = three(mm, split(t_ref[:STATE]), weighted)
    last = e_ref[e_ref.shape[0] - 8 :]
    high, middle, low = parts_of(last)
    spread = mm(high, places) + mm(middle, places) + mm(low, places)
    decay_ref[0] = jnp.broadcast_to(spread[7:8], spread.shape)


def heads_here(cum_ref, first):
    back = STATE - (pl.program_id(0) + first) * 2 * PAIRS
    return pltpu.roll(cum_ref[...], jnp.where(back == STATE, 0, back), 1)


def intra_body(first, x_ref, dt_ref, skip_ref, s_ref, cum_ref, row_ref, y_ref):
    half = s_ref.shape[0] // 2
    places = head_of_lane((pl.program_id(0) + first) * 2 * PAIRS, PAIR_LANES)
    scaled = x_ref[...] * expand(dt_ref[...], places)
    cols = heads_here(cum_ref, first)
    lane = lax.broadcasted_iota(jnp.int32, (2 * half, 128), 1)
    for pair in range(PAIRS):
        here = slice(pair * 128, pair * 128 + 128)
        high, low = split(scaled[:, here])
        right = jnp.concatenate([high, low], axis=1)
        both = []
        for side in range(2):
            head = 2 * pair + side
            col = cols[:, head : head + 1]
            row = row_ref[0, head : head + 1, :]
            top = s_ref[:half, :half] * jnp.exp(jnp.minimum(col[:half] - row[:, :half], 0.0))
            low_part = s_ref[half:, :] * jnp.exp(jnp.minimum(col[half:] - row, 0.0))
            done = []
            for part, count in ((top, half), (low_part, 2 * half)):
                p_high, p_low = split(part)
                first = mm(p_high, right[:count])
                done.append(first[:, :128] + first[:, 128:] + mm(p_low, high[:count]))
            both.append(jnp.concatenate(done, axis=0))
        y_ref[:, here] = (
            jnp.where(lane < HEAD_DIM, both[0], both[1]) + skip_ref[:, here] * x_ref[:, here]
        )


def gate_body(
    ya_ref, yb_ref, za_ref, zb_ref, df_ref, x_ref, c_ref, ct_ref, state_ref, e_ref, gain_ref, skip_ref,
    final_ref, turned_ref, dz_ref, dy_ref, r_ref, dc_ref, q_ref, sums_ref, carry, scaled,
):
    @pl.when(pl.program_id(0) == 0)
    def _():
        r_ref[...] = jnp.zeros_like(r_ref)
        sums_ref[...] = jnp.zeros_like(sums_ref)

    e_high, e_low = split(e_ref[...])
    c_rows = split(c_ref[...])
    for block in range(INNER // BLOCK):
        here = slice(block * BLOCK, block * BLOCK + BLOCK)
        places = head_of_lane(block * BLOCK_HEADS, BLOCK)
        spread = mm(e_high, places) + mm(e_low, places)
        there = slice(block % 3 * BLOCK, block % 3 * BLOCK + BLOCK)
        carry[:, here] = three(mm, c_rows, split(state_ref[block // 3, :, there])) * spread
        scaled[:, here] = spread
    gain, skip = gain_ref[...], skip_ref[...]

    def some(lap, sums):
        at = pl.ds(pl.multiple_of(lap * 16, 16), 16)
        y = jnp.concatenate([ya_ref[at, :], yb_ref[at, :]], axis=1) + carry[at, :]
        z = jnp.concatenate([za_ref[at, :], zb_ref[at, :]], axis=1).astype(F32)
        sig = sigmoid(z)
        gate = z * sig
        gated = y * gate
        scale = lax.rsqrt(jnp.mean(gated * gated, axis=-1, keepdims=True) + EPS)
        unit = gated * scale
        final_ref[at, :] = (unit * gain).astype(BF)
        d_final = df_ref[at, :]
        q = d_final * gain
        inner = jnp.mean(q * unit, axis=-1, keepdims=True)
        d_gated = scale * (q - unit * inner)
        d_y = d_gated * gate
        dz_ref[at, :] = (d_gated * y * (sig * (1.0 + z * (1.0 - sig)))).astype(BF)
        dy_ref[at, :] = d_y
        x = x_ref[at, :]
        scaled[at, :] = scaled[at, :] * d_y
        carry[at, :] = d_y * (y - skip * x)
        d_gain, d_skip = d_final * unit, d_y * x
        return (
            sums[0] + d_gain[:8] + d_gain[8:],
            sums[1] + d_skip[:8] + d_skip[8:],
        )

    zero = jnp.zeros((8, INNER), F32)
    d_gain, d_skip = lax.fori_loop(0, za_ref.shape[0] // 16, some, (zero, zero))
    sums_ref[0:8] += d_gain
    sums_ref[8:16] += d_skip
    ct_rows = split(ct_ref[...])
    d_c = jnp.zeros(dc_ref.shape, F32)
    q_sum = jnp.zeros(q_ref.shape, F32)
    for block in range(INNER // BLOCK):
        here = slice(block * BLOCK, block * BLOCK + BLOCK)
        there = slice(block % 3 * BLOCK, block % 3 * BLOCK + BLOCK)
        piece = split(scaled[:, here])
        r_ref[block // 3, :, there] += three(mm, ct_rows, piece)
        d_c = d_c + three(mm_nt, piece, split(state_ref[block // 3, :, there]))
        turned_ref[here, :] = final_ref[:, here].T
        q_sum = q_sum + fold(carry[:, here], head_of_lane(block * BLOCK_HEADS, BLOCK))
    dc_ref[...] = d_c
    q_ref[...] = q_sum


def back_body(first, x_ref, dy_ref, dt_ref, st_ref, cum_ref, row_ref, bc_ref, doc_ref, m_ref, in_ref, dx_ref, acc, *ends):
    step = pl.program_id(0)
    half = st_ref.shape[0] // 2

    @pl.when(step == 0)
    def _():
        acc[...] = in_ref[...]

    places = head_of_lane((step + first) * 2 * PAIRS, PAIR_LANES)
    scaled = x_ref[...] * expand(dt_ref[...], places)
    cols = heads_here(cum_ref, first)
    lane = lax.broadcasted_iota(jnp.int32, (2 * half, 128), 1)
    for pair in range(PAIRS):
        here = slice(pair * 128, pair * 128 + 128)
        dy_high, dy_low = split(dy_ref[:, here])
        right = jnp.concatenate([dy_high, dy_low], axis=1)
        twice = jnp.concatenate([dy_high, dy_high], axis=1)
        both = []
        for side in range(2):
            head = 2 * pair + side
            mine = (lane < HEAD_DIM) if side == 0 else (lane >= HEAD_DIM)
            x_high, x_low = split(jnp.where(mine, scaled[:, here], 0.0))
            x_both = jnp.concatenate([x_high, x_low], axis=1)
            col = cols[:, head : head + 1]
            row = row_ref[0, head : head + 1, :]
            done = []
            for at, over in ((slice(0, half), slice(0, 2 * half)), (slice(half, 2 * half), slice(half, 2 * half))):
                decay = jnp.exp(jnp.minimum(row[:, over] - col[at], 0.0))
                p_high, p_low = split(st_ref[at, over] * decay)
                first = mm(p_high, right[over])
                done.append(first[:, :128] + first[:, 128:] + mm(p_low, dy_high[over]))
                outer = mm_nt(x_both[at], twice[over]) + mm_nt(x_high[at], dy_low[over])
                acc[at, over] += outer * decay
            both.append(jnp.concatenate(done, axis=0))
        dx_ref[:, here] = jnp.where(lane < HEAD_DIM, both[0], both[1])

    if not ends:
        return

    @pl.when(step == pl.num_programs(0) - 1)
    def _():
        dbc_ref = ends[0]
        doc_col = m_ref[:, CONV_K : CONV_K + 1]
        ds = split(acc[...] * same_mask(doc_ref[0:1], doc_col, True))
        dbc_ref[:, :STATE] = three(mm, ds, split(bc_ref[:, STATE:]))
        dbc_ref[:, STATE:] = three(mm_tn, ds, split(bc_ref[:, :STATE]))


def carry_body(
    first, dx_ref, x_ref, dy_ref, pre_ref, in_ref, w_ref, m_ref, bc_ref, r_ref, end_ref, wl_ref, dt_ref,
    skip_ref, db_in, g_in, flow_in, *refs,
):
    extra = refs[:-6]
    d_ref, edge_ref, conv_ref, db_ref, g_ref, flow_ref = refs[-6:]
    if extra:
        pre_bc, in_bc, w_bc, dbc_ref, dc_ref, shifted_ref, rate_ref, q_ref, heads_ref = extra
    step = pl.program_id(0)
    count = INNER // 2 // BLOCK

    @pl.when(step == 0)
    def _():
        db_ref[...] = db_in[...]
        g_ref[...] = g_in[...]
        flow_ref[...] = flow_in[...]

    def conv(d_act, pre, inputs, weight, width):
        sig = sigmoid(pre)
        d_pre = d_act * (sig * (1.0 + pre * (1.0 - sig)))
        d_ext, sums = conv_back(d_pre, inputs, weight, m_ref[...])
        d_ref[:, :width] = d_ext[LEAD:].astype(BF)
        edge_ref[:LEAD, :width] = d_ext[:LEAD]
        edge_ref[LEAD:, :width] = d_ext[d_ext.shape[0] - LEAD :]
        conv_ref[:, :width] = sums

    @pl.when(step < count)
    def _():
        places = head_of_lane((step + first) * BLOCK_HEADS, BLOCK)
        returned = r_ref[0]
        r_parts = split(returned)
        to_end = expand(wl_ref[...], places)
        steps = expand(dt_ref[...], places)
        x = x_ref[...]
        d_scaled = dx_ref[...] + to_end * three(mm, split(bc_ref[:, :STATE]), r_parts)
        g_ref[...] += fold(x * d_scaled, places)
        db_ref[...] += three(mm_nt, split(to_end * steps * x), r_parts)
        flow = jnp.sum(returned * end_ref[0], axis=0, keepdims=True)
        high, middle, low = parts_of(jnp.broadcast_to(flow, (8, BLOCK)))
        flow_ref[...] += mm_nt(high, places) + mm_nt(middle, places) + mm_nt(low, places)
        d_x = steps * d_scaled + skip_ref[...] * dy_ref[...]
        conv(d_x, pre_ref[...], in_ref[...].astype(F32), w_ref[...], BLOCK)

    if not extra:
        return

    @pl.when(step == count)
    def _():
        width = 2 * STATE
        d_bc = jnp.concatenate([dbc_ref[:, :STATE] + db_ref[...], dbc_ref[:, STATE:] + dc_ref[...]], axis=1)
        conv(d_bc, pre_bc[...], in_bc[...].astype(F32), w_bc[...], width)
        masks = m_ref[...]
        steps, rate, shifted = dt_ref[...], rate_ref[...], shifted_ref[...]
        difference = q_ref[...] - steps * g_ref[...]
        d_log = (flow_ref[0:1] + running_sum(difference, True)) * masks[:, CONV_K - 2 : CONV_K - 1]
        d_steps = g_ref[...] - rate * d_log
        d_dt = d_steps * sigmoid(shifted)
        head = lax.broadcasted_iota(jnp.int32, d_dt.shape, 1) < HEADS
        d_dt = jnp.where(head, d_dt, 0.0)
        d_ref[:, width : width + STATE] = d_dt.astype(BF)
        edge_ref[:LEAD, width : width + STATE] = jnp.zeros((LEAD, STATE), F32)
        edge_ref[LEAD:, width : width + STATE] = d_dt[d_dt.shape[0] - LEAD :]
        conv_ref[:, width : width + STATE] = jnp.zeros((8, STATE), F32)
        heads_ref[0:8] = jnp.broadcast_to(jnp.sum(d_dt, axis=0, keepdims=True), (8, STATE))
        log_sum = -jnp.sum(steps * rate * d_log, axis=0, keepdims=True)
        heads_ref[8:16] = jnp.broadcast_to(log_sum, (8, STATE))


def woven(ref, devices, rows):
    pieces = [ref[side, d * rows : d * rows + rows, :] for d in range(devices) for side in range(2)]
    return jnp.concatenate(pieces, axis=0)


def d_final_body(devices, rows, g_ref, w_ref, o_ref):
    o_ref[...] = mm_nt(g_ref[...], woven(w_ref, devices, rows))


def layer_body(devices, rows, f_ref, w_ref, t_ref, o_ref, total):
    @pl.when(pl.program_id(0) == 0)
    def _():
        total[...] = t_ref[...].astype(F32)

    total[...] += mm(f_ref[...], woven(w_ref, devices, rows))

    @pl.when(pl.program_id(0) == pl.num_programs(0) - 1)
    def _():
        o_ref[...] = total[...].astype(BF)


def back_z_body(d_ref, w_ref, o_ref):
    half = w_ref.shape[2]
    o_ref[...] = mm_nt(d_ref[:, :half], w_ref[0]) + mm_nt(d_ref[:, half:], w_ref[1])


def back_x_body(da_ref, db_ref, w_ref, part_ref, o_ref):
    half = da_ref.shape[1]
    o_ref[...] = part_ref[...] + mm_nt(da_ref[...], w_ref[:, :half]) + mm_nt(db_ref[...], w_ref[:, half:])


def back_norm_body(d_ref, x_ref, og_ref, gain_ref, o_ref, sum_ref):
    @pl.when(pl.program_id(0) == 0)
    def _():
        sum_ref[...] = jnp.zeros_like(sum_ref)

    d_normed = d_ref[...]
    x = x_ref[...].astype(F32)
    scale = lax.rsqrt(jnp.mean(x * x, axis=-1, keepdims=True) + EPS)
    unit = x * scale
    pulled = d_normed * gain_ref[...]
    inner = jnp.mean(pulled * unit, axis=-1, keepdims=True)
    o_ref[...] = og_ref[...].astype(F32) + scale * (pulled - unit * inner)
    total = jnp.sum(d_normed * unit, axis=0, keepdims=True)
    sum_ref[...] += jnp.broadcast_to(total, sum_ref.shape)


def swap(array, axis):
    return lax.ppermute(array, axis, [(0, 1), (1, 0)])


def from_behind(array, by):
    peers = lax.axis_size(CTX[0]) * lax.axis_size(CTX[1])
    pairs = [(i, i + by) for i in range(peers) if 0 <= i + by < peers]
    return lax.ppermute(array, CTX, pairs)


def entering(state, decay, reverse, fills):
    fills = list(fills)

    def meanwhile(sent, arrived):
        return tie(arrived, *fills.pop(0)(sent)) if fills else arrived

    depth, width = lax.axis_size("z"), lax.axis_size("y")
    place_z, place_y = lax.axis_index("z"), lax.axis_index("y")
    if width != 2:
        gathered = lax.all_gather(jnp.concatenate([state, decay], axis=1), CTX)
        while fills:
            gathered = meanwhile(state, gathered)
        count = depth * width
        place = place_z * width + place_y
        ahead = count - 1 - place if reverse else place

        def one(lap, running):
            source = count - 1 - lap if reverse else lap
            item = lax.dynamic_index_in_dim(gathered, source, 0, False)
            return item[:, STATE : STATE + 1] * running + item[:, :STATE]

        return lax.fori_loop(0, ahead, one, jnp.zeros_like(state))
    second = place_y == (0 if reverse else 1)
    sent = pick(state, 1 - place_y)
    got = meanwhile(sent, swap(sent, "y"))
    own = pick(state, place_y)
    decay_own = pick(decay, place_y)[:1]
    decay_got = swap(pick(decay, 1 - place_y), "y")[:1]
    early = jnp.where(second, got, own)
    late = jnp.where(second, own, got)
    decay_early = jnp.where(second, decay_got, decay_own)
    decay_late = jnp.where(second, decay_own, decay_got)
    total = decay_late * early + late
    decay_total = decay_early * decay_late
    before = jnp.zeros_like(total)
    sent = total
    turn = depth - 1 - place_z if reverse else place_z
    for hop in range(1, depth):
        pairs = [(depth - hop, depth - 1 - hop)] if reverse else [(hop - 1, hop)]
        arrived = meanwhile(sent, lax.ppermute(sent, "z", pairs))
        before = jnp.where(turn == hop, arrived, before)
        sent = decay_total * before + total
    middle = decay_early * before + early
    mine = jnp.where(second, middle, before)
    sent = jnp.where(second, before, middle)
    theirs = swap(sent, "y")
    while fills:
        theirs = meanwhile(sent, theirs)
    return in_order(mine, theirs, "y")


def pick(parts, index, dim=0):
    return lax.dynamic_index_in_dim(parts, index, dim, False)


def in_order(mine, theirs, axis):
    first = lax.axis_index(axis) == 0
    return jnp.where(first, jnp.stack([mine, theirs]), jnp.stack([theirs, mine]))


def across(array, axis, by):
    return lax.ppermute(array, axis, [(i, i ^ by) for i in range(lax.axis_size(axis))])


def products_body(
    patched, place_ref, sent_own, kept_own, sent_other, kept_other, own_ref, other_ref, *refs
):
    sent_ref, kept_ref = refs[-2:]
    own, other = own_ref[...], other_ref[...]
    if patched:
        upto = own.shape[0] - LEAD
        own = jnp.concatenate([own[:upto], refs[0][...]], axis=0)
        other = jnp.concatenate([other[:upto], refs[1][...]], axis=0)

    def product(first, second):
        first, second = first[...], second[...]
        first = first.reshape(-1, first.shape[-1])
        second = second.reshape(-1, second.shape[-1])
        return mm(first, own) + mm(second, other)

    sent_ref[...] = product(sent_own, sent_other).astype(BF)
    kept_ref[...] = product(kept_own, kept_other)


def products(left, right, start, count, axis, waits):
    own, other = left
    sizes = [lax.axis_size(a) for a in ("x", "z", "y")]
    tokens = own.shape[1]
    rows = other.shape[0] // sizes[0] // sizes[1] // sizes[2]
    out_rows = other.shape[0] // 2
    places = jnp.stack([lax.axis_index(a) for a in ("core", "x", "y")])
    if axis == "x":
        own = own.reshape(2, 2, out_rows, tokens)
        other = other.reshape(2, out_rows, tokens)
        own_block, other_block = (1, 1, out_rows, tokens), (1, out_rows, tokens)

        def spec(mine, flip):
            if mine:
                return pl.BlockSpec(own_block, lambda g, p: (p[1] ^ flip, p[0], 0, 0))
            return pl.BlockSpec(other_block, lambda g, p: (p[1] ^ flip, 0, 0))
    else:
        own = own.reshape(2, 2, sizes[1], 2, rows, tokens)
        other = other.reshape(2 * sizes[1], 2, rows, tokens)
        own_block = (2, 1, sizes[1], 1, rows, tokens)
        other_block = (2 * sizes[1], 1, rows, tokens)

        def spec(mine, flip):
            if mine:
                return pl.BlockSpec(own_block, lambda g, p: (0, p[0], 0, p[2] ^ flip, 0, 0))
            return pl.BlockSpec(other_block, lambda g, p: (0, p[2] ^ flip, 0, 0))

    block = 384 if count % 384 == 0 else 512
    first = start // block
    columns_of = pl.BlockSpec((tokens, block), lambda g, p: (0, g + first))
    edge_of = pl.BlockSpec((LEAD, block), lambda g, p: (0, g + first))
    result = pl.BlockSpec((out_rows, block), lambda g, p: (0, g))
    return call(
        functools.partial(products_body, len(right) > 2), -(-count // block), count * out_rows / 2.0e5,
        [
            (own, spec(True, 1)), (own, spec(True, 0)), (other, spec(False, 1)), (other, spec(False, 0)),
            (right[0], columns_of), (right[1], columns_of),
            *[(edge, edge_of) for edge in right[2:]],
        ],
        [(out((out_rows, count), BF), result), (out((out_rows, count)), result)],
        waits=waits,
        places=places,
    )


def products_any(left, right, start, count, axis):
    core, place = lax.axis_index("core"), lax.axis_index(axis)
    sizes = [lax.axis_size(a) for a in ("x", "z", "y")]
    own = core_rows(left[0], core).reshape(left[1].shape)
    both = jnp.concatenate([own, left[1]], axis=1)
    view = both.reshape(*sizes, -1, both.shape[1])
    if axis == "y":
        view = jnp.moveaxis(view, 2, 0)
    view = view.reshape(view.shape[0], -1, both.shape[1])
    if len(right) > 2:
        upto = right[0].shape[0] - LEAD
        right = [right[0][:upto], right[2], right[1][:upto], right[3]]
    right = jnp.concatenate(right, axis=0)[:, start : start + count]
    sent = [mm(pick(view, place ^ by), right).astype(BF) for by in range(1, view.shape[0])]
    return sent, mm(pick(view, place), right)


def total_of(kept, got):
    for piece in got:
        kept = kept + piece.astype(F32)
    return kept


def tied(value, others):
    return tie(value, *others) if others else value


def xor_parts(parts, axis):
    count, place = lax.axis_size(axis), lax.axis_index(axis)
    return pick(parts, place), [pick(parts, place ^ by).astype(BF) for by in range(1, count)]


def travel(sent, axis, others):
    return [across(tied(piece, others), axis, by + 1) for by, piece in enumerate(sent)]


class Reduction:
    def __init__(self, left, right, start, middle, end, waits=()):
        if lax.axis_size("x") == 2 and lax.axis_size("y") == 2:
            sent_x, self.kept_x = products(left, right, start, middle - start, "x", waits)
            sent_y, self.kept_y = products(left, right, middle, end - middle, "y", waits)
            self.sent_x, self.sent_y = [sent_x], [sent_y]
        else:
            self.sent_x, self.kept_x = products_any(left, right, start, middle - start, "x")
            self.sent_y, self.kept_y = products_any(left, right, middle, end - middle, "y")

    def made(self):
        return [self.kept_x, self.kept_y, *self.sent_x, *self.sent_y]

    def launch(self, *others):
        self.got_x = travel(self.sent_x, "x", others)
        self.got_y = travel(self.sent_y, "y", others)

    def second(self, *others):
        sizes = [lax.axis_size(a) for a in ("x", "z", "y")]
        part_x = total_of(tied(self.kept_x, others), self.got_x)
        part_y = total_of(tied(self.kept_y, others), self.got_y)
        view_x = part_x.reshape(sizes[1], sizes[2], -1, part_x.shape[1])
        view_y = part_y.reshape(sizes[0], sizes[1], -1, part_y.shape[1])
        self.own_x, self.next_x = xor_parts(jnp.moveaxis(view_x, 1, 0), "y")
        self.own_y, self.next_y = xor_parts(view_y, "x")
        self.came_x = travel(self.next_x, "y", ())
        self.came_y = travel(self.next_y, "x", ())

    def third(self, *others):
        done_x = total_of(tied(self.own_x, others), self.came_x)
        done_y = total_of(tied(self.own_y, others), self.came_y)
        self.parts = jnp.concatenate([done_x, done_y], axis=2)
        self.got_z = lax.all_to_all(self.parts, "z", 0, 0, tiled=True)

    def last(self, *others):
        return jnp.sum(tied(self.got_z, others), axis=0)


def core_rows(turned, core):
    view = turned.reshape(lax.axis_size("x"), 2, -1, turned.shape[1])
    return pick(view, core, 1)


def both_cores(turned, core):
    theirs = core_rows(turned, 1 - core)
    return turned, swap(theirs.reshape(-1, turned.shape[1]), "core")


def document_ids(lengths, positions):
    first_end = lengths[0]
    second_end = lengths[0] + lengths[1]
    inside = (positions >= first_end).astype(jnp.int32) + (positions >= second_end).astype(jnp.int32)
    return jnp.where(positions < 0, -1, inside)


def gather_small(pieces, count):
    flat = jnp.concatenate([piece.reshape(-1) for piece in pieces])
    spread = jnp.broadcast_to(flat[None], (count, flat.shape[0]))
    return lax.all_to_all(spread, EVERY, 0, 0, tiled=True)


def columns(array, width):
    return jnp.pad(array, ((0, 0), (0, width - array.shape[1])))


def shards(
    tokens, out_grad, seq_lengths, norm_gain, in_weight, conv_weight, conv_bias,
    dt_bias, a_log, skip_gain, gated_gain, out_weight,
):
    count = 1
    for axis in EVERY:
        count *= lax.axis_size(axis)
    core = lax.axis_index("core")
    place = lax.axis_index("z") * lax.axis_size("y") + lax.axis_index("y")
    row_count, width = tokens.shape
    first_row = place * row_count
    full_rows = LEAD + row_count
    half = INNER // 2
    bc_width = CONVW - INNER
    square = (row_count, row_count)

    lead_tokens = from_behind(tokens[row_count - LEAD :], 1)
    small = gather_small([norm_gain, conv_weight, conv_bias, gated_gain], count)
    weight_x = lax.all_gather(columns(in_weight[:, INNER:], PROJ_X), EVERY, axis=0, tiled=True)
    rows_out = out_weight.shape[0] // 2
    stacked = jnp.stack(
        [in_weight[:, :half], in_weight[:, half:INNER], out_weight[:rows_out], out_weight[rows_out:]]
    )
    stacked = lax.all_gather(stacked, EVERY, axis=1, tiled=True)
    cuts = [norm_gain.size, conv_weight.size, conv_bias.size]
    cuts = [sum(cuts[: i + 1]) for i in range(3)]
    gain_piece, conv_piece, bias_piece, gated_piece = jnp.split(small, cuts, axis=1)
    full_gain = gain_piece.reshape(1, -1).astype(F32)
    full_conv = jnp.moveaxis(conv_piece.reshape(count, CONV_K, -1), 1, 0).reshape(CONV_K, -1)
    full_conv = jnp.pad(full_conv.astype(F32), ((0, 4), (0, 0)))
    full_bias = bias_piece.reshape(1, -1).astype(F32)
    full_gated = gated_piece.reshape(1, -1).astype(F32)

    normed_ext, turned = call(
        norm_body, 1, 4,
        [
            (lead_tokens, whole(LEAD, width)),
            (tokens, whole(row_count, width)),
            (full_gain, whole(1, width)),
        ],
        [
            (out((full_rows, width), BF), whole(full_rows, width)),
            (out((width, row_count), BF), whole(width, row_count)),
        ],
    )
    normed = normed_ext[LEAD:]
    normed_left = both_cores(turned, core)
    out_grad_theirs = swap(out_grad, "core")

    lengths = seq_lengths[0]
    ordinal = jnp.arange(row_count, dtype=jnp.int32)
    doc_ids = document_ids(lengths, first_row + ordinal)
    doc_before = document_ids(lengths, first_row - 1 + jnp.zeros((1,), jnp.int32))
    marks = [
        document_ids(lengths, first_row + ordinal - (CONV_K - 1 - tap)) == doc_ids
        for tap in range(CONV_K)
    ]
    marks = marks + [doc_ids, doc_ids == doc_before[0], doc_ids == doc_ids[row_count - 1]]
    masks = columns(jnp.stack([mark.astype(F32) for mark in marks], axis=1), 128)
    doc_rows = jnp.broadcast_to(doc_ids.astype(F32)[None], (8, row_count))
    rate = columns(jnp.exp(a_log)[None], 128)
    shift = columns(dt_bias[None], 128)
    skip_wide = jnp.repeat(skip_gain, HEAD_DIM)[None]
    mixed_x = mm(normed_ext, weight_x).astype(BF)

    block_bc = pl.BlockSpec((full_rows, bc_width), lambda g: (0, INNER // bc_width))
    block_dr = pl.BlockSpec((full_rows, 128), lambda g: (0, CONVW // 128))
    per_token = whole(row_count, 128)
    a_token = (out((row_count, 128)), per_token)
    pre_bc, act_bc, act_t, scores, scores_t, steps, enter, to_end, cumulative, cum_turned, shifted = call(
        prep_bc_body, 1, 6,
        [
            (mixed_x, block_bc),
            (mixed_x, block_dr),
            (full_conv[:, INNER:], whole(8, bc_width)),
            (full_bias[:, INNER:], whole(1, bc_width)),
            (masks, per_token),
            (doc_rows, whole(8, row_count)),
            (shift, whole(1, 128)),
            (rate, whole(1, 128)),
        ],
        [
            (out((row_count, bc_width)), whole(row_count, bc_width)),
            (out((row_count, bc_width)), whole(row_count, bc_width)),
            (out((bc_width, row_count)), whole(bc_width, row_count)),
            (out(square), whole(*square)),
            (out(square), whole(*square)),
            a_token, a_token, a_token, a_token,
            (out((128, row_count)), whole(128, row_count)),
            a_token,
        ],
    )
    pre_x, act_x, state_local, device_decay = call(
        prep_x_body, INNER // BLOCK, 12,
        [
            (mixed_x, lanes(full_rows, BLOCK)),
            (full_conv[:, :INNER], lanes(8, BLOCK)),
            (full_bias[:, :INNER], lanes(1, BLOCK)),
            (masks, per_token),
            (to_end, per_token),
            (steps, per_token),
            (enter, per_token),
            (act_t, whole(bc_width, row_count)),
        ],
        [
            (out((row_count, INNER)), lanes(row_count, BLOCK)),
            (out((row_count, INNER)), lanes(row_count, BLOCK)),
            (out((2, STATE, half)), halves(STATE, BLOCK)),
            (out((2, 8, half)), halves(8, BLOCK)),
        ],
    )

    heads_block = 2 * PAIRS
    groups = HEADS // heads_block
    half_groups = groups // 2
    cum_rows = cum_turned[:HEADS].reshape(groups, heads_block, row_count)
    kept = {}

    def pairs_at(index):
        return pl.BlockSpec((row_count, PAIR_LANES), lambda g: (0, g + index * half_groups))

    def cums_at(index):
        return pl.BlockSpec((1, heads_block, row_count), lambda g: (g + index * half_groups, 0, 0))

    def intra(index, wait):
        kept[index] = call(
            functools.partial(intra_body, index * half_groups), half_groups, 12,
            [
                (act_x, pairs_at(index)),
                (steps, per_token),
                (skip_wide, pl.BlockSpec((1, PAIR_LANES), lambda g: (0, g + index * half_groups))),
                (scores, whole(*square)),
                (cumulative, per_token),
                (cum_rows, cums_at(index)),
            ],
            [(out((row_count, half)), lanes(row_count, PAIR_LANES))],
            waits=[wait],
        )[0]
        return [kept[index]]

    devices = 4
    out_block = 2 * devices * rows_out
    out_blocks = count // devices
    weight_block = pl.BlockSpec((2, devices * rows_out, width), lambda g: (1, g, 0))
    direct = rows_out % 16 == 0

    def project(wait):
        if direct:
            kept["d_final"] = call(
                functools.partial(d_final_body, devices, rows_out), out_blocks, 7,
                [(out_grad, whole(row_count, width)), (stacked, weight_block)],
                [(out((row_count, INNER)), lanes(row_count, out_block))],
                waits=[wait],
            )[0]
        else:
            weight_o = jnp.moveaxis(stacked[2:].reshape(2, count, rows_out, width), 0, 1)
            kept["weight_o"] = weight_o.reshape(-1, width)
            kept["d_final"] = mm_nt(out_grad, kept["weight_o"])
        kept["mixed_z"] = [mm(normed, stacked[side]).astype(BF) for side in range(2)]
        return [kept["d_final"], *kept["mixed_z"]]

    state_in = entering(
        state_local, device_decay, False,
        [
            lambda wait: intra(0, wait), lambda wait: intra(1, wait), lambda wait: [], lambda wait: [],
            project,
        ],
    )
    state_end = device_decay[:, :1] * state_in + state_local

    tile = 128
    final, final_turned, d_z, d_y, returned_local, d_c_carry, dy_y, sums = call(
        gate_body, row_count // tile, 31,
        [
            (kept[0], rows_of(tile, half)),
            (kept[1], rows_of(tile, half)),
            (kept["mixed_z"][0], rows_of(tile, half)),
            (kept["mixed_z"][1], rows_of(tile, half)),
            (kept["d_final"], rows_of(tile, INNER)),
            (act_x, rows_of(tile, INNER)),
            (act_bc[:, STATE:], rows_of(tile, STATE)),
            (act_t[STATE:], lanes(STATE, tile)),
            (state_in, whole(2, STATE, half)),
            (enter, rows_of(tile, 128)),
            (full_gated, whole(1, INNER)),
            (skip_wide, whole(1, INNER)),
        ],
        [
            (out((row_count, INNER), BF), rows_of(tile, INNER)),
            (out((INNER, row_count), BF), lanes(INNER, tile)),
            (out((row_count, INNER), BF), rows_of(tile, INNER)),
            (out((row_count, INNER)), rows_of(tile, INNER)),
            (out((2, STATE, half)), whole(2, STATE, half)),
            (out((row_count, STATE)), rows_of(tile, STATE)),
            (out((row_count, 128)), rows_of(tile, 128)),
            (out((16, INNER)), whole(16, INNER)),
        ],
        [pltpu.VMEM((tile, INNER), F32), pltpu.VMEM((tile, INNER), F32)],
    )

    final_left = both_cores(final_turned, core)
    d_z_theirs = swap(d_z, "core")
    back = {"acc": jnp.zeros(square, F32)}

    def out_sums(wait):
        back["out"] = Reduction(final_left, [out_grad, out_grad_theirs], 0, width // 2, width, [wait])
        back["out"].launch()
        return back["out"].made()

    def z_sums(wait):
        back["z"] = Reduction(normed_left, [d_z, d_z_theirs], 0, half, INNER, [wait])
        back["z"].launch()
        return back["z"].made()

    def within(index, wait):
        ends = [(out((row_count, bc_width)), whole(row_count, bc_width))] if index else []
        back[index], back["acc"], *back["bc"] = call(
            functools.partial(back_body, index * half_groups), half_groups, 18,
            [
                (act_x, pairs_at(index)),
                (d_y, pairs_at(index)),
                (steps, per_token),
                (scores_t, whole(*square)),
                (cumulative, per_token),
                (cum_rows, cums_at(index)),
                (act_bc, whole(row_count, bc_width)),
                (doc_rows, whole(8, row_count)),
                (masks, per_token),
                (back["acc"], whole(*square)),
            ],
            [
                (out((row_count, half)), lanes(row_count, PAIR_LANES)),
                (out(square), whole(*square)),
                *ends,
            ],
            waits=[wait],
        )
        return [back[index]]

    def first_within(wait):
        back["out"].second(wait)
        return within(0, wait)

    def second_within(wait):
        return within(1, wait)

    norm_block = 256

    def back_z(wait):
        back["d_normed"] = call(
            back_z_body, width // norm_block, 10,
            [
                (d_z, whole(row_count, INNER)),
                (stacked, pl.BlockSpec((2, norm_block, half), lambda g: (0, g, 0))),
            ],
            [(out((row_count, width)), lanes(row_count, norm_block))],
            waits=[wait],
        )[0]
        back["z"].second(wait)
        back["out"].third(wait)
        return [back["d_normed"], back["out"].parts, *back["z"].next_x, *back["z"].next_y]

    returned = entering(
        returned_local, device_decay, True,
        [out_sums, z_sums, first_within, second_within, back_z],
    )

    blocks = half // BLOCK

    def carried(index, earlier, extra, extra_out, waits):
        steps_count = blocks + len(extra_out)
        own = pl.BlockSpec((row_count, BLOCK), lambda g: (0, jnp.minimum(g, blocks - 1)))

        def at(rows):
            return pl.BlockSpec((rows, BLOCK), lambda g: (0, jnp.minimum(g, blocks - 1) + index * blocks))

        state_at = pl.BlockSpec((1, STATE, BLOCK), lambda g: (index, 0, jnp.minimum(g, blocks - 1)))
        wide = half + len(extra_out) * (PROJ_X - INNER)
        return call(
            functools.partial(carry_body, index * blocks), steps_count, 14 + 4 * index,
            [
                (back[index], own),
                (act_x, at(row_count)),
                (d_y, at(row_count)),
                (pre_x, at(row_count)),
                (mixed_x, at(full_rows)),
                (full_conv[:, :INNER], at(8)),
                (masks, per_token),
                (act_bc, whole(row_count, bc_width)),
                (returned, state_at),
                (state_end, state_at),
                (to_end, per_token),
                (steps, per_token),
                (skip_wide, at(1)),
                *[(array, whole(*array.shape)) for array in earlier],
                *extra,
            ],
            [
                *extra_out,
                (out((row_count, wide), BF), lanes(row_count, BLOCK)),
                (out((2 * LEAD, wide)), lanes(2 * LEAD, BLOCK)),
                (out((8, wide)), lanes(8, BLOCK)),
                (out((row_count, STATE)), whole(row_count, STATE)),
                a_token,
                (out((8, 128)), whole(8, 128)),
            ],
            waits=waits,
        )

    none = jnp.zeros((row_count, 128), F32)
    d_xa, edge_a, conv_a, *so_far = carried(0, [none, none, none[:8]], [], [], [])
    back["z"].third(edge_a)
    d_xa_theirs = swap(d_xa, "core")
    halo_a = from_behind(edge_a[:LEAD], -1)
    last_a = (edge_a[LEAD:] + halo_a).astype(BF)
    last_a_theirs = swap(last_a, "core")
    sums_a = Reduction(normed_left, [d_xa, d_xa_theirs, last_a, last_a_theirs], 0, half // 2, half, [back["z"].parts, back["out"].got_z])
    sums_a.launch()
    heads, d_xb, edge_b, conv_b, *_ = carried(
        1, so_far,
        [
            (pre_bc, whole(row_count, bc_width)),
            (mixed_x, block_bc),
            (full_conv[:, INNER:], whole(8, bc_width)),
            (back["bc"][0], whole(row_count, bc_width)),
            (d_c_carry, whole(row_count, STATE)),
            (shifted, per_token),
            (rate, whole(1, 128)),
            (dy_y, per_token),
        ],
        [(out((16, 128)), whole(16, 128))],
        sums_a.made(),
    )
    d_xb_theirs = swap(d_xb, "core")
    halo_b = from_behind(edge_b[:LEAD], -1)
    sums_a.second(edge_b)
    sums_a.third()
    last_b = (edge_b[LEAD:] + halo_b).astype(BF)
    last_b_theirs = swap(last_b, "core")
    wide_b = d_xb.shape[1]
    sums_b = Reduction(
        normed_left, [d_xb, d_xb_theirs, last_b, last_b_theirs], 0, 1024, wide_b, [sums_a.parts]
    )
    sums_b.launch()

    d_xa = lax.dynamic_update_slice(d_xa, last_a, (row_count - LEAD, 0))
    d_xb = lax.dynamic_update_slice(d_xb, last_b, (row_count - LEAD, 0))
    d_normed = call(
        back_x_body, width // norm_block, 10,
        [
            (d_xa, whole(row_count, half)),
            (d_xb, whole(row_count, wide_b)),
            (weight_x, rows_of(norm_block, PROJ_X)),
            (back["d_normed"], lanes(row_count, norm_block)),
        ],
        [(out((row_count, width)), lanes(row_count, norm_block))],
        waits=sums_b.made(),
    )[0]
    grad_tokens, gain_sums = call(
        back_norm_body, row_count // tile, 4,
        [
            (d_normed, rows_of(tile, width)),
            (tokens, rows_of(tile, width)),
            (out_grad, rows_of(tile, width)),
            (full_gain, whole(1, width)),
        ],
        [
            (out((row_count, width)), rows_of(tile, width)),
            (out((8, width)), whole(8, width)),
        ],
    )
    sums_b.second(grad_tokens)
    if direct:
        layer_out = call(
            functools.partial(layer_body, devices, rows_out), out_blocks, 13,
            [
                (final, lanes(row_count, out_block)),
                (stacked, weight_block),
                (tokens, whole(row_count, width)),
            ],
            [(out((row_count, width), BF), whole(row_count, width))],
            [pltpu.VMEM((row_count, width), F32)],
            waits=[*sums_b.next_x, *sums_b.next_y],
        )[0]
    else:
        layer_out = (tokens.astype(F32) + mm(final, kept["weight_o"])).astype(BF)

    conv_sums = jnp.concatenate([conv_a, conv_b[:, : CONVW - half]], axis=1)
    grad_skip = jnp.sum(jnp.sum(sums[8:], axis=0).reshape(HEADS, HEAD_DIM), axis=1)
    grad_gated = jnp.sum(sums[:8], axis=0)
    per_device = jnp.concatenate(
        [
            gain_sums[0].reshape(count, -1),
            jnp.moveaxis(conv_sums[:CONV_K].reshape(CONV_K, count, -1), 1, 0).reshape(count, -1),
            conv_sums[CONV_K].reshape(count, -1),
            grad_gated.reshape(count, -1),
            jnp.broadcast_to(
                jnp.concatenate([heads[0, :HEADS], heads[8, :HEADS], grad_skip])[None],
                (count, 3 * HEADS),
            ),
        ],
        axis=1,
    )
    sums_b.third()
    per_device = tie(per_device, *sums_b.next_x, *sums_b.next_y)
    arrived = lax.all_to_all(per_device, EVERY, 0, 0, tiled=True)
    done = [layer_out]
    sum_out, sum_in_z, sum_in_a = [each.last(*done) for each in (back["out"], back["z"], sums_a)]
    sum_in_b = sums_b.last()
    small_sums = jnp.sum(tie(arrived, layer_out), axis=0)
    cuts = [norm_gain.size, conv_weight.size, conv_bias.size, gated_gain.size, HEADS, HEADS]
    cuts = [sum(cuts[: i + 1]) for i in range(6)]
    sum_gain, sum_conv, sum_bias, sum_gated, sum_dt, sum_log, sum_skip = jnp.split(small_sums, cuts)
    sum_in = jnp.concatenate([sum_in_z, sum_in_a, sum_in_b[:, : in_weight.shape[1] - INNER - half]], axis=1)
    return (
        layer_out,
        grad_tokens,
        sum_gain,
        sum_in,
        sum_conv.reshape(conv_weight.shape),
        sum_bias,
        sum_dt,
        sum_log,
        sum_skip,
        sum_gated,
        sum_out,
    )


def solution(mesh):
    x = mesh.shape["dp"] // 2
    y = x
    z = mesh.shape["ctx"] // y
    fine = Mesh(mesh.devices.reshape(x, 2, z, y), EVERY)
    rows = P(EVERY, None)
    flat = P(EVERY)
    in_specs = (
        rows, rows, P(("x", "core"), None), flat, rows, P(None, EVERY), flat,
        P(), P(), P(), flat, rows,
    )
    out_specs = (rows, rows, flat, rows, P(None, EVERY), flat, P(), P(), P(), flat, rows)
    return jax.shard_map(shards, mesh=fine, in_specs=in_specs, out_specs=out_specs, check_vma=False)
```

```python
import functools

import jax
import jax.numpy as jnp
from jax import lax
from jax.experimental import pallas as pl
from jax.experimental.pallas import tpu as pltpu
from jax.sharding import Mesh, PartitionSpec as P

HEADS = 48
HEAD_DIM = 64
STATE = 128
CONV_K = 4
INNER = 3072
CONVW = 3328
LEAD = 16
PROJ_X = 3456
BLOCK = 512
BLOCK_HEADS = BLOCK // HEAD_DIM
PAIRS = 2
PAIR_LANES = 128 * PAIRS
VMEM = 56 * 1024 * 1024
F32 = jnp.float32
BF = jnp.bfloat16
EPS = 1e-05
highest = lax.Precision.HIGHEST
EVERY = ("x", "core", "z", "y")
CTX = ("z", "y")


def params():
    return pltpu.CompilerParams(vmem_limit_bytes=VMEM, dimension_semantics=("arbitrary",))


def call(body, grid, micros, ins, outs, scratch=(), waits=(), places=None):
    first = (places is not None) + len(ins)
    anywhere = pl.BlockSpec(memory_space=pl.ANY)

    def run(*refs):
        body(*refs[:first], *refs[first + len(waits) :])

    scalars = [] if places is None else [places]
    return pl.pallas_call(
        run,
        grid_spec=pltpu.PrefetchScalarGridSpec(
            num_scalar_prefetch=len(scalars),
            grid=(grid,),
            in_specs=[spec for _, spec in ins] + [anywhere] * len(waits),
            out_specs=[spec for _, spec in outs],
            scratch_shapes=list(scratch),
        ),
        out_shape=[shape for shape, _ in outs],
        compiler_params=params(),
        cost_estimate=pl.CostEstimate(
            flops=int(micros * 1e9), bytes_accessed=int(micros * 3e6), transcendentals=0
        ),
    )(*scalars, *[array for array, _ in ins], *waits)


def tie(value, *others):
    def body(*refs):
        pass

    anywhere = pl.BlockSpec(memory_space=pl.ANY)
    return pl.pallas_call(
        body,
        in_specs=[anywhere] * (1 + len(others)),
        out_specs=anywhere,
        out_shape=jax.ShapeDtypeStruct(value.shape, value.dtype),
        input_output_aliases={0: 0},
    )(value, *others)


def whole(*shape):
    return pl.BlockSpec(shape, lambda g: (0,) * len(shape))


def lanes(rows, width):
    return pl.BlockSpec((rows, width), lambda g: (0, g))


def rows_of(count, width):
    return pl.BlockSpec((count, width), lambda g: (g, 0))


def halves(rows, width):
    count = INNER // 2 // width
    return pl.BlockSpec((1, rows, width), lambda g: (g // count, 0, g % count))


def group(rows, width):
    return pl.BlockSpec((1, rows, width), lambda g: (g, 0, 0))


def out(shape, dtype=F32):
    return jax.ShapeDtypeStruct(shape, dtype)


def split(value):
    high = value.astype(BF)
    return high, (value - high.astype(F32)).astype(BF)


def mm(left, right):
    return jnp.dot(left, right, preferred_element_type=F32)


def mm_nt(left, right):
    return lax.dot_general(left, right, (((1,), (1,)), ((), ())), preferred_element_type=F32)


def mm_tn(left, right):
    return lax.dot_general(left, right, (((0,), (0,)), ((), ())), preferred_element_type=F32)


def three(product, left, right):
    left_high, left_low = left
    right_high, right_low = right
    return (
        product(left_high, right_high)
        + product(left_high, right_low)
        + product(left_low, right_high)
    )


def head_of_lane(first, count):
    lane = lax.broadcasted_iota(jnp.int32, (STATE, count), 1) // HEAD_DIM + first
    row = lax.broadcasted_iota(jnp.int32, (STATE, count), 0)
    return (lane == row).astype(BF)


def expand(value, places):
    high, low = split(value)
    return mm(high, places) + mm(low, places)


def fold(value, places):
    high, low = split(value)
    return mm_nt(high, places) + mm_nt(low, places)


def sigmoid(value):
    return 1.0 / (1.0 + jnp.exp(-value))


def conv_pre(extended, weight, bias, masks):
    running = jnp.zeros((masks.shape[0], extended.shape[1]), F32) + bias
    for tap in range(CONV_K):
        shifted = extended if tap == CONV_K - 1 else pltpu.roll(extended, CONV_K - 1 - tap, 0)
        running = running + shifted[LEAD:] * weight[tap : tap + 1] * masks[:, tap : tap + 1]
    return running


def conv_back(d_pre, extended, weight, masks):
    zeros = jnp.zeros((LEAD, d_pre.shape[1]), F32)
    total = LEAD + d_pre.shape[0]
    d_ext = jnp.zeros((total, d_pre.shape[1]), F32)
    weight_rows = []
    for tap in range(CONV_K):
        by = CONV_K - 1 - tap
        part = d_pre * masks[:, tap : tap + 1]
        padded = jnp.concatenate([zeros, part], axis=0)
        shifted = extended
        if by:
            padded = pltpu.roll(padded, total - by, 0)
            shifted = pltpu.roll(extended, by, 0)
        d_ext = d_ext + padded * weight[tap : tap + 1]
        weight_rows.append(jnp.sum(shifted[LEAD:] * part, axis=0, keepdims=True))
    weight_rows.append(jnp.sum(d_pre, axis=0, keepdims=True))
    weight_rows.append(jnp.zeros((8 - len(weight_rows), d_pre.shape[1]), F32))
    return d_ext, jnp.concatenate(weight_rows, axis=0)


def same_mask(doc_row, doc_col, transposed):
    count = doc_row.shape[1]
    rows = lax.broadcasted_iota(jnp.int32, (count, count), 0)
    cols = lax.broadcasted_iota(jnp.int32, (count, count), 1)
    order = rows <= cols if transposed else rows >= cols
    return jnp.where((doc_row == doc_col) & order, 1.0, 0.0)


def norm_body(lead_ref, x_ref, gain_ref, normed_ref, turned_ref):
    def normed(value):
        scale = lax.rsqrt(jnp.mean(value * value, axis=-1, keepdims=True) + EPS)
        return value * scale * gain_ref[...]

    normed_ref[:LEAD] = normed(lead_ref[...].astype(F32)).astype(BF)
    for tile in range(x_ref.shape[0] // 128):
        here = slice(tile * 128, tile * 128 + 128)
        value = normed(x_ref[here].astype(F32))
        normed_ref[LEAD + tile * 128 : LEAD + tile * 128 + 128] = value.astype(BF)
        turned_ref[:, here] = value.T.astype(BF)


def parts_of(value):
    high, low = split(value)
    return high, low, (value - high.astype(F32) - low.astype(F32)).astype(BF)


def running_sum(value, transposed):
    count = value.shape[0]
    rows = lax.broadcasted_iota(jnp.int32, (count, count), 0)
    cols = lax.broadcasted_iota(jnp.int32, (count, count), 1)
    side = ((rows <= cols) if transposed else (rows >= cols)).astype(BF)
    high, middle, low = parts_of(value)
    return mm(side, high) + mm(side, middle) + mm(side, low)


def softplus(value):
    return jnp.maximum(value, 0.0) + jnp.log1p(jnp.exp(-jnp.abs(value)))


def prep_bc_body(
    x_ref, dr_ref, w_ref, b_ref, m_ref, doc_ref, shift_ref, rate_ref,
    pre_ref, act_ref, t_ref, s_ref, st_ref, steps_ref, enter_ref, to_end_ref, cum_ref, turned_ref, dt_ref,
):
    masks = m_ref[...]
    pre = conv_pre(x_ref[...].astype(F32), w_ref[...], b_ref[...], masks)
    act = pre * sigmoid(pre)
    pre_ref[...] = pre
    act_ref[...] = act
    t_ref[...] = act.T
    b_rows, c_rows = split(act[:, :STATE]), split(act[:, STATE:])
    doc_row, doc_col = doc_ref[0:1], masks[:, CONV_K : CONV_K + 1]
    s_ref[...] = three(mm_nt, c_rows, b_rows) * same_mask(doc_row, doc_col, False)
    st_ref[...] = three(mm_nt, b_rows, c_rows) * same_mask(doc_row, doc_col, True)
    shifted = dr_ref[LEAD:, :].astype(F32) + shift_ref[...]
    steps = softplus(shifted)
    cumulative = running_sum(-steps * rate_ref[...], False)
    last = cumulative[cumulative.shape[0] - 1 :]
    dt_ref[...] = shifted
    steps_ref[...] = steps
    enter_ref[...] = jnp.exp(cumulative) * masks[:, CONV_K + 1 : CONV_K + 2]
    to_end_ref[...] = jnp.exp(last - cumulative) * masks[:, CONV_K + 2 : CONV_K + 3]
    cum_ref[...] = cumulative
    turned_ref[...] = cumulative.T


def prep_x_body(
    x_ref, w_ref, b_ref, m_ref, wl_ref, dt_ref, e_ref, t_ref, pre_ref, act_ref, state_ref, decay_ref
):
    pre = conv_pre(x_ref[...].astype(F32), w_ref[...], b_ref[...], m_ref[...])
    act = pre * sigmoid(pre)
    pre_ref[...] = pre
    act_ref[...] = act
    places = head_of_lane(pl.program_id(0) * BLOCK_HEADS, BLOCK)
    weighted = split(act * expand(wl_ref[...] * dt_ref[...], places))
    state_ref[0] = three(mm, split(t_ref[:STATE]), weighted)
    last = e_ref[e_ref.shape[0] - 8 :]
    high, middle, low = parts_of(last)
    spread = mm(high, places) + mm(middle, places) + mm(low, places)
    decay_ref[0] = jnp.broadcast_to(spread[7:8], spread.shape)


def heads_here(cum_ref, first):
    back = STATE - (pl.program_id(0) + first) * 2 * PAIRS
    return pltpu.roll(cum_ref[...], jnp.where(back == STATE, 0, back), 1)


def intra_body(first, x_ref, dt_ref, skip_ref, s_ref, cum_ref, row_ref, y_ref):
    half = s_ref.shape[0] // 2
    places = head_of_lane((pl.program_id(0) + first) * 2 * PAIRS, PAIR_LANES)
    scaled = x_ref[...] * expand(dt_ref[...], places)
    cols = heads_here(cum_ref, first)
    lane = lax.broadcasted_iota(jnp.int32, (2 * half, 128), 1)
    for pair in range(PAIRS):
        here = slice(pair * 128, pair * 128 + 128)
        high, low = split(scaled[:, here])
        right = jnp.concatenate([high, low], axis=1)
        both = []
        for side in range(2):
            head = 2 * pair + side
            col = cols[:, head : head + 1]
            row = row_ref[0, head : head + 1, :]
            top = s_ref[:half, :half] * jnp.exp(jnp.minimum(col[:half] - row[:, :half], 0.0))
            low_part = s_ref[half:, :] * jnp.exp(jnp.minimum(col[half:] - row, 0.0))
            done = []
            for part, count in ((top, half), (low_part, 2 * half)):
                p_high, p_low = split(part)
                first = mm(p_high, right[:count])
                done.append(first[:, :128] + first[:, 128:] + mm(p_low, high[:count]))
            both.append(jnp.concatenate(done, axis=0))
        y_ref[:, here] = (
            jnp.where(lane < HEAD_DIM, both[0], both[1]) + skip_ref[:, here] * x_ref[:, here]
        )


def gate_body(
    ya_ref, yb_ref, za_ref, zb_ref, df_ref, x_ref, c_ref, ct_ref, state_ref, e_ref, gain_ref, skip_ref,
    final_ref, turned_ref, dz_ref, dy_ref, r_ref, dc_ref, q_ref, sums_ref, carry, scaled,
):
    @pl.when(pl.program_id(0) == 0)
    def _():
        r_ref[...] = jnp.zeros_like(r_ref)
        sums_ref[...] = jnp.zeros_like(sums_ref)

    e_high, e_low = split(e_ref[...])
    c_rows = split(c_ref[...])
    for block in range(INNER // BLOCK):
        here = slice(block * BLOCK, block * BLOCK + BLOCK)
        places = head_of_lane(block * BLOCK_HEADS, BLOCK)
        spread = mm(e_high, places) + mm(e_low, places)
        there = slice(block % 3 * BLOCK, block % 3 * BLOCK + BLOCK)
        carry[:, here] = three(mm, c_rows, split(state_ref[block // 3, :, there])) * spread
        scaled[:, here] = spread
    gain, skip = gain_ref[...], skip_ref[...]

    def some(lap, sums):
        at = pl.ds(pl.multiple_of(lap * 16, 16), 16)
        y = jnp.concatenate([ya_ref[at, :], yb_ref[at, :]], axis=1) + carry[at, :]
        z = jnp.concatenate([za_ref[at, :], zb_ref[at, :]], axis=1).astype(F32)
        sig = sigmoid(z)
        gate = z * sig
        gated = y * gate
        scale = lax.rsqrt(jnp.mean(gated * gated, axis=-1, keepdims=True) + EPS)
        unit = gated * scale
        final_ref[at, :] = (unit * gain).astype(BF)
        d_final = df_ref[at, :]
        q = d_final * gain
        inner = jnp.mean(q * unit, axis=-1, keepdims=True)
        d_gated = scale * (q - unit * inner)
        d_y = d_gated * gate
        dz_ref[at, :] = (d_gated * y * (sig * (1.0 + z * (1.0 - sig)))).astype(BF)
        dy_ref[at, :] = d_y
        x = x_ref[at, :]
        scaled[at, :] = scaled[at, :] * d_y
        carry[at, :] = d_y * (y - skip * x)
        d_gain, d_skip = d_final * unit, d_y * x
        return (
            sums[0] + d_gain[:8] + d_gain[8:],
            sums[1] + d_skip[:8] + d_skip[8:],
        )

    zero = jnp.zeros((8, INNER), F32)
    d_gain, d_skip = lax.fori_loop(0, za_ref.shape[0] // 16, some, (zero, zero))
    sums_ref[0:8] += d_gain
    sums_ref[8:16] += d_skip
    ct_rows = split(ct_ref[...])
    d_c = jnp.zeros(dc_ref.shape, F32)
    q_sum = jnp.zeros(q_ref.shape, F32)
    for block in range(INNER // BLOCK):
        here = slice(block * BLOCK, block * BLOCK + BLOCK)
        there = slice(block % 3 * BLOCK, block % 3 * BLOCK + BLOCK)
        piece = split(scaled[:, here])
        r_ref[block // 3, :, there] += three(mm, ct_rows, piece)
        d_c = d_c + three(mm_nt, piece, split(state_ref[block // 3, :, there]))
        turned_ref[here, :] = final_ref[:, here].T
        q_sum = q_sum + fold(carry[:, here], head_of_lane(block * BLOCK_HEADS, BLOCK))
    dc_ref[...] = d_c
    q_ref[...] = q_sum


def back_body(first, x_ref, dy_ref, dt_ref, st_ref, cum_ref, row_ref, bc_ref, doc_ref, m_ref, in_ref, dx_ref, acc, *ends):
    step = pl.program_id(0)
    half = st_ref.shape[0] // 2

    @pl.when(step == 0)
    def _():
        acc[...] = in_ref[...]

    places = head_of_lane((step + first) * 2 * PAIRS, PAIR_LANES)
    scaled = x_ref[...] * expand(dt_ref[...], places)
    cols = heads_here(cum_ref, first)
    lane = lax.broadcasted_iota(jnp.int32, (2 * half, 128), 1)
    for pair in range(PAIRS):
        here = slice(pair * 128, pair * 128 + 128)
        dy_high, dy_low = split(dy_ref[:, here])
        right = jnp.concatenate([dy_high, dy_low], axis=1)
        twice = jnp.concatenate([dy_high, dy_high], axis=1)
        both = []
        for side in range(2):
            head = 2 * pair + side
            mine = (lane < HEAD_DIM) if side == 0 else (lane >= HEAD_DIM)
            x_high, x_low = split(jnp.where(mine, scaled[:, here], 0.0))
            x_both = jnp.concatenate([x_high, x_low], axis=1)
            col = cols[:, head : head + 1]
            row = row_ref[0, head : head + 1, :]
            done = []
            for at, over in ((slice(0, half), slice(0, 2 * half)), (slice(half, 2 * half), slice(half, 2 * half))):
                decay = jnp.exp(jnp.minimum(row[:, over] - col[at], 0.0))
                p_high, p_low = split(st_ref[at, over] * decay)
                first = mm(p_high, right[over])
                done.append(first[:, :128] + first[:, 128:] + mm(p_low, dy_high[over]))
                outer = mm_nt(x_both[at], twice[over]) + mm_nt(x_high[at], dy_low[over])
                acc[at, over] += outer * decay
            both.append(jnp.concatenate(done, axis=0))
        dx_ref[:, here] = jnp.where(lane < HEAD_DIM, both[0], both[1])

    if not ends:
        return

    @pl.when(step == pl.num_programs(0) - 1)
    def _():
        dbc_ref = ends[0]
        doc_col = m_ref[:, CONV_K : CONV_K + 1]
        ds = split(acc[...] * same_mask(doc_ref[0:1], doc_col, True))
        dbc_ref[:, :STATE] = three(mm, ds, split(bc_ref[:, STATE:]))
        dbc_ref[:, STATE:] = three(mm_tn, ds, split(bc_ref[:, :STATE]))


def carry_body(
    first, dx_ref, x_ref, dy_ref, pre_ref, in_ref, w_ref, m_ref, bc_ref, r_ref, end_ref, wl_ref, dt_ref,
    skip_ref, db_in, g_in, flow_in, *refs,
):
    extra = refs[:-6]
    d_ref, edge_ref, conv_ref, db_ref, g_ref, flow_ref = refs[-6:]
    if extra:
        pre_bc, in_bc, w_bc, dbc_ref, dc_ref, shifted_ref, rate_ref, q_ref, heads_ref = extra
    step = pl.program_id(0)
    count = INNER // 2 // BLOCK

    @pl.when(step == 0)
    def _():
        db_ref[...] = db_in[...]
        g_ref[...] = g_in[...]
        flow_ref[...] = flow_in[...]

    def conv(d_act, pre, inputs, weight, width):
        sig = sigmoid(pre)
        d_pre = d_act * (sig * (1.0 + pre * (1.0 - sig)))
        d_ext, sums = conv_back(d_pre, inputs, weight, m_ref[...])
        d_ref[:, :width] = d_ext[LEAD:].astype(BF)
        edge_ref[:LEAD, :width] = d_ext[:LEAD]
        edge_ref[LEAD:, :width] = d_ext[d_ext.shape[0] - LEAD :]
        conv_ref[:, :width] = sums

    @pl.when(step < count)
    def _():
        places = head_of_lane((step + first) * BLOCK_HEADS, BLOCK)
        returned = r_ref[0]
        r_parts = split(returned)
        to_end = expand(wl_ref[...], places)
        steps = expand(dt_ref[...], places)
        x = x_ref[...]
        d_scaled = dx_ref[...] + to_end * three(mm, split(bc_ref[:, :STATE]), r_parts)
        g_ref[...] += fold(x * d_scaled, places)
        db_ref[...] += three(mm_nt, split(to_end * steps * x), r_parts)
        flow = jnp.sum(returned * end_ref[0], axis=0, keepdims=True)
        high, middle, low = parts_of(jnp.broadcast_to(flow, (8, BLOCK)))
        flow_ref[...] += mm_nt(high, places) + mm_nt(middle, places) + mm_nt(low, places)
        d_x = steps * d_scaled + skip_ref[...] * dy_ref[...]
        conv(d_x, pre_ref[...], in_ref[...].astype(F32), w_ref[...], BLOCK)

    if not extra:
        return

    @pl.when(step == count)
    def _():
        width = 2 * STATE
        d_bc = jnp.concatenate([dbc_ref[:, :STATE] + db_ref[...], dbc_ref[:, STATE:] + dc_ref[...]], axis=1)
        conv(d_bc, pre_bc[...], in_bc[...].astype(F32), w_bc[...], width)
        masks = m_ref[...]
        steps, rate, shifted = dt_ref[...], rate_ref[...], shifted_ref[...]
        difference = q_ref[...] - steps * g_ref[...]
        d_log = (flow_ref[0:1] + running_sum(difference, True)) * masks[:, CONV_K - 2 : CONV_K - 1]
        d_steps = g_ref[...] - rate * d_log
        d_dt = d_steps * sigmoid(shifted)
        head = lax.broadcasted_iota(jnp.int32, d_dt.shape, 1) < HEADS
        d_dt = jnp.where(head, d_dt, 0.0)
        d_ref[:, width : width + STATE] = d_dt.astype(BF)
        edge_ref[:LEAD, width : width + STATE] = jnp.zeros((LEAD, STATE), F32)
        edge_ref[LEAD:, width : width + STATE] = d_dt[d_dt.shape[0] - LEAD :]
        conv_ref[:, width : width + STATE] = jnp.zeros((8, STATE), F32)
        heads_ref[0:8] = jnp.broadcast_to(jnp.sum(d_dt, axis=0, keepdims=True), (8, STATE))
        log_sum = -jnp.sum(steps * rate * d_log, axis=0, keepdims=True)
        heads_ref[8:16] = jnp.broadcast_to(log_sum, (8, STATE))


def woven(ref, devices, rows):
    pieces = [ref[side, d * rows : d * rows + rows, :] for d in range(devices) for side in range(2)]
    return jnp.concatenate(pieces, axis=0)


def d_final_body(devices, rows, g_ref, w_ref, o_ref):
    o_ref[...] = mm_nt(g_ref[...], woven(w_ref, devices, rows))


def layer_body(devices, rows, f_ref, w_ref, t_ref, o_ref, total):
    @pl.when(pl.program_id(0) == 0)
    def _():
        total[...] = t_ref[...].astype(F32)

    total[...] += mm(f_ref[...], woven(w_ref, devices, rows))

    @pl.when(pl.program_id(0) == pl.num_programs(0) - 1)
    def _():
        o_ref[...] = total[...].astype(BF)


def back_z_body(d_ref, w_ref, o_ref):
    half = w_ref.shape[2]
    o_ref[...] = mm_nt(d_ref[:, :half], w_ref[0]) + mm_nt(d_ref[:, half:], w_ref[1])


def back_x_body(da_ref, db_ref, w_ref, part_ref, o_ref):
    half = da_ref.shape[1]
    o_ref[...] = part_ref[...] + mm_nt(da_ref[...], w_ref[:, :half]) + mm_nt(db_ref[...], w_ref[:, half:])


def back_norm_body(d_ref, x_ref, og_ref, gain_ref, o_ref, sum_ref):
    @pl.when(pl.program_id(0) == 0)
    def _():
        sum_ref[...] = jnp.zeros_like(sum_ref)

    d_normed = d_ref[...]
    x = x_ref[...].astype(F32)
    scale = lax.rsqrt(jnp.mean(x * x, axis=-1, keepdims=True) + EPS)
    unit = x * scale
    pulled = d_normed * gain_ref[...]
    inner = jnp.mean(pulled * unit, axis=-1, keepdims=True)
    o_ref[...] = og_ref[...].astype(F32) + scale * (pulled - unit * inner)
    total = jnp.sum(d_normed * unit, axis=0, keepdims=True)
    sum_ref[...] += jnp.broadcast_to(total, sum_ref.shape)


def swap(array, axis):
    return lax.ppermute(array, axis, [(0, 1), (1, 0)])


def from_behind(array, by):
    peers = lax.axis_size(CTX[0]) * lax.axis_size(CTX[1])
    pairs = [(i, i + by) for i in range(peers) if 0 <= i + by < peers]
    return lax.ppermute(array, CTX, pairs)


def entering(state, decay, reverse, fills):
    fills = list(fills)

    def meanwhile(sent, arrived):
        return tie(arrived, *fills.pop(0)(sent)) if fills else arrived

    depth, width = lax.axis_size("z"), lax.axis_size("y")
    place_z, place_y = lax.axis_index("z"), lax.axis_index("y")
    if width != 2:
        gathered = lax.all_gather(jnp.concatenate([state, decay], axis=1), CTX)
        while fills:
            gathered = meanwhile(state, gathered)
        count = depth * width
        place = place_z * width + place_y
        ahead = count - 1 - place if reverse else place

        def one(lap, running):
            source = count - 1 - lap if reverse else lap
            item = lax.dynamic_index_in_dim(gathered, source, 0, False)
            return item[:, STATE : STATE + 1] * running + item[:, :STATE]

        return lax.fori_loop(0, ahead, one, jnp.zeros_like(state))
    second = place_y == (0 if reverse else 1)
    sent = pick(state, 1 - place_y)
    got = meanwhile(sent, swap(sent, "y"))
    own = pick(state, place_y)
    decay_own = pick(decay, place_y)[:1]
    decay_got = swap(pick(decay, 1 - place_y), "y")[:1]
    early = jnp.where(second, got, own)
    late = jnp.where(second, own, got)
    decay_early = jnp.where(second, decay_got, decay_own)
    decay_late = jnp.where(second, decay_own, decay_got)
    total = decay_late * early + late
    decay_total = decay_early * decay_late
    before = jnp.zeros_like(total)
    sent = total
    turn = depth - 1 - place_z if reverse else place_z
    for hop in range(1, depth):
        pairs = [(depth - hop, depth - 1 - hop)] if reverse else [(hop - 1, hop)]
        arrived = meanwhile(sent, lax.ppermute(sent, "z", pairs))
        before = jnp.where(turn == hop, arrived, before)
        sent = decay_total * before + total
    middle = decay_early * before + early
    mine = jnp.where(second, middle, before)
    sent = jnp.where(second, before, middle)
    theirs = swap(sent, "y")
    while fills:
        theirs = meanwhile(sent, theirs)
    return in_order(mine, theirs, "y")


def pick(parts, index, dim=0):
    return lax.dynamic_index_in_dim(parts, index, dim, False)


def in_order(mine, theirs, axis):
    first = lax.axis_index(axis) == 0
    return jnp.where(first, jnp.stack([mine, theirs]), jnp.stack([theirs, mine]))


def across(array, axis, by):
    return lax.ppermute(array, axis, [(i, i ^ by) for i in range(lax.axis_size(axis))])


def products_body(
    patched, place_ref, sent_own, kept_own, sent_other, kept_other, own_ref, other_ref, *refs
):
    sent_ref, kept_ref = refs[-2:]
    own, other = own_ref[...], other_ref[...]
    if patched:
        upto = own.shape[0] - LEAD
        own = jnp.concatenate([own[:upto], refs[0][...]], axis=0)
        other = jnp.concatenate([other[:upto], refs[1][...]], axis=0)

    def product(first, second):
        first, second = first[...], second[...]
        first = first.reshape(-1, first.shape[-1])
        second = second.reshape(-1, second.shape[-1])
        return mm(first, own) + mm(second, other)

    sent_ref[...] = product(sent_own, sent_other).astype(BF)
    kept_ref[...] = product(kept_own, kept_other)


def products(left, right, start, count, axis, waits):
    own, other = left
    sizes = [lax.axis_size(a) for a in ("x", "z", "y")]
    tokens = own.shape[1]
    rows = other.shape[0] // sizes[0] // sizes[1] // sizes[2]
    out_rows = other.shape[0] // 2
    places = jnp.stack([lax.axis_index(a) for a in ("core", "x", "y")])
    if axis == "x":
        own = own.reshape(2, 2, out_rows, tokens)
        other = other.reshape(2, out_rows, tokens)
        own_block, other_block = (1, 1, out_rows, tokens), (1, out_rows, tokens)

        def spec(mine, flip):
            if mine:
                return pl.BlockSpec(own_block, lambda g, p: (p[1] ^ flip, p[0], 0, 0))
            return pl.BlockSpec(other_block, lambda g, p: (p[1] ^ flip, 0, 0))
    else:
        own = own.reshape(2, 2, sizes[1], 2, rows, tokens)
        other = other.reshape(2 * sizes[1], 2, rows, tokens)
        own_block = (2, 1, sizes[1], 1, rows, tokens)
        other_block = (2 * sizes[1], 1, rows, tokens)

        def spec(mine, flip):
            if mine:
                return pl.BlockSpec(own_block, lambda g, p: (0, p[0], 0, p[2] ^ flip, 0, 0))
            return pl.BlockSpec(other_block, lambda g, p: (0, p[2] ^ flip, 0, 0))

    block = 384 if count % 384 == 0 else 512
    first = start // block
    columns_of = pl.BlockSpec((tokens, block), lambda g, p: (0, g + first))
    edge_of = pl.BlockSpec((LEAD, block), lambda g, p: (0, g + first))
    result = pl.BlockSpec((out_rows, block), lambda g, p: (0, g))
    return call(
        functools.partial(products_body, len(right) > 2), -(-count // block), count * out_rows / 2.0e5,
        [
            (own, spec(True, 1)), (own, spec(True, 0)), (other, spec(False, 1)), (other, spec(False, 0)),
            (right[0], columns_of), (right[1], columns_of),
            *[(edge, edge_of) for edge in right[2:]],
        ],
        [(out((out_rows, count), BF), result), (out((out_rows, count)), result)],
        waits=waits,
        places=places,
    )


def products_any(left, right, start, count, axis):
    core, place = lax.axis_index("core"), lax.axis_index(axis)
    sizes = [lax.axis_size(a) for a in ("x", "z", "y")]
    own = core_rows(left[0], core).reshape(left[1].shape)
    both = jnp.concatenate([own, left[1]], axis=1)
    view = both.reshape(*sizes, -1, both.shape[1])
    if axis == "y":
        view = jnp.moveaxis(view, 2, 0)
    view = view.reshape(view.shape[0], -1, both.shape[1])
    if len(right) > 2:
        upto = right[0].shape[0] - LEAD
        right = [right[0][:upto], right[2], right[1][:upto], right[3]]
    right = jnp.concatenate(right, axis=0)[:, start : start + count]
    sent = [mm(pick(view, place ^ by), right).astype(BF) for by in range(1, view.shape[0])]
    return sent, mm(pick(view, place), right)


def total_of(kept, got):
    for piece in got:
        kept = kept + piece.astype(F32)
    return kept


def tied(value, others):
    return tie(value, *others) if others else value


def xor_parts(parts, axis):
    count, place = lax.axis_size(axis), lax.axis_index(axis)
    return pick(parts, place), [pick(parts, place ^ by).astype(BF) for by in range(1, count)]


def travel(sent, axis, others):
    return [across(tied(piece, others), axis, by + 1) for by, piece in enumerate(sent)]


class Reduction:
    def __init__(self, left, right, start, middle, end, waits=()):
        if lax.axis_size("x") == 2 and lax.axis_size("y") == 2:
            sent_x, self.kept_x = products(left, right, start, middle - start, "x", waits)
            sent_y, self.kept_y = products(left, right, middle, end - middle, "y", waits)
            self.sent_x, self.sent_y = [sent_x], [sent_y]
        else:
            self.sent_x, self.kept_x = products_any(left, right, start, middle - start, "x")
            self.sent_y, self.kept_y = products_any(left, right, middle, end - middle, "y")

    def made(self):
        return [self.kept_x, self.kept_y, *self.sent_x, *self.sent_y]

    def launch(self, *others):
        self.got_x = travel(self.sent_x, "x", others)
        self.got_y = travel(self.sent_y, "y", others)

    def second(self, *others):
        sizes = [lax.axis_size(a) for a in ("x", "z", "y")]
        part_x = total_of(tied(self.kept_x, others), self.got_x)
        part_y = total_of(tied(self.kept_y, others), self.got_y)
        view_x = part_x.reshape(sizes[1], sizes[2], -1, part_x.shape[1])
        view_y = part_y.reshape(sizes[0], sizes[1], -1, part_y.shape[1])
        self.own_x, self.next_x = xor_parts(jnp.moveaxis(view_x, 1, 0), "y")
        self.own_y, self.next_y = xor_parts(view_y, "x")
        self.came_x = travel(self.next_x, "y", ())
        self.came_y = travel(self.next_y, "x", ())

    def third(self, *others, kind=F32):
        done_x = total_of(tied(self.own_x, others), self.came_x)
        done_y = total_of(tied(self.own_y, others), self.came_y)
        self.parts = jnp.concatenate([done_x, done_y], axis=2)
        place = lax.axis_index("z")
        self.mine = pick(self.parts, place) if kind == BF else None
        self.got_z = lax.all_to_all(self.parts.astype(kind), "z", 0, 0, tiled=True)

    def last(self, *others):
        got = tied(self.got_z, others)
        if self.mine is None:
            return jnp.sum(got, axis=0)
        others_only = lax.broadcasted_iota(jnp.int32, got.shape, 0) != lax.axis_index("z")
        return self.mine + jnp.sum(jnp.where(others_only, got.astype(F32), 0.0), axis=0)


def core_rows(turned, core):
    view = turned.reshape(lax.axis_size("x"), 2, -1, turned.shape[1])
    return pick(view, core, 1)


def both_cores(turned, core):
    theirs = core_rows(turned, 1 - core)
    return turned, swap(theirs.reshape(-1, turned.shape[1]), "core")


def document_ids(lengths, positions):
    first_end = lengths[0]
    second_end = lengths[0] + lengths[1]
    inside = (positions >= first_end).astype(jnp.int32) + (positions >= second_end).astype(jnp.int32)
    return jnp.where(positions < 0, -1, inside)


def gather_small(pieces, count):
    flat = jnp.concatenate([piece.reshape(-1) for piece in pieces])
    spread = jnp.broadcast_to(flat[None], (count, flat.shape[0]))
    return lax.all_to_all(spread, EVERY, 0, 0, tiled=True)


def columns(array, width):
    return jnp.pad(array, ((0, 0), (0, width - array.shape[1])))


def shards(
    tokens, out_grad, seq_lengths, norm_gain, in_weight, conv_weight, conv_bias,
    dt_bias, a_log, skip_gain, gated_gain, out_weight,
):
    count = 1
    for axis in EVERY:
        count *= lax.axis_size(axis)
    core = lax.axis_index("core")
    place = lax.axis_index("z") * lax.axis_size("y") + lax.axis_index("y")
    row_count, width = tokens.shape
    first_row = place * row_count
    full_rows = LEAD + row_count
    half = INNER // 2
    bc_width = CONVW - INNER
    square = (row_count, row_count)

    lead_tokens = from_behind(tokens[row_count - LEAD :], 1)
    small = gather_small([norm_gain, conv_weight, conv_bias, gated_gain], count)
    weight_x = lax.all_gather(columns(in_weight[:, INNER:], PROJ_X), EVERY, axis=0, tiled=True)
    rows_out = out_weight.shape[0] // 2
    stacked = jnp.stack(
        [in_weight[:, :half], in_weight[:, half:INNER], out_weight[:rows_out], out_weight[rows_out:]]
    )
    stacked = lax.all_gather(stacked, EVERY, axis=1, tiled=True)
    cuts = [norm_gain.size, conv_weight.size, conv_bias.size]
    cuts = [sum(cuts[: i + 1]) for i in range(3)]
    gain_piece, conv_piece, bias_piece, gated_piece = jnp.split(small, cuts, axis=1)
    full_gain = gain_piece.reshape(1, -1).astype(F32)
    full_conv = jnp.moveaxis(conv_piece.reshape(count, CONV_K, -1), 1, 0).reshape(CONV_K, -1)
    full_conv = jnp.pad(full_conv.astype(F32), ((0, 4), (0, 0)))
    full_bias = bias_piece.reshape(1, -1).astype(F32)
    full_gated = gated_piece.reshape(1, -1).astype(F32)

    normed_ext, turned = call(
        norm_body, 1, 4,
        [
            (lead_tokens, whole(LEAD, width)),
            (tokens, whole(row_count, width)),
            (full_gain, whole(1, width)),
        ],
        [
            (out((full_rows, width), BF), whole(full_rows, width)),
            (out((width, row_count), BF), whole(width, row_count)),
        ],
    )
    normed = normed_ext[LEAD:]
    normed_left = both_cores(turned, core)
    out_grad_theirs = swap(out_grad, "core")

    lengths = seq_lengths[0]
    ordinal = jnp.arange(row_count, dtype=jnp.int32)
    doc_ids = document_ids(lengths, first_row + ordinal)
    doc_before = document_ids(lengths, first_row - 1 + jnp.zeros((1,), jnp.int32))
    marks = [
        document_ids(lengths, first_row + ordinal - (CONV_K - 1 - tap)) == doc_ids
        for tap in range(CONV_K)
    ]
    marks = marks + [doc_ids, doc_ids == doc_before[0], doc_ids == doc_ids[row_count - 1]]
    masks = columns(jnp.stack([mark.astype(F32) for mark in marks], axis=1), 128)
    doc_rows = jnp.broadcast_to(doc_ids.astype(F32)[None], (8, row_count))
    rate = columns(jnp.exp(a_log)[None], 128)
    shift = columns(dt_bias[None], 128)
    skip_wide = jnp.repeat(skip_gain, HEAD_DIM)[None]
    mixed_x = mm(normed_ext, weight_x).astype(BF)

    block_bc = pl.BlockSpec((full_rows, bc_width), lambda g: (0, INNER // bc_width))
    block_dr = pl.BlockSpec((full_rows, 128), lambda g: (0, CONVW // 128))
    per_token = whole(row_count, 128)
    a_token = (out((row_count, 128)), per_token)
    pre_bc, act_bc, act_t, scores, scores_t, steps, enter, to_end, cumulative, cum_turned, shifted = call(
        prep_bc_body, 1, 6,
        [
            (mixed_x, block_bc),
            (mixed_x, block_dr),
            (full_conv[:, INNER:], whole(8, bc_width)),
            (full_bias[:, INNER:], whole(1, bc_width)),
            (masks, per_token),
            (doc_rows, whole(8, row_count)),
            (shift, whole(1, 128)),
            (rate, whole(1, 128)),
        ],
        [
            (out((row_count, bc_width)), whole(row_count, bc_width)),
            (out((row_count, bc_width)), whole(row_count, bc_width)),
            (out((bc_width, row_count)), whole(bc_width, row_count)),
            (out(square), whole(*square)),
            (out(square), whole(*square)),
            a_token, a_token, a_token, a_token,
            (out((128, row_count)), whole(128, row_count)),
            a_token,
        ],
    )
    pre_x, act_x, state_local, device_decay = call(
        prep_x_body, INNER // BLOCK, 12,
        [
            (mixed_x, lanes(full_rows, BLOCK)),
            (full_conv[:, :INNER], lanes(8, BLOCK)),
            (full_bias[:, :INNER], lanes(1, BLOCK)),
            (masks, per_token),
            (to_end, per_token),
            (steps, per_token),
            (enter, per_token),
            (act_t, whole(bc_width, row_count)),
        ],
        [
            (out((row_count, INNER)), lanes(row_count, BLOCK)),
            (out((row_count, INNER)), lanes(row_count, BLOCK)),
            (out((2, STATE, half)), halves(STATE, BLOCK)),
            (out((2, 8, half)), halves(8, BLOCK)),
        ],
    )

    heads_block = 2 * PAIRS
    groups = HEADS // heads_block
    half_groups = groups // 2
    cum_rows = cum_turned[:HEADS].reshape(groups, heads_block, row_count)
    kept = {}

    def pairs_at(index):
        return pl.BlockSpec((row_count, PAIR_LANES), lambda g: (0, g + index * half_groups))

    def cums_at(index):
        return pl.BlockSpec((1, heads_block, row_count), lambda g: (g + index * half_groups, 0, 0))

    def intra(index, wait):
        kept[index] = call(
            functools.partial(intra_body, index * half_groups), half_groups, 12,
            [
                (act_x, pairs_at(index)),
                (steps, per_token),
                (skip_wide, pl.BlockSpec((1, PAIR_LANES), lambda g: (0, g + index * half_groups))),
                (scores, whole(*square)),
                (cumulative, per_token),
                (cum_rows, cums_at(index)),
            ],
            [(out((row_count, half)), lanes(row_count, PAIR_LANES))],
            waits=[wait],
        )[0]
        return [kept[index]]

    devices = 4
    out_block = 2 * devices * rows_out
    out_blocks = count // devices
    weight_block = pl.BlockSpec((2, devices * rows_out, width), lambda g: (1, g, 0))
    direct = rows_out % 16 == 0

    def project(wait):
        if direct:
            kept["d_final"] = call(
                functools.partial(d_final_body, devices, rows_out), out_blocks, 7,
                [(out_grad, whole(row_count, width)), (stacked, weight_block)],
                [(out((row_count, INNER)), lanes(row_count, out_block))],
                waits=[wait],
            )[0]
        else:
            weight_o = jnp.moveaxis(stacked[2:].reshape(2, count, rows_out, width), 0, 1)
            kept["weight_o"] = weight_o.reshape(-1, width)
            kept["d_final"] = mm_nt(out_grad, kept["weight_o"])
        kept["mixed_z"] = [mm(normed, stacked[side]).astype(BF) for side in range(2)]
        return [kept["d_final"], *kept["mixed_z"]]

    state_in = entering(
        state_local, device_decay, False,
        [
            lambda wait: intra(0, wait), lambda wait: intra(1, wait), lambda wait: [], lambda wait: [],
            project,
        ],
    )
    state_end = device_decay[:, :1] * state_in + state_local

    tile = 128
    final, final_turned, d_z, d_y, returned_local, d_c_carry, dy_y, sums = call(
        gate_body, row_count // tile, 31,
        [
            (kept[0], rows_of(tile, half)),
            (kept[1], rows_of(tile, half)),
            (kept["mixed_z"][0], rows_of(tile, half)),
            (kept["mixed_z"][1], rows_of(tile, half)),
            (kept["d_final"], rows_of(tile, INNER)),
            (act_x, rows_of(tile, INNER)),
            (act_bc[:, STATE:], rows_of(tile, STATE)),
            (act_t[STATE:], lanes(STATE, tile)),
            (state_in, whole(2, STATE, half)),
            (enter, rows_of(tile, 128)),
            (full_gated, whole(1, INNER)),
            (skip_wide, whole(1, INNER)),
        ],
        [
            (out((row_count, INNER), BF), rows_of(tile, INNER)),
            (out((INNER, row_count), BF), lanes(INNER, tile)),
            (out((row_count, INNER), BF), rows_of(tile, INNER)),
            (out((row_count, INNER)), rows_of(tile, INNER)),
            (out((2, STATE, half)), whole(2, STATE, half)),
            (out((row_count, STATE)), rows_of(tile, STATE)),
            (out((row_count, 128)), rows_of(tile, 128)),
            (out((16, INNER)), whole(16, INNER)),
        ],
        [pltpu.VMEM((tile, INNER), F32), pltpu.VMEM((tile, INNER), F32)],
    )

    final_left = both_cores(final_turned, core)
    d_z_theirs = swap(d_z, "core")
    back = {"acc": jnp.zeros(square, F32)}

    def out_sums(wait):
        back["out"] = Reduction(final_left, [out_grad, out_grad_theirs], 0, width // 2, width, [wait])
        back["out"].launch()
        return back["out"].made()

    def z_sums(wait):
        back["z"] = Reduction(normed_left, [d_z, d_z_theirs], 0, half, INNER, [wait])
        back["z"].launch()
        return back["z"].made()

    def within(index, wait):
        ends = [(out((row_count, bc_width)), whole(row_count, bc_width))] if index else []
        back[index], back["acc"], *back["bc"] = call(
            functools.partial(back_body, index * half_groups), half_groups, 18,
            [
                (act_x, pairs_at(index)),
                (d_y, pairs_at(index)),
                (steps, per_token),
                (scores_t, whole(*square)),
                (cumulative, per_token),
                (cum_rows, cums_at(index)),
                (act_bc, whole(row_count, bc_width)),
                (doc_rows, whole(8, row_count)),
                (masks, per_token),
                (back["acc"], whole(*square)),
            ],
            [
                (out((row_count, half)), lanes(row_count, PAIR_LANES)),
                (out(square), whole(*square)),
                *ends,
            ],
            waits=[wait],
        )
        return [back[index]]

    def first_within(wait):
        back["out"].second(wait)
        return within(0, wait)

    def second_within(wait):
        return within(1, wait)

    norm_block = 256

    def send_out(wait):
        back["z"].second(wait)
        back["out"].third(wait)
        return [back["out"].parts, *back["z"].next_x, *back["z"].next_y]

    returned = entering(
        returned_local, device_decay, True,
        [out_sums, z_sums, first_within, second_within, send_out],
    )

    blocks = half // BLOCK

    def carried(index, earlier, extra, extra_out, waits):
        steps_count = blocks + len(extra_out)
        own = pl.BlockSpec((row_count, BLOCK), lambda g: (0, jnp.minimum(g, blocks - 1)))

        def at(rows):
            return pl.BlockSpec((rows, BLOCK), lambda g: (0, jnp.minimum(g, blocks - 1) + index * blocks))

        state_at = pl.BlockSpec((1, STATE, BLOCK), lambda g: (index, 0, jnp.minimum(g, blocks - 1)))
        wide = half + len(extra_out) * (PROJ_X - INNER)
        return call(
            functools.partial(carry_body, index * blocks), steps_count, 14 + 4 * index,
            [
                (back[index], own),
                (act_x, at(row_count)),
                (d_y, at(row_count)),
                (pre_x, at(row_count)),
                (mixed_x, at(full_rows)),
                (full_conv[:, :INNER], at(8)),
                (masks, per_token),
                (act_bc, whole(row_count, bc_width)),
                (returned, state_at),
                (state_end, state_at),
                (to_end, per_token),
                (steps, per_token),
                (skip_wide, at(1)),
                *[(array, whole(*array.shape)) for array in earlier],
                *extra,
            ],
            [
                *extra_out,
                (out((row_count, wide), BF), lanes(row_count, BLOCK)),
                (out((2 * LEAD, wide)), lanes(2 * LEAD, BLOCK)),
                (out((8, wide)), lanes(8, BLOCK)),
                (out((row_count, STATE)), whole(row_count, STATE)),
                a_token,
                (out((8, 128)), whole(8, 128)),
            ],
            waits=waits,
        )

    none = jnp.zeros((row_count, 128), F32)
    d_xa, edge_a, conv_a, *so_far = carried(0, [none, none, none[:8]], [], [], [])
    back["z"].third(edge_a)
    d_xa_theirs = swap(d_xa, "core")
    halo_a = from_behind(edge_a[:LEAD], -1)
    last_a = (edge_a[LEAD:] + halo_a).astype(BF)
    last_a_theirs = swap(last_a, "core")
    sums_a = Reduction(normed_left, [d_xa, d_xa_theirs, last_a, last_a_theirs], 0, half // 2, half, [back["z"].parts, back["out"].got_z])
    sums_a.launch()
    heads, d_xb, edge_b, conv_b, *_ = carried(
        1, so_far,
        [
            (pre_bc, whole(row_count, bc_width)),
            (mixed_x, block_bc),
            (full_conv[:, INNER:], whole(8, bc_width)),
            (back["bc"][0], whole(row_count, bc_width)),
            (d_c_carry, whole(row_count, STATE)),
            (shifted, per_token),
            (rate, whole(1, 128)),
            (dy_y, per_token),
        ],
        [(out((16, 128)), whole(16, 128))],
        sums_a.made(),
    )
    d_xb_theirs = swap(d_xb, "core")
    halo_b = from_behind(edge_b[:LEAD], -1)
    sums_a.second(edge_b)
    sums_a.third()
    d_normed_z = call(
        back_z_body, width // norm_block, 10,
        [
            (d_z, whole(row_count, INNER)),
            (stacked, pl.BlockSpec((2, norm_block, half), lambda g: (0, g, 0))),
        ],
        [(out((row_count, width)), lanes(row_count, norm_block))],
        waits=[edge_b],
    )[0]
    last_b = (edge_b[LEAD:] + tie(halo_b, d_normed_z)).astype(BF)
    last_b_theirs = swap(last_b, "core")
    wide_b = d_xb.shape[1]
    sums_b = Reduction(
        normed_left, [d_xb, d_xb_theirs, last_b, last_b_theirs], 0, 1024, wide_b, [sums_a.parts]
    )
    sums_b.launch()

    d_xa = lax.dynamic_update_slice(d_xa, last_a, (row_count - LEAD, 0))
    d_xb = lax.dynamic_update_slice(d_xb, last_b, (row_count - LEAD, 0))
    d_normed = call(
        back_x_body, width // norm_block, 10,
        [
            (d_xa, whole(row_count, half)),
            (d_xb, whole(row_count, wide_b)),
            (weight_x, rows_of(norm_block, PROJ_X)),
            (d_normed_z, lanes(row_count, norm_block)),
        ],
        [(out((row_count, width)), lanes(row_count, norm_block))],
        waits=sums_b.made(),
    )[0]
    grad_tokens, gain_sums = call(
        back_norm_body, row_count // tile, 4,
        [
            (d_normed, rows_of(tile, width)),
            (tokens, rows_of(tile, width)),
            (out_grad, rows_of(tile, width)),
            (full_gain, whole(1, width)),
        ],
        [
            (out((row_count, width)), rows_of(tile, width)),
            (out((8, width)), whole(8, width)),
        ],
    )
    sums_b.second(grad_tokens)
    if direct:
        layer_out = call(
            functools.partial(layer_body, devices, rows_out), out_blocks, 13,
            [
                (final, lanes(row_count, out_block)),
                (stacked, weight_block),
                (tokens, whole(row_count, width)),
            ],
            [(out((row_count, width), BF), whole(row_count, width))],
            [pltpu.VMEM((row_count, width), F32)],
            waits=[*sums_b.next_x, *sums_b.next_y],
        )[0]
    else:
        layer_out = (tokens.astype(F32) + mm(final, kept["weight_o"])).astype(BF)

    conv_sums = jnp.concatenate([conv_a, conv_b[:, : CONVW - half]], axis=1)
    grad_skip = jnp.sum(jnp.sum(sums[8:], axis=0).reshape(HEADS, HEAD_DIM), axis=1)
    grad_gated = jnp.sum(sums[:8], axis=0)
    per_device = jnp.concatenate(
        [
            gain_sums[0].reshape(count, -1),
            jnp.moveaxis(conv_sums[:CONV_K].reshape(CONV_K, count, -1), 1, 0).reshape(count, -1),
            conv_sums[CONV_K].reshape(count, -1),
            grad_gated.reshape(count, -1),
            jnp.broadcast_to(
                jnp.concatenate([heads[0, :HEADS], heads[8, :HEADS], grad_skip])[None],
                (count, 3 * HEADS),
            ),
        ],
        axis=1,
    )
    sums_b.third(kind=BF)
    per_device = tie(per_device, *sums_b.next_x, *sums_b.next_y)
    arrived = lax.all_to_all(per_device, EVERY, 0, 0, tiled=True)
    done = [layer_out]
    sum_out, sum_in_z, sum_in_a = [each.last(*done) for each in (back["out"], back["z"], sums_a)]
    sum_in_b = sums_b.last()
    small_sums = jnp.sum(tie(arrived, layer_out), axis=0)
    cuts = [norm_gain.size, conv_weight.size, conv_bias.size, gated_gain.size, HEADS, HEADS]
    cuts = [sum(cuts[: i + 1]) for i in range(6)]
    sum_gain, sum_conv, sum_bias, sum_gated, sum_dt, sum_log, sum_skip = jnp.split(small_sums, cuts)
    sum_in = jnp.concatenate([sum_in_z, sum_in_a, sum_in_b[:, : in_weight.shape[1] - INNER - half]], axis=1)
    return (
        layer_out,
        grad_tokens,
        sum_gain,
        sum_in,
        sum_conv.reshape(conv_weight.shape),
        sum_bias,
        sum_dt,
        sum_log,
        sum_skip,
        sum_gated,
        sum_out,
    )


def solution(mesh):
    x = mesh.shape["dp"] // 2
    y = x
    z = mesh.shape["ctx"] // y
    fine = Mesh(mesh.devices.reshape(x, 2, z, y), EVERY)
    rows = P(EVERY, None)
    flat = P(EVERY)
    in_specs = (
        rows, rows, P(("x", "core"), None), flat, rows, P(None, EVERY), flat,
        P(), P(), P(), flat, rows,
    )
    out_specs = (rows, rows, flat, rows, P(None, EVERY), flat, P(), P(), P(), flat, rows)
    return jax.shard_map(shards, mesh=fine, in_specs=in_specs, out_specs=out_specs, check_vma=False)
```

```python
import functools

import jax
import jax.numpy as jnp
from jax import lax
from jax.experimental import pallas as pl
from jax.experimental.pallas import tpu as pltpu
from jax.sharding import Mesh, PartitionSpec as P

HEADS = 48
HEAD_DIM = 64
STATE = 128
CONV_K = 4
INNER = 3072
CONVW = 3328
LEAD = 16
PROJ_X = 3456
BLOCK = 512
BLOCK_HEADS = BLOCK // HEAD_DIM
PAIRS = 2
PAIR_LANES = 128 * PAIRS
VMEM = 56 * 1024 * 1024
F32 = jnp.float32
BF = jnp.bfloat16
EPS = 1e-05
highest = lax.Precision.HIGHEST
EVERY = ("x", "core", "z", "y")
CTX = ("z", "y")


def params():
    return pltpu.CompilerParams(vmem_limit_bytes=VMEM, dimension_semantics=("arbitrary",))


def call(body, grid, micros, ins, outs, scratch=(), waits=(), places=None):
    first = (places is not None) + len(ins)
    anywhere = pl.BlockSpec(memory_space=pl.ANY)

    def run(*refs):
        body(*refs[:first], *refs[first + len(waits) :])

    scalars = [] if places is None else [places]
    return pl.pallas_call(
        run,
        grid_spec=pltpu.PrefetchScalarGridSpec(
            num_scalar_prefetch=len(scalars),
            grid=(grid,),
            in_specs=[spec for _, spec in ins] + [anywhere] * len(waits),
            out_specs=[spec for _, spec in outs],
            scratch_shapes=list(scratch),
        ),
        out_shape=[shape for shape, _ in outs],
        compiler_params=params(),
        cost_estimate=pl.CostEstimate(
            flops=int(micros * 1e9), bytes_accessed=int(micros * 3e6), transcendentals=0
        ),
    )(*scalars, *[array for array, _ in ins], *waits)


def tie(value, *others):
    def body(*refs):
        pass

    anywhere = pl.BlockSpec(memory_space=pl.ANY)
    return pl.pallas_call(
        body,
        in_specs=[anywhere] * (1 + len(others)),
        out_specs=anywhere,
        out_shape=jax.ShapeDtypeStruct(value.shape, value.dtype),
        input_output_aliases={0: 0},
    )(value, *others)


def whole(*shape):
    return pl.BlockSpec(shape, lambda g: (0,) * len(shape))


def lanes(rows, width):
    return pl.BlockSpec((rows, width), lambda g: (0, g))


def rows_of(count, width):
    return pl.BlockSpec((count, width), lambda g: (g, 0))


def halves(rows, width):
    count = INNER // 2 // width
    return pl.BlockSpec((1, rows, width), lambda g: (g // count, 0, g % count))


def group(rows, width):
    return pl.BlockSpec((1, rows, width), lambda g: (g, 0, 0))


def out(shape, dtype=F32):
    return jax.ShapeDtypeStruct(shape, dtype)


def split(value):
    high = value.astype(BF)
    return high, (value - high.astype(F32)).astype(BF)


def mm(left, right):
    return jnp.dot(left, right, preferred_element_type=F32)


def mm_nt(left, right):
    return lax.dot_general(left, right, (((1,), (1,)), ((), ())), preferred_element_type=F32)


def mm_tn(left, right):
    return lax.dot_general(left, right, (((0,), (0,)), ((), ())), preferred_element_type=F32)


def three(product, left, right):
    left_high, left_low = left
    right_high, right_low = right
    return (
        product(left_high, right_high)
        + product(left_high, right_low)
        + product(left_low, right_high)
    )


def head_of_lane(first, count):
    lane = lax.broadcasted_iota(jnp.int32, (STATE, count), 1) // HEAD_DIM + first
    row = lax.broadcasted_iota(jnp.int32, (STATE, count), 0)
    return (lane == row).astype(BF)


def expand(value, places):
    high, low = split(value)
    return mm(high, places) + mm(low, places)


def fold(value, places):
    high, low = split(value)
    return mm_nt(high, places) + mm_nt(low, places)


def sigmoid(value):
    return 1.0 / (1.0 + jnp.exp(-value))


def conv_pre(extended, weight, bias, masks):
    running = jnp.zeros((masks.shape[0], extended.shape[1]), F32) + bias
    for tap in range(CONV_K):
        shifted = extended if tap == CONV_K - 1 else pltpu.roll(extended, CONV_K - 1 - tap, 0)
        running = running + shifted[LEAD:] * weight[tap : tap + 1] * masks[:, tap : tap + 1]
    return running


def conv_back(d_pre, extended, weight, masks):
    zeros = jnp.zeros((LEAD, d_pre.shape[1]), F32)
    total = LEAD + d_pre.shape[0]
    d_ext = jnp.zeros((total, d_pre.shape[1]), F32)
    weight_rows = []
    for tap in range(CONV_K):
        by = CONV_K - 1 - tap
        part = d_pre * masks[:, tap : tap + 1]
        padded = jnp.concatenate([zeros, part], axis=0)
        shifted = extended
        if by:
            padded = pltpu.roll(padded, total - by, 0)
            shifted = pltpu.roll(extended, by, 0)
        d_ext = d_ext + padded * weight[tap : tap + 1]
        weight_rows.append(jnp.sum(shifted[LEAD:] * part, axis=0, keepdims=True))
    weight_rows.append(jnp.sum(d_pre, axis=0, keepdims=True))
    weight_rows.append(jnp.zeros((8 - len(weight_rows), d_pre.shape[1]), F32))
    return d_ext, jnp.concatenate(weight_rows, axis=0)


def same_mask(doc_row, doc_col, transposed):
    count = doc_row.shape[1]
    rows = lax.broadcasted_iota(jnp.int32, (count, count), 0)
    cols = lax.broadcasted_iota(jnp.int32, (count, count), 1)
    order = rows <= cols if transposed else rows >= cols
    return jnp.where((doc_row == doc_col) & order, 1.0, 0.0)


def norm_body(lead_ref, x_ref, gain_ref, normed_ref, turned_ref):
    def normed(value):
        scale = lax.rsqrt(jnp.mean(value * value, axis=-1, keepdims=True) + EPS)
        return value * scale * gain_ref[...]

    normed_ref[:LEAD] = normed(lead_ref[...].astype(F32)).astype(BF)
    for tile in range(x_ref.shape[0] // 128):
        here = slice(tile * 128, tile * 128 + 128)
        value = normed(x_ref[here].astype(F32))
        normed_ref[LEAD + tile * 128 : LEAD + tile * 128 + 128] = value.astype(BF)
        turned_ref[:, here] = value.T.astype(BF)


def parts_of(value):
    high, low = split(value)
    return high, low, (value - high.astype(F32) - low.astype(F32)).astype(BF)


def running_sum(value, transposed):
    count = value.shape[0]
    rows = lax.broadcasted_iota(jnp.int32, (count, count), 0)
    cols = lax.broadcasted_iota(jnp.int32, (count, count), 1)
    side = ((rows <= cols) if transposed else (rows >= cols)).astype(BF)
    high, middle, low = parts_of(value)
    return mm(side, high) + mm(side, middle) + mm(side, low)


def softplus(value):
    return jnp.maximum(value, 0.0) + jnp.log1p(jnp.exp(-jnp.abs(value)))


def prep_bc_body(
    x_ref, dr_ref, w_ref, b_ref, m_ref, doc_ref, shift_ref, rate_ref,
    pre_ref, act_ref, t_ref, s_ref, st_ref, steps_ref, enter_ref, to_end_ref, cum_ref, turned_ref, dt_ref,
):
    masks = m_ref[...]
    pre = conv_pre(x_ref[...].astype(F32), w_ref[...], b_ref[...], masks)
    act = pre * sigmoid(pre)
    pre_ref[...] = pre
    act_ref[...] = act
    t_ref[...] = act.T
    b_rows, c_rows = split(act[:, :STATE]), split(act[:, STATE:])
    doc_row, doc_col = doc_ref[0:1], masks[:, CONV_K : CONV_K + 1]
    s_ref[...] = three(mm_nt, c_rows, b_rows) * same_mask(doc_row, doc_col, False)
    st_ref[...] = three(mm_nt, b_rows, c_rows) * same_mask(doc_row, doc_col, True)
    shifted = dr_ref[LEAD:, :].astype(F32) + shift_ref[...]
    steps = softplus(shifted)
    cumulative = running_sum(-steps * rate_ref[...], False)
    last = cumulative[cumulative.shape[0] - 1 :]
    dt_ref[...] = shifted
    steps_ref[...] = steps
    enter_ref[...] = jnp.exp(cumulative) * masks[:, CONV_K + 1 : CONV_K + 2]
    to_end_ref[...] = jnp.exp(last - cumulative) * masks[:, CONV_K + 2 : CONV_K + 3]
    cum_ref[...] = cumulative
    turned_ref[...] = cumulative.T


def prep_x_body(
    x_ref, w_ref, b_ref, m_ref, wl_ref, dt_ref, e_ref, t_ref, pre_ref, act_ref, state_ref, decay_ref
):
    pre = conv_pre(x_ref[...].astype(F32), w_ref[...], b_ref[...], m_ref[...])
    act = pre * sigmoid(pre)
    pre_ref[...] = pre
    act_ref[...] = act
    places = head_of_lane(pl.program_id(0) * BLOCK_HEADS, BLOCK)
    weighted = split(act * expand(wl_ref[...] * dt_ref[...], places))
    state_ref[0] = three(mm, split(t_ref[:STATE]), weighted)
    last = e_ref[e_ref.shape[0] - 8 :]
    high, middle, low = parts_of(last)
    spread = mm(high, places) + mm(middle, places) + mm(low, places)
    decay_ref[0] = jnp.broadcast_to(spread[7:8], spread.shape)


def heads_here(cum_ref, first):
    back = STATE - (pl.program_id(0) + first) * 2 * PAIRS
    return pltpu.roll(cum_ref[...], jnp.where(back == STATE, 0, back), 1)


def intra_body(first, x_ref, dt_ref, skip_ref, s_ref, cum_ref, row_ref, y_ref):
    half = s_ref.shape[0] // 2
    places = head_of_lane((pl.program_id(0) + first) * 2 * PAIRS, PAIR_LANES)
    scaled = x_ref[...] * expand(dt_ref[...], places)
    cols = heads_here(cum_ref, first)
    lane = lax.broadcasted_iota(jnp.int32, (2 * half, 128), 1)
    for pair in range(PAIRS):
        here = slice(pair * 128, pair * 128 + 128)
        high, low = split(scaled[:, here])
        right = jnp.concatenate([high, low], axis=1)
        both = []
        for side in range(2):
            head = 2 * pair + side
            col = cols[:, head : head + 1]
            row = row_ref[0, head : head + 1, :]
            top = s_ref[:half, :half] * jnp.exp(jnp.minimum(col[:half] - row[:, :half], 0.0))
            low_part = s_ref[half:, :] * jnp.exp(jnp.minimum(col[half:] - row, 0.0))
            done = []
            for part, count in ((top, half), (low_part, 2 * half)):
                p_high, p_low = split(part)
                first = mm(p_high, right[:count])
                done.append(first[:, :128] + first[:, 128:] + mm(p_low, high[:count]))
            both.append(jnp.concatenate(done, axis=0))
        y_ref[:, here] = (
            jnp.where(lane < HEAD_DIM, both[0], both[1]) + skip_ref[:, here] * x_ref[:, here]
        )


def gate_body(
    ya_ref, yb_ref, za_ref, zb_ref, df_ref, x_ref, c_ref, ct_ref, state_ref, e_ref, gain_ref, skip_ref,
    final_ref, turned_ref, dz_ref, dy_ref, r_ref, dc_ref, q_ref, sums_ref, carry, scaled,
):
    @pl.when(pl.program_id(0) == 0)
    def _():
        r_ref[...] = jnp.zeros_like(r_ref)
        sums_ref[...] = jnp.zeros_like(sums_ref)

    e_high, e_low = split(e_ref[...])
    c_rows = split(c_ref[...])
    for block in range(INNER // BLOCK):
        here = slice(block * BLOCK, block * BLOCK + BLOCK)
        places = head_of_lane(block * BLOCK_HEADS, BLOCK)
        spread = mm(e_high, places) + mm(e_low, places)
        there = slice(block % 3 * BLOCK, block % 3 * BLOCK + BLOCK)
        carry[:, here] = three(mm, c_rows, split(state_ref[block // 3, :, there])) * spread
        scaled[:, here] = spread
    gain, skip = gain_ref[...], skip_ref[...]

    def some(lap, sums):
        at = pl.ds(pl.multiple_of(lap * 16, 16), 16)
        y = jnp.concatenate([ya_ref[at, :], yb_ref[at, :]], axis=1) + carry[at, :]
        z = jnp.concatenate([za_ref[at, :], zb_ref[at, :]], axis=1).astype(F32)
        sig = sigmoid(z)
        gate = z * sig
        gated = y * gate
        scale = lax.rsqrt(jnp.mean(gated * gated, axis=-1, keepdims=True) + EPS)
        unit = gated * scale
        final_ref[at, :] = (unit * gain).astype(BF)
        d_final = df_ref[at, :]
        q = d_final * gain
        inner = jnp.mean(q * unit, axis=-1, keepdims=True)
        d_gated = scale * (q - unit * inner)
        d_y = d_gated * gate
        dz_ref[at, :] = (d_gated * y * (sig * (1.0 + z * (1.0 - sig)))).astype(BF)
        dy_ref[at, :] = d_y
        x = x_ref[at, :]
        scaled[at, :] = scaled[at, :] * d_y
        carry[at, :] = d_y * (y - skip * x)
        d_gain, d_skip = d_final * unit, d_y * x
        return (
            sums[0] + d_gain[:8] + d_gain[8:],
            sums[1] + d_skip[:8] + d_skip[8:],
        )

    zero = jnp.zeros((8, INNER), F32)
    d_gain, d_skip = lax.fori_loop(0, za_ref.shape[0] // 16, some, (zero, zero))
    sums_ref[0:8] += d_gain
    sums_ref[8:16] += d_skip
    ct_rows = split(ct_ref[...])
    d_c = jnp.zeros(dc_ref.shape, F32)
    q_sum = jnp.zeros(q_ref.shape, F32)
    for block in range(INNER // BLOCK):
        here = slice(block * BLOCK, block * BLOCK + BLOCK)
        there = slice(block % 3 * BLOCK, block % 3 * BLOCK + BLOCK)
        piece = split(scaled[:, here])
        r_ref[block // 3, :, there] += three(mm, ct_rows, piece)
        d_c = d_c + three(mm_nt, piece, split(state_ref[block // 3, :, there]))
        turned_ref[here, :] = final_ref[:, here].T
        q_sum = q_sum + fold(carry[:, here], head_of_lane(block * BLOCK_HEADS, BLOCK))
    dc_ref[...] = d_c
    q_ref[...] = q_sum


def back_body(first, x_ref, dy_ref, dt_ref, st_ref, cum_ref, row_ref, bc_ref, doc_ref, m_ref, in_ref, dx_ref, acc, *ends):
    step = pl.program_id(0)
    half = st_ref.shape[0] // 2

    @pl.when(step == 0)
    def _():
        acc[...] = in_ref[...]

    places = head_of_lane((step + first) * 2 * PAIRS, PAIR_LANES)
    scaled = x_ref[...] * expand(dt_ref[...], places)
    cols = heads_here(cum_ref, first)
    lane = lax.broadcasted_iota(jnp.int32, (2 * half, 128), 1)
    for pair in range(PAIRS):
        here = slice(pair * 128, pair * 128 + 128)
        dy_high, dy_low = split(dy_ref[:, here])
        right = jnp.concatenate([dy_high, dy_low], axis=1)
        twice = jnp.concatenate([dy_high, dy_high], axis=1)
        both = []
        for side in range(2):
            head = 2 * pair + side
            mine = (lane < HEAD_DIM) if side == 0 else (lane >= HEAD_DIM)
            x_high, x_low = split(jnp.where(mine, scaled[:, here], 0.0))
            x_both = jnp.concatenate([x_high, x_low], axis=1)
            col = cols[:, head : head + 1]
            row = row_ref[0, head : head + 1, :]
            done = []
            for at, over in ((slice(0, half), slice(0, 2 * half)), (slice(half, 2 * half), slice(half, 2 * half))):
                decay = jnp.exp(jnp.minimum(row[:, over] - col[at], 0.0))
                p_high, p_low = split(st_ref[at, over] * decay)
                first = mm(p_high, right[over])
                done.append(first[:, :128] + first[:, 128:] + mm(p_low, dy_high[over]))
                outer = mm_nt(x_both[at], twice[over]) + mm_nt(x_high[at], dy_low[over])
                acc[at, over] += outer * decay
            both.append(jnp.concatenate(done, axis=0))
        dx_ref[:, here] = jnp.where(lane < HEAD_DIM, both[0], both[1])

    if not ends:
        return

    @pl.when(step == pl.num_programs(0) - 1)
    def _():
        dbc_ref = ends[0]
        doc_col = m_ref[:, CONV_K : CONV_K + 1]
        ds = split(acc[...] * same_mask(doc_ref[0:1], doc_col, True))
        dbc_ref[:, :STATE] = three(mm, ds, split(bc_ref[:, STATE:]))
        dbc_ref[:, STATE:] = three(mm_tn, ds, split(bc_ref[:, :STATE]))


def carry_body(
    first, dx_ref, x_ref, dy_ref, pre_ref, in_ref, w_ref, m_ref, bc_ref, r_ref, end_ref, wl_ref, dt_ref,
    skip_ref, db_in, g_in, flow_in, *refs,
):
    extra = refs[:-6]
    d_ref, edge_ref, conv_ref, db_ref, g_ref, flow_ref = refs[-6:]
    if extra:
        pre_bc, in_bc, w_bc, dbc_ref, dc_ref, shifted_ref, rate_ref, q_ref, heads_ref = extra
    step = pl.program_id(0)
    count = INNER // 2 // BLOCK

    @pl.when(step == 0)
    def _():
        db_ref[...] = db_in[...]
        g_ref[...] = g_in[...]
        flow_ref[...] = flow_in[...]

    def conv(d_act, pre, inputs, weight, width):
        sig = sigmoid(pre)
        d_pre = d_act * (sig * (1.0 + pre * (1.0 - sig)))
        d_ext, sums = conv_back(d_pre, inputs, weight, m_ref[...])
        d_ref[:, :width] = d_ext[LEAD:].astype(BF)
        edge_ref[:LEAD, :width] = d_ext[:LEAD]
        edge_ref[LEAD:, :width] = d_ext[d_ext.shape[0] - LEAD :]
        conv_ref[:, :width] = sums

    @pl.when(step < count)
    def _():
        places = head_of_lane((step + first) * BLOCK_HEADS, BLOCK)
        returned = r_ref[0]
        r_parts = split(returned)
        to_end = expand(wl_ref[...], places)
        steps = expand(dt_ref[...], places)
        x = x_ref[...]
        d_scaled = dx_ref[...] + to_end * three(mm, split(bc_ref[:, :STATE]), r_parts)
        g_ref[...] += fold(x * d_scaled, places)
        db_ref[...] += three(mm_nt, split(to_end * steps * x), r_parts)
        flow = jnp.sum(returned * end_ref[0], axis=0, keepdims=True)
        high, middle, low = parts_of(jnp.broadcast_to(flow, (8, BLOCK)))
        flow_ref[...] += mm_nt(high, places) + mm_nt(middle, places) + mm_nt(low, places)
        d_x = steps * d_scaled + skip_ref[...] * dy_ref[...]
        conv(d_x, pre_ref[...], in_ref[...].astype(F32), w_ref[...], BLOCK)

    if not extra:
        return

    @pl.when(step == count)
    def _():
        width = 2 * STATE
        d_bc = jnp.concatenate([dbc_ref[:, :STATE] + db_ref[...], dbc_ref[:, STATE:] + dc_ref[...]], axis=1)
        conv(d_bc, pre_bc[...], in_bc[...].astype(F32), w_bc[...], width)
        masks = m_ref[...]
        steps, rate, shifted = dt_ref[...], rate_ref[...], shifted_ref[...]
        difference = q_ref[...] - steps * g_ref[...]
        d_log = (flow_ref[0:1] + running_sum(difference, True)) * masks[:, CONV_K - 2 : CONV_K - 1]
        d_steps = g_ref[...] - rate * d_log
        d_dt = d_steps * sigmoid(shifted)
        head = lax.broadcasted_iota(jnp.int32, d_dt.shape, 1) < HEADS
        d_dt = jnp.where(head, d_dt, 0.0)
        d_ref[:, width : width + STATE] = d_dt.astype(BF)
        edge_ref[:LEAD, width : width + STATE] = jnp.zeros((LEAD, STATE), F32)
        edge_ref[LEAD:, width : width + STATE] = d_dt[d_dt.shape[0] - LEAD :]
        conv_ref[:, width : width + STATE] = jnp.zeros((8, STATE), F32)
        heads_ref[0:8] = jnp.broadcast_to(jnp.sum(d_dt, axis=0, keepdims=True), (8, STATE))
        log_sum = -jnp.sum(steps * rate * d_log, axis=0, keepdims=True)
        heads_ref[8:16] = jnp.broadcast_to(log_sum, (8, STATE))


def woven(ref, devices, rows):
    pieces = [ref[side, d * rows : d * rows + rows, :] for d in range(devices) for side in range(2)]
    return jnp.concatenate(pieces, axis=0)


def d_final_body(devices, rows, g_ref, w_ref, o_ref):
    o_ref[...] = mm_nt(g_ref[...], woven(w_ref, devices, rows))


def layer_body(devices, rows, f_ref, w_ref, t_ref, o_ref, total):
    @pl.when(pl.program_id(0) == 0)
    def _():
        total[...] = t_ref[...].astype(F32)

    total[...] += mm(f_ref[...], woven(w_ref, devices, rows))

    @pl.when(pl.program_id(0) == pl.num_programs(0) - 1)
    def _():
        o_ref[...] = total[...].astype(BF)


def back_z_body(d_ref, w_ref, o_ref):
    half = w_ref.shape[2]
    o_ref[...] = mm_nt(d_ref[:, :half], w_ref[0]) + mm_nt(d_ref[:, half:], w_ref[1])


def back_x_body(da_ref, db_ref, w_ref, part_ref, o_ref):
    half = da_ref.shape[1]
    o_ref[...] = part_ref[...] + mm_nt(da_ref[...], w_ref[:, :half]) + mm_nt(db_ref[...], w_ref[:, half:])


def back_norm_body(d_ref, x_ref, og_ref, gain_ref, o_ref, sum_ref):
    @pl.when(pl.program_id(0) == 0)
    def _():
        sum_ref[...] = jnp.zeros_like(sum_ref)

    d_normed = d_ref[...]
    x = x_ref[...].astype(F32)
    scale = lax.rsqrt(jnp.mean(x * x, axis=-1, keepdims=True) + EPS)
    unit = x * scale
    pulled = d_normed * gain_ref[...]
    inner = jnp.mean(pulled * unit, axis=-1, keepdims=True)
    o_ref[...] = og_ref[...].astype(F32) + scale * (pulled - unit * inner)
    total = jnp.sum(d_normed * unit, axis=0, keepdims=True)
    sum_ref[...] += jnp.broadcast_to(total, sum_ref.shape)


def swap(array, axis):
    return lax.ppermute(array, axis, [(0, 1), (1, 0)])


def from_behind(array, by):
    peers = lax.axis_size(CTX[0]) * lax.axis_size(CTX[1])
    pairs = [(i, i + by) for i in range(peers) if 0 <= i + by < peers]
    return lax.ppermute(array, CTX, pairs)


def entering(state, decay, reverse, fills):
    fills = list(fills)

    def meanwhile(sent, arrived):
        return tie(arrived, *fills.pop(0)(sent)) if fills else arrived

    depth, width = lax.axis_size("z"), lax.axis_size("y")
    place_z, place_y = lax.axis_index("z"), lax.axis_index("y")
    if width != 2:
        gathered = lax.all_gather(jnp.concatenate([state, decay], axis=1), CTX)
        while fills:
            gathered = meanwhile(state, gathered)
        count = depth * width
        place = place_z * width + place_y
        ahead = count - 1 - place if reverse else place

        def one(lap, running):
            source = count - 1 - lap if reverse else lap
            item = lax.dynamic_index_in_dim(gathered, source, 0, False)
            return item[:, STATE : STATE + 1] * running + item[:, :STATE]

        return lax.fori_loop(0, ahead, one, jnp.zeros_like(state))
    second = place_y == (0 if reverse else 1)
    sent = pick(state, 1 - place_y)
    got = meanwhile(sent, swap(sent, "y"))
    own = pick(state, place_y)
    decay_own = pick(decay, place_y)[:1]
    decay_got = swap(pick(decay, 1 - place_y), "y")[:1]
    early = jnp.where(second, got, own)
    late = jnp.where(second, own, got)
    decay_early = jnp.where(second, decay_got, decay_own)
    decay_late = jnp.where(second, decay_own, decay_got)
    total = decay_late * early + late
    decay_total = decay_early * decay_late
    before = jnp.zeros_like(total)
    sent = total
    turn = depth - 1 - place_z if reverse else place_z
    for hop in range(1, depth):
        pairs = [(depth - hop, depth - 1 - hop)] if reverse else [(hop - 1, hop)]
        arrived = meanwhile(sent, lax.ppermute(sent, "z", pairs))
        before = jnp.where(turn == hop, arrived, before)
        sent = decay_total * before + total
    middle = decay_early * before + early
    mine = jnp.where(second, middle, before)
    sent = jnp.where(second, before, middle)
    theirs = swap(sent, "y")
    while fills:
        theirs = meanwhile(sent, theirs)
    return in_order(mine, theirs, "y")


def pick(parts, index, dim=0):
    return lax.dynamic_index_in_dim(parts, index, dim, False)


def in_order(mine, theirs, axis):
    first = lax.axis_index(axis) == 0
    return jnp.where(first, jnp.stack([mine, theirs]), jnp.stack([theirs, mine]))


def across(array, axis, by):
    return lax.ppermute(array, axis, [(i, i ^ by) for i in range(lax.axis_size(axis))])


def products_body(
    patched, place_ref, sent_own, kept_own, sent_other, kept_other, own_ref, other_ref, *refs
):
    sent_ref, kept_ref = refs[-2:]
    own, other = own_ref[...], other_ref[...]
    if patched:
        upto = own.shape[0] - LEAD
        own = jnp.concatenate([own[:upto], refs[0][...]], axis=0)
        other = jnp.concatenate([other[:upto], refs[1][...]], axis=0)

    def product(first, second):
        first, second = first[...], second[...]
        first = first.reshape(-1, first.shape[-1])
        second = second.reshape(-1, second.shape[-1])
        return mm(first, own) + mm(second, other)

    sent_ref[...] = product(sent_own, sent_other).astype(BF)
    kept_ref[...] = product(kept_own, kept_other)


def products(left, right, start, count, axis, waits):
    own, other = left
    sizes = [lax.axis_size(a) for a in ("x", "z", "y")]
    tokens = own.shape[1]
    rows = other.shape[0] // sizes[0] // sizes[1] // sizes[2]
    out_rows = other.shape[0] // 2
    places = jnp.stack([lax.axis_index(a) for a in ("core", "x", "y")])
    if axis == "x":
        own = own.reshape(2, 2, out_rows, tokens)
        other = other.reshape(2, out_rows, tokens)
        own_block, other_block = (1, 1, out_rows, tokens), (1, out_rows, tokens)

        def spec(mine, flip):
            if mine:
                return pl.BlockSpec(own_block, lambda g, p: (p[1] ^ flip, p[0], 0, 0))
            return pl.BlockSpec(other_block, lambda g, p: (p[1] ^ flip, 0, 0))
    else:
        own = own.reshape(2, 2, sizes[1], 2, rows, tokens)
        other = other.reshape(2 * sizes[1], 2, rows, tokens)
        own_block = (2, 1, sizes[1], 1, rows, tokens)
        other_block = (2 * sizes[1], 1, rows, tokens)

        def spec(mine, flip):
            if mine:
                return pl.BlockSpec(own_block, lambda g, p: (0, p[0], 0, p[2] ^ flip, 0, 0))
            return pl.BlockSpec(other_block, lambda g, p: (0, p[2] ^ flip, 0, 0))

    block = 384 if count % 384 == 0 else 512
    first = start // block
    columns_of = pl.BlockSpec((tokens, block), lambda g, p: (0, g + first))
    edge_of = pl.BlockSpec((LEAD, block), lambda g, p: (0, g + first))
    result = pl.BlockSpec((out_rows, block), lambda g, p: (0, g))
    return call(
        functools.partial(products_body, len(right) > 2), -(-count // block), count * out_rows / 2.0e5,
        [
            (own, spec(True, 1)), (own, spec(True, 0)), (other, spec(False, 1)), (other, spec(False, 0)),
            (right[0], columns_of), (right[1], columns_of),
            *[(edge, edge_of) for edge in right[2:]],
        ],
        [(out((out_rows, count), BF), result), (out((out_rows, count)), result)],
        waits=waits,
        places=places,
    )


def products_any(left, right, start, count, axis):
    core, place = lax.axis_index("core"), lax.axis_index(axis)
    sizes = [lax.axis_size(a) for a in ("x", "z", "y")]
    own = core_rows(left[0], core).reshape(left[1].shape)
    both = jnp.concatenate([own, left[1]], axis=1)
    view = both.reshape(*sizes, -1, both.shape[1])
    if axis == "y":
        view = jnp.moveaxis(view, 2, 0)
    view = view.reshape(view.shape[0], -1, both.shape[1])
    if len(right) > 2:
        upto = right[0].shape[0] - LEAD
        right = [right[0][:upto], right[2], right[1][:upto], right[3]]
    right = jnp.concatenate(right, axis=0)[:, start : start + count]
    sent = [mm(pick(view, place ^ by), right).astype(BF) for by in range(1, view.shape[0])]
    return sent, mm(pick(view, place), right)


def total_of(kept, got):
    for piece in got:
        kept = kept + piece.astype(F32)
    return kept


def tied(value, others):
    return tie(value, *others) if others else value


def xor_parts(parts, axis):
    count, place = lax.axis_size(axis), lax.axis_index(axis)
    return pick(parts, place), [pick(parts, place ^ by).astype(BF) for by in range(1, count)]


def travel(sent, axis, others):
    return [across(tied(piece, others), axis, by + 1) for by, piece in enumerate(sent)]


def places_here():
    return jnp.stack([lax.axis_index(a) for a in ("core", "x", "y")])


def second_body(place_ref, *refs):
    for side in range(2):
        kept_own, got_own, kept_next, got_next = refs[4 * side : 4 * side + 4]
        own_ref, next_ref = refs[8 + 2 * side : 10 + 2 * side]
        own_ref[...] = (kept_own[...] + got_own[...].astype(F32)).reshape(own_ref.shape)
        next_ref[...] = (kept_next[...] + got_next[...].astype(F32)).reshape(next_ref.shape).astype(BF)


def second_stage(kept_x, got_x, kept_y, got_y, depth, waits):
    rows = kept_x.shape[0] // (2 * depth)
    ins, outs = [], []
    for kept, got, by_y in ((kept_x, got_x, True), (kept_y, got_y, False)):
        width = kept.shape[1]
        shape = (depth, 2, rows, width) if by_y else (2, depth, rows, width)

        def spec(flip, by_y=by_y, width=width):
            if by_y:
                return pl.BlockSpec((1, 1, rows, width), lambda g, p: (g, p[2] ^ flip, 0, 0))
            return pl.BlockSpec((1, 1, rows, width), lambda g, p: (p[1] ^ flip, g, 0, 0))

        for flip in (0, 1):
            ins += [(kept.reshape(shape), spec(flip)), (got.reshape(shape), spec(flip))]
        result = pl.BlockSpec((1, rows, width), lambda g, p: (g, 0, 0))
        outs += [(out((depth, rows, width)), result), (out((depth, rows, width), BF), result)]
    return call(second_body, depth, 3, ins, outs, waits=waits, places=places_here())


def third_body(own_x, came_x, own_y, came_y, o_ref):
    width = own_x.shape[2]
    o_ref[:, :, :width] = (own_x[...] + came_x[...].astype(F32)).astype(o_ref.dtype)
    o_ref[:, :, width:] = (own_y[...] + came_y[...].astype(F32)).astype(o_ref.dtype)


def third_stage(own_x, came_x, own_y, came_y, kind, waits):
    depth, rows, wide_x = own_x.shape
    wide_y = own_y.shape[2]

    def spec(width):
        return pl.BlockSpec((1, rows, width), lambda g: (g, 0, 0))

    return call(
        third_body, depth, 2,
        [(own_x, spec(wide_x)), (came_x, spec(wide_x)), (own_y, spec(wide_y)), (came_y, spec(wide_y))],
        [(out((depth, rows, wide_x + wide_y), kind), spec(wide_x + wide_y))],
        waits=waits,
    )[0]


class Reduction:
    def __init__(self, left, right, start, middle, end, waits=()):
        if lax.axis_size("x") == 2 and lax.axis_size("y") == 2:
            sent_x, self.kept_x = products(left, right, start, middle - start, "x", waits)
            sent_y, self.kept_y = products(left, right, middle, end - middle, "y", waits)
            self.sent_x, self.sent_y = [sent_x], [sent_y]
        else:
            self.sent_x, self.kept_x = products_any(left, right, start, middle - start, "x")
            self.sent_y, self.kept_y = products_any(left, right, middle, end - middle, "y")

    def made(self):
        return [self.kept_x, self.kept_y, *self.sent_x, *self.sent_y]

    def launch(self, *others):
        self.got_x = travel(self.sent_x, "x", others)
        self.got_y = travel(self.sent_y, "y", others)

    def second(self, *others):
        sizes = [lax.axis_size(a) for a in ("x", "z", "y")]
        self.pairs = sizes[0] == 2 and sizes[2] == 2
        if self.pairs:
            self.own_x, next_x, self.own_y, next_y = second_stage(
                self.kept_x, self.got_x[0], self.kept_y, self.got_y[0], sizes[1], others
            )
            self.next_x, self.next_y = [next_x], [next_y]
            self.came_x = travel(self.next_x, "y", ())
            self.came_y = travel(self.next_y, "x", ())
            return
        part_x = total_of(tied(self.kept_x, others), self.got_x)
        part_y = total_of(tied(self.kept_y, others), self.got_y)
        view_x = part_x.reshape(sizes[1], sizes[2], -1, part_x.shape[1])
        view_y = part_y.reshape(sizes[0], sizes[1], -1, part_y.shape[1])
        self.own_x, self.next_x = xor_parts(jnp.moveaxis(view_x, 1, 0), "y")
        self.own_y, self.next_y = xor_parts(view_y, "x")
        self.came_x = travel(self.next_x, "y", ())
        self.came_y = travel(self.next_y, "x", ())

    def third(self, *others, kind=F32):
        place = lax.axis_index("z")
        if self.pairs:
            self.parts = third_stage(
                self.own_x, self.came_x[0], self.own_y, self.came_y[0], kind, others
            )
        else:
            done_x = total_of(tied(self.own_x, others), self.came_x)
            done_y = total_of(tied(self.own_y, others), self.came_y)
            self.parts = jnp.concatenate([done_x, done_y], axis=2).astype(kind)
        self.mine = None
        if kind == BF:
            sides = ((self.own_x, self.came_x), (self.own_y, self.came_y))
            self.mine = jnp.concatenate(
                [total_of(pick(own, place), [pick(c, place) for c in came]) for own, came in sides], axis=1
            )
        self.got_z = lax.all_to_all(self.parts, "z", 0, 0, tiled=True)

    def last(self, *others):
        got = tied(self.got_z, others)
        if self.mine is None:
            return jnp.sum(got, axis=0)
        others_only = lax.broadcasted_iota(jnp.int32, got.shape, 0) != lax.axis_index("z")
        return self.mine + jnp.sum(jnp.where(others_only, got.astype(F32), 0.0), axis=0)


def core_rows(turned, core):
    view = turned.reshape(lax.axis_size("x"), 2, -1, turned.shape[1])
    return pick(view, core, 1)


def both_cores(turned, core):
    theirs = core_rows(turned, 1 - core)
    return turned, swap(theirs.reshape(-1, turned.shape[1]), "core")


def document_ids(lengths, positions):
    first_end = lengths[0]
    second_end = lengths[0] + lengths[1]
    inside = (positions >= first_end).astype(jnp.int32) + (positions >= second_end).astype(jnp.int32)
    return jnp.where(positions < 0, -1, inside)


def gather_small(pieces, count):
    flat = jnp.concatenate([piece.reshape(-1) for piece in pieces])
    spread = jnp.broadcast_to(flat[None], (count, flat.shape[0]))
    return lax.all_to_all(spread, EVERY, 0, 0, tiled=True)


def columns(array, width):
    return jnp.pad(array, ((0, 0), (0, width - array.shape[1])))


def shards(
    tokens, out_grad, seq_lengths, norm_gain, in_weight, conv_weight, conv_bias,
    dt_bias, a_log, skip_gain, gated_gain, out_weight,
):
    count = 1
    for axis in EVERY:
        count *= lax.axis_size(axis)
    core = lax.axis_index("core")
    place = lax.axis_index("z") * lax.axis_size("y") + lax.axis_index("y")
    row_count, width = tokens.shape
    first_row = place * row_count
    full_rows = LEAD + row_count
    half = INNER // 2
    bc_width = CONVW - INNER
    square = (row_count, row_count)

    lead_tokens = from_behind(tokens[row_count - LEAD :], 1)
    small = gather_small([norm_gain, conv_weight, conv_bias, gated_gain], count)
    weight_x = lax.all_gather(columns(in_weight[:, INNER:], PROJ_X), EVERY, axis=0, tiled=True)
    rows_out = out_weight.shape[0] // 2
    stacked = jnp.stack(
        [in_weight[:, :half], in_weight[:, half:INNER], out_weight[:rows_out], out_weight[rows_out:]]
    )
    stacked = lax.all_gather(stacked, EVERY, axis=1, tiled=True)
    cuts = [norm_gain.size, conv_weight.size, conv_bias.size]
    cuts = [sum(cuts[: i + 1]) for i in range(3)]
    gain_piece, conv_piece, bias_piece, gated_piece = jnp.split(small, cuts, axis=1)
    full_gain = gain_piece.reshape(1, -1).astype(F32)
    full_conv = jnp.moveaxis(conv_piece.reshape(count, CONV_K, -1), 1, 0).reshape(CONV_K, -1)
    full_conv = jnp.pad(full_conv.astype(F32), ((0, 4), (0, 0)))
    full_bias = bias_piece.reshape(1, -1).astype(F32)
    full_gated = gated_piece.reshape(1, -1).astype(F32)

    normed_ext, turned = call(
        norm_body, 1, 4,
        [
            (lead_tokens, whole(LEAD, width)),
            (tokens, whole(row_count, width)),
            (full_gain, whole(1, width)),
        ],
        [
            (out((full_rows, width), BF), whole(full_rows, width)),
            (out((width, row_count), BF), whole(width, row_count)),
        ],
    )
    normed = normed_ext[LEAD:]
    normed_left = both_cores(turned, core)
    out_grad_theirs = swap(out_grad, "core")

    lengths = seq_lengths[0]
    ordinal = jnp.arange(row_count, dtype=jnp.int32)
    doc_ids = document_ids(lengths, first_row + ordinal)
    doc_before = document_ids(lengths, first_row - 1 + jnp.zeros((1,), jnp.int32))
    marks = [
        document_ids(lengths, first_row + ordinal - (CONV_K - 1 - tap)) == doc_ids
        for tap in range(CONV_K)
    ]
    marks = marks + [doc_ids, doc_ids == doc_before[0], doc_ids == doc_ids[row_count - 1]]
    masks = columns(jnp.stack([mark.astype(F32) for mark in marks], axis=1), 128)
    doc_rows = jnp.broadcast_to(doc_ids.astype(F32)[None], (8, row_count))
    rate = columns(jnp.exp(a_log)[None], 128)
    shift = columns(dt_bias[None], 128)
    skip_wide = jnp.repeat(skip_gain, HEAD_DIM)[None]
    mixed_x = mm(normed_ext, weight_x).astype(BF)

    block_bc = pl.BlockSpec((full_rows, bc_width), lambda g: (0, INNER // bc_width))
    block_dr = pl.BlockSpec((full_rows, 128), lambda g: (0, CONVW // 128))
    per_token = whole(row_count, 128)
    a_token = (out((row_count, 128)), per_token)
    pre_bc, act_bc, act_t, scores, scores_t, steps, enter, to_end, cumulative, cum_turned, shifted = call(
        prep_bc_body, 1, 6,
        [
            (mixed_x, block_bc),
            (mixed_x, block_dr),
            (full_conv[:, INNER:], whole(8, bc_width)),
            (full_bias[:, INNER:], whole(1, bc_width)),
            (masks, per_token),
            (doc_rows, whole(8, row_count)),
            (shift, whole(1, 128)),
            (rate, whole(1, 128)),
        ],
        [
            (out((row_count, bc_width)), whole(row_count, bc_width)),
            (out((row_count, bc_width)), whole(row_count, bc_width)),
            (out((bc_width, row_count)), whole(bc_width, row_count)),
            (out(square), whole(*square)),
            (out(square), whole(*square)),
            a_token, a_token, a_token, a_token,
            (out((128, row_count)), whole(128, row_count)),
            a_token,
        ],
    )
    pre_x, act_x, state_local, device_decay = call(
        prep_x_body, INNER // BLOCK, 12,
        [
            (mixed_x, lanes(full_rows, BLOCK)),
            (full_conv[:, :INNER], lanes(8, BLOCK)),
            (full_bias[:, :INNER], lanes(1, BLOCK)),
            (masks, per_token),
            (to_end, per_token),
            (steps, per_token),
            (enter, per_token),
            (act_t, whole(bc_width, row_count)),
        ],
        [
            (out((row_count, INNER)), lanes(row_count, BLOCK)),
            (out((row_count, INNER)), lanes(row_count, BLOCK)),
            (out((2, STATE, half)), halves(STATE, BLOCK)),
            (out((2, 8, half)), halves(8, BLOCK)),
        ],
    )

    heads_block = 2 * PAIRS
    groups = HEADS // heads_block
    half_groups = groups // 2
    cum_rows = cum_turned[:HEADS].reshape(groups, heads_block, row_count)
    kept = {}

    def pairs_at(index):
        return pl.BlockSpec((row_count, PAIR_LANES), lambda g: (0, g + index * half_groups))

    def cums_at(index):
        return pl.BlockSpec((1, heads_block, row_count), lambda g: (g + index * half_groups, 0, 0))

    def intra(index, wait):
        kept[index] = call(
            functools.partial(intra_body, index * half_groups), half_groups, 12,
            [
                (act_x, pairs_at(index)),
                (steps, per_token),
                (skip_wide, pl.BlockSpec((1, PAIR_LANES), lambda g: (0, g + index * half_groups))),
                (scores, whole(*square)),
                (cumulative, per_token),
                (cum_rows, cums_at(index)),
            ],
            [(out((row_count, half)), lanes(row_count, PAIR_LANES))],
            waits=[wait],
        )[0]
        return [kept[index]]

    devices = 4
    out_block = 2 * devices * rows_out
    out_blocks = count // devices
    weight_block = pl.BlockSpec((2, devices * rows_out, width), lambda g: (1, g, 0))
    direct = rows_out % 16 == 0

    def project(wait):
        if direct:
            kept["d_final"] = call(
                functools.partial(d_final_body, devices, rows_out), out_blocks, 7,
                [(out_grad, whole(row_count, width)), (stacked, weight_block)],
                [(out((row_count, INNER)), lanes(row_count, out_block))],
                waits=[wait],
            )[0]
        else:
            weight_o = jnp.moveaxis(stacked[2:].reshape(2, count, rows_out, width), 0, 1)
            kept["weight_o"] = weight_o.reshape(-1, width)
            kept["d_final"] = mm_nt(out_grad, kept["weight_o"])
        kept["mixed_z"] = [mm(normed, stacked[side]).astype(BF) for side in range(2)]
        return [kept["d_final"], *kept["mixed_z"]]

    state_in = entering(
        state_local, device_decay, False,
        [
            lambda wait: intra(0, wait), lambda wait: intra(1, wait), lambda wait: [], lambda wait: [],
            project,
        ],
    )
    state_end = device_decay[:, :1] * state_in + state_local

    tile = 128
    final, final_turned, d_z, d_y, returned_local, d_c_carry, dy_y, sums = call(
        gate_body, row_count // tile, 31,
        [
            (kept[0], rows_of(tile, half)),
            (kept[1], rows_of(tile, half)),
            (kept["mixed_z"][0], rows_of(tile, half)),
            (kept["mixed_z"][1], rows_of(tile, half)),
            (kept["d_final"], rows_of(tile, INNER)),
            (act_x, rows_of(tile, INNER)),
            (act_bc[:, STATE:], rows_of(tile, STATE)),
            (act_t[STATE:], lanes(STATE, tile)),
            (state_in, whole(2, STATE, half)),
            (enter, rows_of(tile, 128)),
            (full_gated, whole(1, INNER)),
            (skip_wide, whole(1, INNER)),
        ],
        [
            (out((row_count, INNER), BF), rows_of(tile, INNER)),
            (out((INNER, row_count), BF), lanes(INNER, tile)),
            (out((row_count, INNER), BF), rows_of(tile, INNER)),
            (out((row_count, INNER)), rows_of(tile, INNER)),
            (out((2, STATE, half)), whole(2, STATE, half)),
            (out((row_count, STATE)), rows_of(tile, STATE)),
            (out((row_count, 128)), rows_of(tile, 128)),
            (out((16, INNER)), whole(16, INNER)),
        ],
        [pltpu.VMEM((tile, INNER), F32), pltpu.VMEM((tile, INNER), F32)],
    )

    final_left = both_cores(final_turned, core)
    d_z_theirs = swap(d_z, "core")
    back = {"acc": jnp.zeros(square, F32)}

    def out_sums(wait):
        back["out"] = Reduction(final_left, [out_grad, out_grad_theirs], 0, width // 2, width, [wait])
        back["out"].launch()
        return back["out"].made()

    def z_sums(wait):
        back["z"] = Reduction(normed_left, [d_z, d_z_theirs], 0, half, INNER, [wait])
        back["z"].launch()
        return back["z"].made()

    def within(index, wait):
        ends = [(out((row_count, bc_width)), whole(row_count, bc_width))] if index else []
        back[index], back["acc"], *back["bc"] = call(
            functools.partial(back_body, index * half_groups), half_groups, 18,
            [
                (act_x, pairs_at(index)),
                (d_y, pairs_at(index)),
                (steps, per_token),
                (scores_t, whole(*square)),
                (cumulative, per_token),
                (cum_rows, cums_at(index)),
                (act_bc, whole(row_count, bc_width)),
                (doc_rows, whole(8, row_count)),
                (masks, per_token),
                (back["acc"], whole(*square)),
            ],
            [
                (out((row_count, half)), lanes(row_count, PAIR_LANES)),
                (out(square), whole(*square)),
                *ends,
            ],
            waits=[wait],
        )
        return [back[index]]

    def first_within(wait):
        back["out"].second(wait)
        return within(0, wait)

    def second_within(wait):
        return within(1, wait)

    norm_block = 256

    def send_out(wait):
        back["z"].second(wait)
        back["out"].third(wait)
        return [back["out"].parts, *back["z"].next_x, *back["z"].next_y]

    returned = entering(
        returned_local, device_decay, True,
        [out_sums, z_sums, first_within, second_within, send_out],
    )

    blocks = half // BLOCK

    def carried(index, earlier, extra, extra_out, waits):
        steps_count = blocks + len(extra_out)
        own = pl.BlockSpec((row_count, BLOCK), lambda g: (0, jnp.minimum(g, blocks - 1)))

        def at(rows):
            return pl.BlockSpec((rows, BLOCK), lambda g: (0, jnp.minimum(g, blocks - 1) + index * blocks))

        state_at = pl.BlockSpec((1, STATE, BLOCK), lambda g: (index, 0, jnp.minimum(g, blocks - 1)))
        wide = half + len(extra_out) * (PROJ_X - INNER)
        return call(
            functools.partial(carry_body, index * blocks), steps_count, 14 + 4 * index,
            [
                (back[index], own),
                (act_x, at(row_count)),
                (d_y, at(row_count)),
                (pre_x, at(row_count)),
                (mixed_x, at(full_rows)),
                (full_conv[:, :INNER], at(8)),
                (masks, per_token),
                (act_bc, whole(row_count, bc_width)),
                (returned, state_at),
                (state_end, state_at),
                (to_end, per_token),
                (steps, per_token),
                (skip_wide, at(1)),
                *[(array, whole(*array.shape)) for array in earlier],
                *extra,
            ],
            [
                *extra_out,
                (out((row_count, wide), BF), lanes(row_count, BLOCK)),
                (out((2 * LEAD, wide)), lanes(2 * LEAD, BLOCK)),
                (out((8, wide)), lanes(8, BLOCK)),
                (out((row_count, STATE)), whole(row_count, STATE)),
                a_token,
                (out((8, 128)), whole(8, 128)),
            ],
            waits=waits,
        )

    none = jnp.zeros((row_count, 128), F32)
    d_xa, edge_a, conv_a, *so_far = carried(0, [none, none, none[:8]], [], [], [])
    back["z"].third(edge_a)
    d_xa_theirs = swap(d_xa, "core")
    halo_a = from_behind(edge_a[:LEAD], -1)
    last_a = (edge_a[LEAD:] + halo_a).astype(BF)
    last_a_theirs = swap(last_a, "core")
    sums_a = Reduction(normed_left, [d_xa, d_xa_theirs, last_a, last_a_theirs], 0, half // 2, half, [back["z"].parts, back["out"].got_z])
    sums_a.launch()
    heads, d_xb, edge_b, conv_b, *_ = carried(
        1, so_far,
        [
            (pre_bc, whole(row_count, bc_width)),
            (mixed_x, block_bc),
            (full_conv[:, INNER:], whole(8, bc_width)),
            (back["bc"][0], whole(row_count, bc_width)),
            (d_c_carry, whole(row_count, STATE)),
            (shifted, per_token),
            (rate, whole(1, 128)),
            (dy_y, per_token),
        ],
        [(out((16, 128)), whole(16, 128))],
        sums_a.made(),
    )
    d_xb_theirs = swap(d_xb, "core")
    halo_b = from_behind(edge_b[:LEAD], -1)
    sums_a.second(edge_b)
    sums_a.third()
    d_normed_z = call(
        back_z_body, width // norm_block, 10,
        [
            (d_z, whole(row_count, INNER)),
            (stacked, pl.BlockSpec((2, norm_block, half), lambda g: (0, g, 0))),
        ],
        [(out((row_count, width)), lanes(row_count, norm_block))],
        waits=[edge_b],
    )[0]
    last_b = (edge_b[LEAD:] + tie(halo_b, d_normed_z)).astype(BF)
    last_b_theirs = swap(last_b, "core")
    wide_b = d_xb.shape[1]
    sums_b = Reduction(
        normed_left, [d_xb, d_xb_theirs, last_b, last_b_theirs], 0, 1024, wide_b, [sums_a.parts]
    )
    sums_b.launch()

    d_xa = lax.dynamic_update_slice(d_xa, last_a, (row_count - LEAD, 0))
    d_xb = lax.dynamic_update_slice(d_xb, last_b, (row_count - LEAD, 0))
    d_normed = call(
        back_x_body, width // norm_block, 10,
        [
            (d_xa, whole(row_count, half)),
            (d_xb, whole(row_count, wide_b)),
            (weight_x, rows_of(norm_block, PROJ_X)),
            (d_normed_z, lanes(row_count, norm_block)),
        ],
        [(out((row_count, width)), lanes(row_count, norm_block))],
        waits=sums_b.made(),
    )[0]
    grad_tokens, gain_sums = call(
        back_norm_body, row_count // tile, 4,
        [
            (d_normed, rows_of(tile, width)),
            (tokens, rows_of(tile, width)),
            (out_grad, rows_of(tile, width)),
            (full_gain, whole(1, width)),
        ],
        [
            (out((row_count, width)), rows_of(tile, width)),
            (out((8, width)), whole(8, width)),
        ],
    )
    sums_b.second(grad_tokens)
    if direct:
        layer_out = call(
            functools.partial(layer_body, devices, rows_out), out_blocks, 13,
            [
                (final, lanes(row_count, out_block)),
                (stacked, weight_block),
                (tokens, whole(row_count, width)),
            ],
            [(out((row_count, width), BF), whole(row_count, width))],
            [pltpu.VMEM((row_count, width), F32)],
            waits=[*sums_b.next_x, *sums_b.next_y],
        )[0]
    else:
        layer_out = (tokens.astype(F32) + mm(final, kept["weight_o"])).astype(BF)

    conv_sums = jnp.concatenate([conv_a, conv_b[:, : CONVW - half]], axis=1)
    grad_skip = jnp.sum(jnp.sum(sums[8:], axis=0).reshape(HEADS, HEAD_DIM), axis=1)
    grad_gated = jnp.sum(sums[:8], axis=0)
    per_device = jnp.concatenate(
        [
            gain_sums[0].reshape(count, -1),
            jnp.moveaxis(conv_sums[:CONV_K].reshape(CONV_K, count, -1), 1, 0).reshape(count, -1),
            conv_sums[CONV_K].reshape(count, -1),
            grad_gated.reshape(count, -1),
            jnp.broadcast_to(
                jnp.concatenate([heads[0, :HEADS], heads[8, :HEADS], grad_skip])[None],
                (count, 3 * HEADS),
            ),
        ],
        axis=1,
    )
    sums_b.third(kind=BF)
    per_device = tie(per_device, *sums_b.next_x, *sums_b.next_y)
    arrived = lax.all_to_all(per_device, EVERY, 0, 0, tiled=True)
    done = [layer_out]
    sum_out, sum_in_z, sum_in_a = [each.last(*done) for each in (back["out"], back["z"], sums_a)]
    sum_in_b = sums_b.last()
    small_sums = jnp.sum(tie(arrived, layer_out), axis=0)
    cuts = [norm_gain.size, conv_weight.size, conv_bias.size, gated_gain.size, HEADS, HEADS]
    cuts = [sum(cuts[: i + 1]) for i in range(6)]
    sum_gain, sum_conv, sum_bias, sum_gated, sum_dt, sum_log, sum_skip = jnp.split(small_sums, cuts)
    sum_in = jnp.concatenate([sum_in_z, sum_in_a, sum_in_b[:, : in_weight.shape[1] - INNER - half]], axis=1)
    return (
        layer_out,
        grad_tokens,
        sum_gain,
        sum_in,
        sum_conv.reshape(conv_weight.shape),
        sum_bias,
        sum_dt,
        sum_log,
        sum_skip,
        sum_gated,
        sum_out,
    )


def solution(mesh):
    x = mesh.shape["dp"] // 2
    y = x
    z = mesh.shape["ctx"] // y
    fine = Mesh(mesh.devices.reshape(x, 2, z, y), EVERY)
    rows = P(EVERY, None)
    flat = P(EVERY)
    in_specs = (
        rows, rows, P(("x", "core"), None), flat, rows, P(None, EVERY), flat,
        P(), P(), P(), flat, rows,
    )
    out_specs = (rows, rows, flat, rows, P(None, EVERY), flat, P(), P(), P(), flat, rows)
    return jax.shard_map(shards, mesh=fine, in_specs=in_specs, out_specs=out_specs, check_vma=False)
```

```python
import functools

import jax
import jax.numpy as jnp
from jax import lax
from jax.experimental import pallas as pl
from jax.experimental.pallas import tpu as pltpu
from jax.sharding import Mesh, PartitionSpec as P

HEADS = 48
HEAD_DIM = 64
STATE = 128
CONV_K = 4
INNER = 3072
CONVW = 3328
LEAD = 16
PROJ_X = 3456
BLOCK = 512
BLOCK_HEADS = BLOCK // HEAD_DIM
PAIRS = 2
PAIR_LANES = 128 * PAIRS
VMEM = 56 * 1024 * 1024
F32 = jnp.float32
BF = jnp.bfloat16
EPS = 1e-05
highest = lax.Precision.HIGHEST
EVERY = ("x", "core", "z", "y")
CTX = ("z", "y")


def params():
    return pltpu.CompilerParams(vmem_limit_bytes=VMEM, dimension_semantics=("arbitrary",))


def call(body, grid, micros, ins, outs, scratch=(), waits=(), places=None):
    first = (places is not None) + len(ins)
    anywhere = pl.BlockSpec(memory_space=pl.ANY)

    def run(*refs):
        body(*refs[:first], *refs[first + len(waits) :])

    scalars = [] if places is None else [places]
    return pl.pallas_call(
        run,
        grid_spec=pltpu.PrefetchScalarGridSpec(
            num_scalar_prefetch=len(scalars),
            grid=(grid,),
            in_specs=[spec for _, spec in ins] + [anywhere] * len(waits),
            out_specs=[spec for _, spec in outs],
            scratch_shapes=list(scratch),
        ),
        out_shape=[shape for shape, _ in outs],
        compiler_params=params(),
        cost_estimate=pl.CostEstimate(
            flops=int(micros * 1e9), bytes_accessed=int(micros * 3e6), transcendentals=0
        ),
    )(*scalars, *[array for array, _ in ins], *waits)


def tie(value, *others):
    def body(*refs):
        pass

    anywhere = pl.BlockSpec(memory_space=pl.ANY)
    return pl.pallas_call(
        body,
        in_specs=[anywhere] * (1 + len(others)),
        out_specs=anywhere,
        out_shape=jax.ShapeDtypeStruct(value.shape, value.dtype),
        input_output_aliases={0: 0},
    )(value, *others)


def whole(*shape):
    return pl.BlockSpec(shape, lambda g: (0,) * len(shape))


def lanes(rows, width):
    return pl.BlockSpec((rows, width), lambda g: (0, g))


def rows_of(count, width):
    return pl.BlockSpec((count, width), lambda g: (g, 0))


def halves(rows, width):
    count = INNER // 2 // width
    return pl.BlockSpec((1, rows, width), lambda g: (g // count, 0, g % count))


def group(rows, width):
    return pl.BlockSpec((1, rows, width), lambda g: (g, 0, 0))


def out(shape, dtype=F32):
    return jax.ShapeDtypeStruct(shape, dtype)


def split(value):
    high = value.astype(BF)
    return high, (value - high.astype(F32)).astype(BF)


def mm(left, right):
    return jnp.dot(left, right, preferred_element_type=F32)


def mm_nt(left, right):
    return lax.dot_general(left, right, (((1,), (1,)), ((), ())), preferred_element_type=F32)


def mm_tn(left, right):
    return lax.dot_general(left, right, (((0,), (0,)), ((), ())), preferred_element_type=F32)


def three(product, left, right):
    left_high, left_low = left
    right_high, right_low = right
    return (
        product(left_high, right_high)
        + product(left_high, right_low)
        + product(left_low, right_high)
    )


def head_of_lane(first, count):
    lane = lax.broadcasted_iota(jnp.int32, (STATE, count), 1) // HEAD_DIM + first
    row = lax.broadcasted_iota(jnp.int32, (STATE, count), 0)
    return (lane == row).astype(BF)


def expand(value, places):
    high, low = split(value)
    return mm(high, places) + mm(low, places)


def fold(value, places):
    high, low = split(value)
    return mm_nt(high, places) + mm_nt(low, places)


def sigmoid(value):
    return 1.0 / (1.0 + jnp.exp(-value))


def conv_pre(extended, weight, bias, masks):
    running = jnp.zeros((masks.shape[0], extended.shape[1]), F32) + bias
    for tap in range(CONV_K):
        shifted = extended if tap == CONV_K - 1 else pltpu.roll(extended, CONV_K - 1 - tap, 0)
        running = running + shifted[LEAD:] * weight[tap : tap + 1] * masks[:, tap : tap + 1]
    return running


def conv_back(d_pre, extended, weight, masks):
    zeros = jnp.zeros((LEAD, d_pre.shape[1]), F32)
    total = LEAD + d_pre.shape[0]
    d_ext = jnp.zeros((total, d_pre.shape[1]), F32)
    weight_rows = []
    for tap in range(CONV_K):
        by = CONV_K - 1 - tap
        part = d_pre * masks[:, tap : tap + 1]
        padded = jnp.concatenate([zeros, part], axis=0)
        shifted = extended
        if by:
            padded = pltpu.roll(padded, total - by, 0)
            shifted = pltpu.roll(extended, by, 0)
        d_ext = d_ext + padded * weight[tap : tap + 1]
        weight_rows.append(jnp.sum(shifted[LEAD:] * part, axis=0, keepdims=True))
    weight_rows.append(jnp.sum(d_pre, axis=0, keepdims=True))
    weight_rows.append(jnp.zeros((8 - len(weight_rows), d_pre.shape[1]), F32))
    return d_ext, jnp.concatenate(weight_rows, axis=0)


def same_mask(doc_row, doc_col, transposed):
    count = doc_row.shape[1]
    rows = lax.broadcasted_iota(jnp.int32, (count, count), 0)
    cols = lax.broadcasted_iota(jnp.int32, (count, count), 1)
    order = rows <= cols if transposed else rows >= cols
    return jnp.where((doc_row == doc_col) & order, 1.0, 0.0)


def norm_body(lead_ref, x_ref, gain_ref, normed_ref, turned_ref):
    def normed(value):
        scale = lax.rsqrt(jnp.mean(value * value, axis=-1, keepdims=True) + EPS)
        return value * scale * gain_ref[...]

    normed_ref[:LEAD] = normed(lead_ref[...].astype(F32)).astype(BF)
    for tile in range(x_ref.shape[0] // 128):
        here = slice(tile * 128, tile * 128 + 128)
        value = normed(x_ref[here].astype(F32))
        normed_ref[LEAD + tile * 128 : LEAD + tile * 128 + 128] = value.astype(BF)
        turned_ref[:, here] = value.T.astype(BF)


def parts_of(value):
    high, low = split(value)
    return high, low, (value - high.astype(F32) - low.astype(F32)).astype(BF)


def running_sum(value, transposed):
    count = value.shape[0]
    rows = lax.broadcasted_iota(jnp.int32, (count, count), 0)
    cols = lax.broadcasted_iota(jnp.int32, (count, count), 1)
    side = ((rows <= cols) if transposed else (rows >= cols)).astype(BF)
    high, middle, low = parts_of(value)
    return mm(side, high) + mm(side, middle) + mm(side, low)


def softplus(value):
    return jnp.maximum(value, 0.0) + jnp.log1p(jnp.exp(-jnp.abs(value)))


def prep_bc_body(
    x_ref, dr_ref, w_ref, b_ref, m_ref, doc_ref, shift_ref, rate_ref,
    pre_ref, act_ref, t_ref, s_ref, st_ref, steps_ref, enter_ref, to_end_ref, cum_ref, turned_ref, dt_ref,
):
    masks = m_ref[...]
    pre = conv_pre(x_ref[...].astype(F32), w_ref[...], b_ref[...], masks)
    act = pre * sigmoid(pre)
    pre_ref[...] = pre
    act_ref[...] = act
    t_ref[...] = act.T
    b_rows, c_rows = split(act[:, :STATE]), split(act[:, STATE:])
    doc_row, doc_col = doc_ref[0:1], masks[:, CONV_K : CONV_K + 1]
    s_ref[...] = three(mm_nt, c_rows, b_rows) * same_mask(doc_row, doc_col, False)
    st_ref[...] = three(mm_nt, b_rows, c_rows) * same_mask(doc_row, doc_col, True)
    shifted = dr_ref[LEAD:, :].astype(F32) + shift_ref[...]
    steps = softplus(shifted)
    cumulative = running_sum(-steps * rate_ref[...], False)
    last = cumulative[cumulative.shape[0] - 1 :]
    dt_ref[...] = shifted
    steps_ref[...] = steps
    enter_ref[...] = jnp.exp(cumulative) * masks[:, CONV_K + 1 : CONV_K + 2]
    to_end_ref[...] = jnp.exp(last - cumulative) * masks[:, CONV_K + 2 : CONV_K + 3]
    cum_ref[...] = cumulative
    turned_ref[...] = cumulative.T


def prep_x_body(
    x_ref, w_ref, b_ref, m_ref, wl_ref, dt_ref, e_ref, t_ref, pre_ref, act_ref, state_ref, decay_ref
):
    pre = conv_pre(x_ref[...].astype(F32), w_ref[...], b_ref[...], m_ref[...])
    act = pre * sigmoid(pre)
    pre_ref[...] = pre
    act_ref[...] = act
    places = head_of_lane(pl.program_id(0) * BLOCK_HEADS, BLOCK)
    weighted = split(act * expand(wl_ref[...] * dt_ref[...], places))
    state_ref[0] = three(mm, split(t_ref[:STATE]), weighted)
    last = e_ref[e_ref.shape[0] - 8 :]
    high, middle, low = parts_of(last)
    spread = mm(high, places) + mm(middle, places) + mm(low, places)
    decay_ref[0] = jnp.broadcast_to(spread[7:8], spread.shape)


def heads_here(cum_ref, first):
    back = STATE - (pl.program_id(0) + first) * 2 * PAIRS
    return pltpu.roll(cum_ref[...], jnp.where(back == STATE, 0, back), 1)


def intra_body(first, x_ref, dt_ref, skip_ref, s_ref, cum_ref, row_ref, y_ref):
    half = s_ref.shape[0] // 2
    places = head_of_lane((pl.program_id(0) + first) * 2 * PAIRS, PAIR_LANES)
    scaled = x_ref[...] * expand(dt_ref[...], places)
    cols = heads_here(cum_ref, first)
    lane = lax.broadcasted_iota(jnp.int32, (2 * half, 128), 1)
    for pair in range(PAIRS):
        here = slice(pair * 128, pair * 128 + 128)
        high, low = split(scaled[:, here])
        right = jnp.concatenate([high, low], axis=1)
        both = []
        for side in range(2):
            head = 2 * pair + side
            col = cols[:, head : head + 1]
            row = row_ref[0, head : head + 1, :]
            top = s_ref[:half, :half] * jnp.exp(jnp.minimum(col[:half] - row[:, :half], 0.0))
            low_part = s_ref[half:, :] * jnp.exp(jnp.minimum(col[half:] - row, 0.0))
            done = []
            for part, count in ((top, half), (low_part, 2 * half)):
                p_high, p_low = split(part)
                first = mm(p_high, right[:count])
                done.append(first[:, :128] + first[:, 128:] + mm(p_low, high[:count]))
            both.append(jnp.concatenate(done, axis=0))
        y_ref[:, here] = (
            jnp.where(lane < HEAD_DIM, both[0], both[1]) + skip_ref[:, here] * x_ref[:, here]
        )


def gate_body(
    ya_ref, yb_ref, za_ref, zb_ref, df_ref, x_ref, c_ref, ct_ref, state_ref, e_ref, gain_ref, skip_ref,
    final_ref, turned_ref, dz_ref, dy_ref, r_ref, dc_ref, q_ref, sums_ref, carry, scaled,
):
    @pl.when(pl.program_id(0) == 0)
    def _():
        r_ref[...] = jnp.zeros_like(r_ref)
        sums_ref[...] = jnp.zeros_like(sums_ref)

    e_high, e_low = split(e_ref[...])
    c_rows = split(c_ref[...])
    for block in range(INNER // BLOCK):
        here = slice(block * BLOCK, block * BLOCK + BLOCK)
        places = head_of_lane(block * BLOCK_HEADS, BLOCK)
        spread = mm(e_high, places) + mm(e_low, places)
        there = slice(block % 3 * BLOCK, block % 3 * BLOCK + BLOCK)
        carry[:, here] = three(mm, c_rows, split(state_ref[block // 3, :, there])) * spread
        scaled[:, here] = spread
    gain, skip = gain_ref[...], skip_ref[...]

    def some(lap, sums):
        at = pl.ds(pl.multiple_of(lap * 16, 16), 16)
        y = jnp.concatenate([ya_ref[at, :], yb_ref[at, :]], axis=1) + carry[at, :]
        z = jnp.concatenate([za_ref[at, :], zb_ref[at, :]], axis=1).astype(F32)
        sig = sigmoid(z)
        gate = z * sig
        gated = y * gate
        scale = lax.rsqrt(jnp.mean(gated * gated, axis=-1, keepdims=True) + EPS)
        unit = gated * scale
        final_ref[at, :] = (unit * gain).astype(BF)
        d_final = df_ref[at, :]
        q = d_final * gain
        inner = jnp.mean(q * unit, axis=-1, keepdims=True)
        d_gated = scale * (q - unit * inner)
        d_y = d_gated * gate
        dz_ref[at, :] = (d_gated * y * (sig * (1.0 + z * (1.0 - sig)))).astype(BF)
        dy_ref[at, :] = d_y
        x = x_ref[at, :]
        scaled[at, :] = scaled[at, :] * d_y
        carry[at, :] = d_y * (y - skip * x)
        d_gain, d_skip = d_final * unit, d_y * x
        return (
            sums[0] + d_gain[:8] + d_gain[8:],
            sums[1] + d_skip[:8] + d_skip[8:],
        )

    zero = jnp.zeros((8, INNER), F32)
    d_gain, d_skip = lax.fori_loop(0, za_ref.shape[0] // 16, some, (zero, zero))
    sums_ref[0:8] += d_gain
    sums_ref[8:16] += d_skip
    ct_rows = split(ct_ref[...])
    d_c = jnp.zeros(dc_ref.shape, F32)
    q_sum = jnp.zeros(q_ref.shape, F32)
    for block in range(INNER // BLOCK):
        here = slice(block * BLOCK, block * BLOCK + BLOCK)
        there = slice(block % 3 * BLOCK, block % 3 * BLOCK + BLOCK)
        piece = split(scaled[:, here])
        r_ref[block // 3, :, there] += three(mm, ct_rows, piece)
        d_c = d_c + three(mm_nt, piece, split(state_ref[block // 3, :, there]))
        turned_ref[here, :] = final_ref[:, here].T
        q_sum = q_sum + fold(carry[:, here], head_of_lane(block * BLOCK_HEADS, BLOCK))
    dc_ref[...] = d_c
    q_ref[...] = q_sum


def back_body(first, x_ref, dy_ref, dt_ref, st_ref, cum_ref, row_ref, bc_ref, doc_ref, m_ref, in_ref, dx_ref, acc, *ends):
    step = pl.program_id(0)
    half = st_ref.shape[0] // 2

    @pl.when(step == 0)
    def _():
        acc[...] = in_ref[...]

    places = head_of_lane((step + first) * 2 * PAIRS, PAIR_LANES)
    scaled = x_ref[...] * expand(dt_ref[...], places)
    cols = heads_here(cum_ref, first)
    lane = lax.broadcasted_iota(jnp.int32, (2 * half, 128), 1)
    for pair in range(PAIRS):
        here = slice(pair * 128, pair * 128 + 128)
        dy_high, dy_low = split(dy_ref[:, here])
        right = jnp.concatenate([dy_high, dy_low], axis=1)
        twice = jnp.concatenate([dy_high, dy_high], axis=1)
        both = []
        for side in range(2):
            head = 2 * pair + side
            mine = (lane < HEAD_DIM) if side == 0 else (lane >= HEAD_DIM)
            x_high, x_low = split(jnp.where(mine, scaled[:, here], 0.0))
            x_both = jnp.concatenate([x_high, x_low], axis=1)
            col = cols[:, head : head + 1]
            row = row_ref[0, head : head + 1, :]
            done = []
            for at, over in ((slice(0, half), slice(0, 2 * half)), (slice(half, 2 * half), slice(half, 2 * half))):
                decay = jnp.exp(jnp.minimum(row[:, over] - col[at], 0.0))
                p_high, p_low = split(st_ref[at, over] * decay)
                first = mm(p_high, right[over])
                done.append(first[:, :128] + first[:, 128:] + mm(p_low, dy_high[over]))
                outer = mm_nt(x_both[at], twice[over]) + mm_nt(x_high[at], dy_low[over])
                acc[at, over] += outer * decay
            both.append(jnp.concatenate(done, axis=0))
        dx_ref[:, here] = jnp.where(lane < HEAD_DIM, both[0], both[1])

    if not ends:
        return

    @pl.when(step == pl.num_programs(0) - 1)
    def _():
        dbc_ref = ends[0]
        doc_col = m_ref[:, CONV_K : CONV_K + 1]
        ds = split(acc[...] * same_mask(doc_ref[0:1], doc_col, True))
        dbc_ref[:, :STATE] = three(mm, ds, split(bc_ref[:, STATE:]))
        dbc_ref[:, STATE:] = three(mm_tn, ds, split(bc_ref[:, :STATE]))


def carry_body(
    first, dx_ref, x_ref, dy_ref, pre_ref, in_ref, w_ref, m_ref, bc_ref, r_ref, end_ref, wl_ref, dt_ref,
    skip_ref, db_in, g_in, flow_in, *refs,
):
    extra = refs[:-6]
    d_ref, edge_ref, conv_ref, db_ref, g_ref, flow_ref = refs[-6:]
    if extra:
        pre_bc, in_bc, w_bc, dbc_ref, dc_ref, shifted_ref, rate_ref, q_ref, heads_ref = extra
    step = pl.program_id(0)
    count = INNER // 2 // BLOCK

    @pl.when(step == 0)
    def _():
        db_ref[...] = db_in[...]
        g_ref[...] = g_in[...]
        flow_ref[...] = flow_in[...]

    def conv(d_act, pre, inputs, weight, width):
        sig = sigmoid(pre)
        d_pre = d_act * (sig * (1.0 + pre * (1.0 - sig)))
        d_ext, sums = conv_back(d_pre, inputs, weight, m_ref[...])
        d_ref[:, :width] = d_ext[LEAD:].astype(BF)
        edge_ref[:LEAD, :width] = d_ext[:LEAD]
        edge_ref[LEAD:, :width] = d_ext[d_ext.shape[0] - LEAD :]
        conv_ref[:, :width] = sums

    @pl.when(step < count)
    def _():
        places = head_of_lane((step + first) * BLOCK_HEADS, BLOCK)
        returned = r_ref[0]
        r_parts = split(returned)
        to_end = expand(wl_ref[...], places)
        steps = expand(dt_ref[...], places)
        x = x_ref[...]
        d_scaled = dx_ref[...] + to_end * three(mm, split(bc_ref[:, :STATE]), r_parts)
        g_ref[...] += fold(x * d_scaled, places)
        db_ref[...] += three(mm_nt, split(to_end * steps * x), r_parts)
        flow = jnp.sum(returned * end_ref[0], axis=0, keepdims=True)
        high, middle, low = parts_of(jnp.broadcast_to(flow, (8, BLOCK)))
        flow_ref[...] += mm_nt(high, places) + mm_nt(middle, places) + mm_nt(low, places)
        d_x = steps * d_scaled + skip_ref[...] * dy_ref[...]
        conv(d_x, pre_ref[...], in_ref[...].astype(F32), w_ref[...], BLOCK)

    if not extra:
        return

    @pl.when(step == count)
    def _():
        width = 2 * STATE
        d_bc = jnp.concatenate([dbc_ref[:, :STATE] + db_ref[...], dbc_ref[:, STATE:] + dc_ref[...]], axis=1)
        conv(d_bc, pre_bc[...], in_bc[...].astype(F32), w_bc[...], width)
        masks = m_ref[...]
        steps, rate, shifted = dt_ref[...], rate_ref[...], shifted_ref[...]
        difference = q_ref[...] - steps * g_ref[...]
        d_log = (flow_ref[0:1] + running_sum(difference, True)) * masks[:, CONV_K - 2 : CONV_K - 1]
        d_steps = g_ref[...] - rate * d_log
        d_dt = d_steps * sigmoid(shifted)
        head = lax.broadcasted_iota(jnp.int32, d_dt.shape, 1) < HEADS
        d_dt = jnp.where(head, d_dt, 0.0)
        d_ref[:, width : width + STATE] = d_dt.astype(BF)
        edge_ref[:LEAD, width : width + STATE] = jnp.zeros((LEAD, STATE), F32)
        edge_ref[LEAD:, width : width + STATE] = d_dt[d_dt.shape[0] - LEAD :]
        conv_ref[:, width : width + STATE] = jnp.zeros((8, STATE), F32)
        heads_ref[0:8] = jnp.broadcast_to(jnp.sum(d_dt, axis=0, keepdims=True), (8, STATE))
        log_sum = -jnp.sum(steps * rate * d_log, axis=0, keepdims=True)
        heads_ref[8:16] = jnp.broadcast_to(log_sum, (8, STATE))


def woven(ref, devices, rows):
    pieces = [ref[side, d * rows : d * rows + rows, :] for d in range(devices) for side in range(2)]
    return jnp.concatenate(pieces, axis=0)


def d_final_body(devices, rows, g_ref, w_ref, o_ref):
    o_ref[...] = mm_nt(g_ref[...], woven(w_ref, devices, rows))


def layer_body(devices, rows, f_ref, w_ref, t_ref, o_ref, total):
    @pl.when(pl.program_id(0) == 0)
    def _():
        total[...] = t_ref[...].astype(F32)

    total[...] += mm(f_ref[...], woven(w_ref, devices, rows))

    @pl.when(pl.program_id(0) == pl.num_programs(0) - 1)
    def _():
        o_ref[...] = total[...].astype(BF)


def back_z_body(d_ref, w_ref, o_ref):
    half = w_ref.shape[2]
    o_ref[...] = mm_nt(d_ref[:, :half], w_ref[0]) + mm_nt(d_ref[:, half:], w_ref[1])


def back_x_body(da_ref, db_ref, w_ref, part_ref, o_ref):
    half = da_ref.shape[1]
    o_ref[...] = part_ref[...] + mm_nt(da_ref[...], w_ref[:, :half]) + mm_nt(db_ref[...], w_ref[:, half:])


def back_norm_body(d_ref, x_ref, og_ref, gain_ref, o_ref, sum_ref):
    @pl.when(pl.program_id(0) == 0)
    def _():
        sum_ref[...] = jnp.zeros_like(sum_ref)

    d_normed = d_ref[...]
    x = x_ref[...].astype(F32)
    scale = lax.rsqrt(jnp.mean(x * x, axis=-1, keepdims=True) + EPS)
    unit = x * scale
    pulled = d_normed * gain_ref[...]
    inner = jnp.mean(pulled * unit, axis=-1, keepdims=True)
    o_ref[...] = og_ref[...].astype(F32) + scale * (pulled - unit * inner)
    total = jnp.sum(d_normed * unit, axis=0, keepdims=True)
    sum_ref[...] += jnp.broadcast_to(total, sum_ref.shape)


def swap(array, axis):
    return lax.ppermute(array, axis, [(0, 1), (1, 0)])


def from_behind(array, by):
    peers = lax.axis_size(CTX[0]) * lax.axis_size(CTX[1])
    pairs = [(i, i + by) for i in range(peers) if 0 <= i + by < peers]
    return lax.ppermute(array, CTX, pairs)


def entering(state, decay, reverse, fills):
    fills = list(fills)

    def meanwhile(sent, arrived):
        return tie(arrived, *fills.pop(0)(sent)) if fills else arrived

    depth, width = lax.axis_size("z"), lax.axis_size("y")
    place_z, place_y = lax.axis_index("z"), lax.axis_index("y")
    if width != 2:
        gathered = lax.all_gather(jnp.concatenate([state, decay], axis=1), CTX)
        while fills:
            gathered = meanwhile(state, gathered)
        count = depth * width
        place = place_z * width + place_y
        ahead = count - 1 - place if reverse else place

        def one(lap, running):
            source = count - 1 - lap if reverse else lap
            item = lax.dynamic_index_in_dim(gathered, source, 0, False)
            return item[:, STATE : STATE + 1] * running + item[:, :STATE]

        return lax.fori_loop(0, ahead, one, jnp.zeros_like(state))
    second = place_y == (0 if reverse else 1)
    sent = pick(state, 1 - place_y)
    got = meanwhile(sent, swap(sent, "y"))
    own = pick(state, place_y)
    decay_own = pick(decay, place_y)[:1]
    decay_got = swap(pick(decay, 1 - place_y), "y")[:1]
    early = jnp.where(second, got, own)
    late = jnp.where(second, own, got)
    decay_early = jnp.where(second, decay_got, decay_own)
    decay_late = jnp.where(second, decay_own, decay_got)
    total = decay_late * early + late
    decay_total = decay_early * decay_late
    before = jnp.zeros_like(total)
    sent = total
    turn = depth - 1 - place_z if reverse else place_z
    for hop in range(1, depth):
        pairs = [(depth - hop, depth - 1 - hop)] if reverse else [(hop - 1, hop)]
        arrived = meanwhile(sent, lax.ppermute(sent, "z", pairs))
        before = jnp.where(turn == hop, arrived, before)
        sent = decay_total * before + total
    middle = decay_early * before + early
    mine = jnp.where(second, middle, before)
    sent = jnp.where(second, before, middle)
    theirs = swap(sent, "y")
    while fills:
        theirs = meanwhile(sent, theirs)
    return in_order(mine, theirs, "y")


def pick(parts, index, dim=0):
    return lax.dynamic_index_in_dim(parts, index, dim, False)


def in_order(mine, theirs, axis):
    first = lax.axis_index(axis) == 0
    return jnp.where(first, jnp.stack([mine, theirs]), jnp.stack([theirs, mine]))


def across(array, axis, by):
    return lax.ppermute(array, axis, [(i, i ^ by) for i in range(lax.axis_size(axis))])


def products_body(
    patched, place_ref, sent_own, kept_own, sent_other, kept_other, own_ref, other_ref, *refs
):
    sent_ref, kept_ref = refs[-2:]
    own, other = own_ref[...], other_ref[...]
    if patched:
        upto = own.shape[0] - LEAD
        own = jnp.concatenate([own[:upto], refs[0][...]], axis=0)
        other = jnp.concatenate([other[:upto], refs[1][...]], axis=0)

    def product(first, second):
        first, second = first[...], second[...]
        first = first.reshape(-1, first.shape[-1])
        second = second.reshape(-1, second.shape[-1])
        return mm(first, own) + mm(second, other)

    sent_ref[...] = product(sent_own, sent_other).astype(BF)
    kept_ref[...] = product(kept_own, kept_other)


def products(left, right, start, count, axis, waits):
    own, other = left
    sizes = [lax.axis_size(a) for a in ("x", "z", "y")]
    tokens = own.shape[1]
    rows = other.shape[0] // sizes[0] // sizes[1] // sizes[2]
    out_rows = other.shape[0] // 2
    places = jnp.stack([lax.axis_index(a) for a in ("core", "x", "y")])
    if axis == "x":
        own = own.reshape(2, 2, out_rows, tokens)
        other = other.reshape(2, out_rows, tokens)
        own_block, other_block = (1, 1, out_rows, tokens), (1, out_rows, tokens)

        def spec(mine, flip):
            if mine:
                return pl.BlockSpec(own_block, lambda g, p: (p[1] ^ flip, p[0], 0, 0))
            return pl.BlockSpec(other_block, lambda g, p: (p[1] ^ flip, 0, 0))
    else:
        own = own.reshape(2, 2, sizes[1], 2, rows, tokens)
        other = other.reshape(2 * sizes[1], 2, rows, tokens)
        own_block = (2, 1, sizes[1], 1, rows, tokens)
        other_block = (2 * sizes[1], 1, rows, tokens)

        def spec(mine, flip):
            if mine:
                return pl.BlockSpec(own_block, lambda g, p: (0, p[0], 0, p[2] ^ flip, 0, 0))
            return pl.BlockSpec(other_block, lambda g, p: (0, p[2] ^ flip, 0, 0))

    block = 384 if count % 384 == 0 else 512
    first = start // block
    columns_of = pl.BlockSpec((tokens, block), lambda g, p: (0, g + first))
    edge_of = pl.BlockSpec((LEAD, block), lambda g, p: (0, g + first))
    result = pl.BlockSpec((out_rows, block), lambda g, p: (0, g))
    return call(
        functools.partial(products_body, len(right) > 2), -(-count // block), count * out_rows / 2.0e5,
        [
            (own, spec(True, 1)), (own, spec(True, 0)), (other, spec(False, 1)), (other, spec(False, 0)),
            (right[0], columns_of), (right[1], columns_of),
            *[(edge, edge_of) for edge in right[2:]],
        ],
        [(out((out_rows, count), BF), result), (out((out_rows, count)), result)],
        waits=waits,
        places=places,
    )


def products_any(left, right, start, count, axis):
    core, place = lax.axis_index("core"), lax.axis_index(axis)
    sizes = [lax.axis_size(a) for a in ("x", "z", "y")]
    own = core_rows(left[0], core).reshape(left[1].shape)
    both = jnp.concatenate([own, left[1]], axis=1)
    view = both.reshape(*sizes, -1, both.shape[1])
    if axis == "y":
        view = jnp.moveaxis(view, 2, 0)
    view = view.reshape(view.shape[0], -1, both.shape[1])
    if len(right) > 2:
        upto = right[0].shape[0] - LEAD
        right = [right[0][:upto], right[2], right[1][:upto], right[3]]
    right = jnp.concatenate(right, axis=0)[:, start : start + count]
    sent = [mm(pick(view, place ^ by), right).astype(BF) for by in range(1, view.shape[0])]
    return sent, mm(pick(view, place), right)


def total_of(kept, got):
    for piece in got:
        kept = kept + piece.astype(F32)
    return kept


def tied(value, others):
    return tie(value, *others) if others else value


def xor_parts(parts, axis):
    count, place = lax.axis_size(axis), lax.axis_index(axis)
    return pick(parts, place), [pick(parts, place ^ by).astype(BF) for by in range(1, count)]


def travel(sent, axis, others):
    return [across(tied(piece, others), axis, by + 1) for by, piece in enumerate(sent)]


def places_here():
    return jnp.stack([lax.axis_index(a) for a in ("core", "x", "y")])


def second_body(place_ref, *refs):
    for side in range(2):
        kept_own, got_own, kept_next, got_next = refs[4 * side : 4 * side + 4]
        own_ref, next_ref = refs[8 + 2 * side : 10 + 2 * side]
        own_ref[...] = (kept_own[...] + got_own[...].astype(F32)).reshape(own_ref.shape)
        next_ref[...] = (kept_next[...] + got_next[...].astype(F32)).reshape(next_ref.shape).astype(BF)


def second_stage(kept_x, got_x, kept_y, got_y, depth, waits):
    rows = kept_x.shape[0] // (2 * depth)
    ins, outs = [], []
    for kept, got, by_y in ((kept_x, got_x, True), (kept_y, got_y, False)):
        width = kept.shape[1]
        shape = (depth, 2, rows, width) if by_y else (2, depth, rows, width)

        def spec(flip, by_y=by_y, width=width):
            if by_y:
                return pl.BlockSpec((1, 1, rows, width), lambda g, p: (g, p[2] ^ flip, 0, 0))
            return pl.BlockSpec((1, 1, rows, width), lambda g, p: (p[1] ^ flip, g, 0, 0))

        for flip in (0, 1):
            ins += [(kept.reshape(shape), spec(flip)), (got.reshape(shape), spec(flip))]
        result = pl.BlockSpec((1, rows, width), lambda g, p: (g, 0, 0))
        outs += [(out((depth, rows, width)), result), (out((depth, rows, width), BF), result)]
    return call(second_body, depth, 3, ins, outs, waits=waits, places=places_here())


def third_body(own_x, came_x, own_y, came_y, o_ref):
    width = own_x.shape[2]
    o_ref[:, :, :width] = (own_x[...] + came_x[...].astype(F32)).astype(o_ref.dtype)
    o_ref[:, :, width:] = (own_y[...] + came_y[...].astype(F32)).astype(o_ref.dtype)


def third_stage(own_x, came_x, own_y, came_y, kind, waits):
    depth, rows, wide_x = own_x.shape
    wide_y = own_y.shape[2]

    def spec(width):
        return pl.BlockSpec((1, rows, width), lambda g: (g, 0, 0))

    return call(
        third_body, depth, 2,
        [(own_x, spec(wide_x)), (came_x, spec(wide_x)), (own_y, spec(wide_y)), (came_y, spec(wide_y))],
        [(out((depth, rows, wide_x + wide_y), kind), spec(wide_x + wide_y))],
        waits=waits,
    )[0]


class Reduction:
    def __init__(self, left, right, start, middle, end, waits=()):
        if lax.axis_size("x") == 2 and lax.axis_size("y") == 2:
            sent_x, self.kept_x = products(left, right, start, middle - start, "x", waits)
            sent_y, self.kept_y = products(left, right, middle, end - middle, "y", waits)
            self.sent_x, self.sent_y = [sent_x], [sent_y]
        else:
            self.sent_x, self.kept_x = products_any(left, right, start, middle - start, "x")
            self.sent_y, self.kept_y = products_any(left, right, middle, end - middle, "y")

    def made(self):
        return [self.kept_x, self.kept_y, *self.sent_x, *self.sent_y]

    def launch(self, *others):
        self.got_x = travel(self.sent_x, "x", others)
        self.got_y = travel(self.sent_y, "y", others)

    def second(self, *others):
        sizes = [lax.axis_size(a) for a in ("x", "z", "y")]
        self.pairs = sizes[0] == 2 and sizes[2] == 2
        if self.pairs:
            self.own_x, next_x, self.own_y, next_y = second_stage(
                self.kept_x, self.got_x[0], self.kept_y, self.got_y[0], sizes[1], others
            )
            self.next_x, self.next_y = [next_x], [next_y]
            self.came_x = travel(self.next_x, "y", ())
            self.came_y = travel(self.next_y, "x", ())
            return
        part_x = total_of(tied(self.kept_x, others), self.got_x)
        part_y = total_of(tied(self.kept_y, others), self.got_y)
        view_x = part_x.reshape(sizes[1], sizes[2], -1, part_x.shape[1])
        view_y = part_y.reshape(sizes[0], sizes[1], -1, part_y.shape[1])
        self.own_x, self.next_x = xor_parts(jnp.moveaxis(view_x, 1, 0), "y")
        self.own_y, self.next_y = xor_parts(view_y, "x")
        self.came_x = travel(self.next_x, "y", ())
        self.came_y = travel(self.next_y, "x", ())

    def third(self, *others, kind=F32):
        place = lax.axis_index("z")
        if self.pairs:
            self.parts = third_stage(
                self.own_x, self.came_x[0], self.own_y, self.came_y[0], kind, others
            )
        else:
            done_x = total_of(tied(self.own_x, others), self.came_x)
            done_y = total_of(tied(self.own_y, others), self.came_y)
            self.parts = jnp.concatenate([done_x, done_y], axis=2).astype(kind)
        self.mine = None
        if kind == BF:
            sides = ((self.own_x, self.came_x), (self.own_y, self.came_y))
            self.mine = jnp.concatenate(
                [total_of(pick(own, place), [pick(c, place) for c in came]) for own, came in sides], axis=1
            )
        self.got_z = lax.all_to_all(self.parts, "z", 0, 0, tiled=True)

    def last(self, *others):
        got = tied(self.got_z, others)
        if self.mine is None:
            return jnp.sum(got, axis=0)
        others_only = lax.broadcasted_iota(jnp.int32, got.shape, 0) != lax.axis_index("z")
        return self.mine + jnp.sum(jnp.where(others_only, got.astype(F32), 0.0), axis=0)


def core_rows(turned, core):
    view = turned.reshape(lax.axis_size("x"), 2, -1, turned.shape[1])
    return pick(view, core, 1)


def both_cores(turned, core):
    theirs = core_rows(turned, 1 - core)
    return turned, swap(theirs.reshape(-1, turned.shape[1]), "core")


def document_ids(lengths, positions):
    first_end = lengths[0]
    second_end = lengths[0] + lengths[1]
    inside = (positions >= first_end).astype(jnp.int32) + (positions >= second_end).astype(jnp.int32)
    return jnp.where(positions < 0, -1, inside)


def gather_small(pieces, count):
    flat = jnp.concatenate([piece.reshape(-1) for piece in pieces])
    spread = jnp.broadcast_to(flat[None], (count, flat.shape[0]))
    return lax.all_to_all(spread, EVERY, 0, 0, tiled=True)


def columns(array, width):
    return jnp.pad(array, ((0, 0), (0, width - array.shape[1])))


def shards(
    tokens, out_grad, seq_lengths, norm_gain, in_weight, conv_weight, conv_bias,
    dt_bias, a_log, skip_gain, gated_gain, out_weight,
):
    count = 1
    for axis in EVERY:
        count *= lax.axis_size(axis)
    core = lax.axis_index("core")
    place = lax.axis_index("z") * lax.axis_size("y") + lax.axis_index("y")
    row_count, width = tokens.shape
    first_row = place * row_count
    full_rows = LEAD + row_count
    half = INNER // 2
    bc_width = CONVW - INNER
    square = (row_count, row_count)

    lead_tokens = from_behind(tokens[row_count - LEAD :], 1)
    small = gather_small([norm_gain, conv_weight, conv_bias, gated_gain], count)
    weight_x = lax.all_gather(columns(in_weight[:, INNER:], PROJ_X), EVERY, axis=0, tiled=True)
    rows_out = out_weight.shape[0] // 2
    stacked = jnp.stack(
        [in_weight[:, :half], in_weight[:, half:INNER], out_weight[:rows_out], out_weight[rows_out:]]
    )
    stacked = lax.all_gather(stacked, EVERY, axis=1, tiled=True)
    cuts = [norm_gain.size, conv_weight.size, conv_bias.size]
    cuts = [sum(cuts[: i + 1]) for i in range(3)]
    gain_piece, conv_piece, bias_piece, gated_piece = jnp.split(small, cuts, axis=1)
    full_gain = gain_piece.reshape(1, -1).astype(F32)
    full_conv = jnp.moveaxis(conv_piece.reshape(count, CONV_K, -1), 1, 0).reshape(CONV_K, -1)
    full_conv = jnp.pad(full_conv.astype(F32), ((0, 4), (0, 0)))
    full_bias = bias_piece.reshape(1, -1).astype(F32)
    full_gated = gated_piece.reshape(1, -1).astype(F32)

    normed_ext, turned = call(
        norm_body, 1, 4,
        [
            (lead_tokens, whole(LEAD, width)),
            (tokens, whole(row_count, width)),
            (full_gain, whole(1, width)),
        ],
        [
            (out((full_rows, width), BF), whole(full_rows, width)),
            (out((width, row_count), BF), whole(width, row_count)),
        ],
    )
    normed = normed_ext[LEAD:]
    normed_left = both_cores(turned, core)
    out_grad_theirs = swap(out_grad, "core")

    lengths = seq_lengths[0]
    ordinal = jnp.arange(row_count, dtype=jnp.int32)
    doc_ids = document_ids(lengths, first_row + ordinal)
    doc_before = document_ids(lengths, first_row - 1 + jnp.zeros((1,), jnp.int32))
    marks = [
        document_ids(lengths, first_row + ordinal - (CONV_K - 1 - tap)) == doc_ids
        for tap in range(CONV_K)
    ]
    marks = marks + [doc_ids, doc_ids == doc_before[0], doc_ids == doc_ids[row_count - 1]]
    masks = columns(jnp.stack([mark.astype(F32) for mark in marks], axis=1), 128)
    doc_rows = jnp.broadcast_to(doc_ids.astype(F32)[None], (8, row_count))
    rate = columns(jnp.exp(a_log)[None], 128)
    shift = columns(dt_bias[None], 128)
    skip_wide = jnp.repeat(skip_gain, HEAD_DIM)[None]
    mixed_x = mm(normed_ext, weight_x).astype(BF)

    block_bc = pl.BlockSpec((full_rows, bc_width), lambda g: (0, INNER // bc_width))
    block_dr = pl.BlockSpec((full_rows, 128), lambda g: (0, CONVW // 128))
    per_token = whole(row_count, 128)
    a_token = (out((row_count, 128)), per_token)
    pre_bc, act_bc, act_t, scores, scores_t, steps, enter, to_end, cumulative, cum_turned, shifted = call(
        prep_bc_body, 1, 6,
        [
            (mixed_x, block_bc),
            (mixed_x, block_dr),
            (full_conv[:, INNER:], whole(8, bc_width)),
            (full_bias[:, INNER:], whole(1, bc_width)),
            (masks, per_token),
            (doc_rows, whole(8, row_count)),
            (shift, whole(1, 128)),
            (rate, whole(1, 128)),
        ],
        [
            (out((row_count, bc_width)), whole(row_count, bc_width)),
            (out((row_count, bc_width)), whole(row_count, bc_width)),
            (out((bc_width, row_count)), whole(bc_width, row_count)),
            (out(square), whole(*square)),
            (out(square), whole(*square)),
            a_token, a_token, a_token, a_token,
            (out((128, row_count)), whole(128, row_count)),
            a_token,
        ],
    )
    pre_x, act_x, state_local, device_decay = call(
        prep_x_body, INNER // BLOCK, 12,
        [
            (mixed_x, lanes(full_rows, BLOCK)),
            (full_conv[:, :INNER], lanes(8, BLOCK)),
            (full_bias[:, :INNER], lanes(1, BLOCK)),
            (masks, per_token),
            (to_end, per_token),
            (steps, per_token),
            (enter, per_token),
            (act_t, whole(bc_width, row_count)),
        ],
        [
            (out((row_count, INNER)), lanes(row_count, BLOCK)),
            (out((row_count, INNER)), lanes(row_count, BLOCK)),
            (out((2, STATE, half)), halves(STATE, BLOCK)),
            (out((2, 8, half)), halves(8, BLOCK)),
        ],
    )

    heads_block = 2 * PAIRS
    groups = HEADS // heads_block
    half_groups = groups // 2
    cum_rows = cum_turned[:HEADS].reshape(groups, heads_block, row_count)
    kept = {}

    def pairs_at(index):
        return pl.BlockSpec((row_count, PAIR_LANES), lambda g: (0, g + index * half_groups))

    def cums_at(index):
        return pl.BlockSpec((1, heads_block, row_count), lambda g: (g + index * half_groups, 0, 0))

    def intra(index, wait):
        kept[index] = call(
            functools.partial(intra_body, index * half_groups), half_groups, 12,
            [
                (act_x, pairs_at(index)),
                (steps, per_token),
                (skip_wide, pl.BlockSpec((1, PAIR_LANES), lambda g: (0, g + index * half_groups))),
                (scores, whole(*square)),
                (cumulative, per_token),
                (cum_rows, cums_at(index)),
            ],
            [(out((row_count, half)), lanes(row_count, PAIR_LANES))],
            waits=[wait],
        )[0]
        return [kept[index]]

    devices = 4
    out_block = 2 * devices * rows_out
    out_blocks = count // devices
    weight_block = pl.BlockSpec((2, devices * rows_out, width), lambda g: (1, g, 0))
    direct = rows_out % 16 == 0

    def project_z(wait):
        kept["mixed_z"] = [mm(normed, stacked[side]).astype(BF) for side in range(2)]
        return kept["mixed_z"]

    def project(wait):
        if direct:
            kept["d_final"] = call(
                functools.partial(d_final_body, devices, rows_out), out_blocks, 7,
                [(out_grad, whole(row_count, width)), (stacked, weight_block)],
                [(out((row_count, INNER)), lanes(row_count, out_block))],
                waits=[wait],
            )[0]
        else:
            weight_o = jnp.moveaxis(stacked[2:].reshape(2, count, rows_out, width), 0, 1)
            kept["weight_o"] = weight_o.reshape(-1, width)
            kept["d_final"] = mm_nt(out_grad, kept["weight_o"])
        return [kept["d_final"]]

    state_in = entering(
        state_local, device_decay, False,
        [
            lambda wait: intra(0, wait), lambda wait: intra(1, wait), lambda wait: [], project_z,
            project,
        ],
    )
    state_end = device_decay[:, :1] * state_in + state_local

    tile = 128
    final, final_turned, d_z, d_y, returned_local, d_c_carry, dy_y, sums = call(
        gate_body, row_count // tile, 31,
        [
            (kept[0], rows_of(tile, half)),
            (kept[1], rows_of(tile, half)),
            (kept["mixed_z"][0], rows_of(tile, half)),
            (kept["mixed_z"][1], rows_of(tile, half)),
            (kept["d_final"], rows_of(tile, INNER)),
            (act_x, rows_of(tile, INNER)),
            (act_bc[:, STATE:], rows_of(tile, STATE)),
            (act_t[STATE:], lanes(STATE, tile)),
            (state_in, whole(2, STATE, half)),
            (enter, rows_of(tile, 128)),
            (full_gated, whole(1, INNER)),
            (skip_wide, whole(1, INNER)),
        ],
        [
            (out((row_count, INNER), BF), rows_of(tile, INNER)),
            (out((INNER, row_count), BF), lanes(INNER, tile)),
            (out((row_count, INNER), BF), rows_of(tile, INNER)),
            (out((row_count, INNER)), rows_of(tile, INNER)),
            (out((2, STATE, half)), whole(2, STATE, half)),
            (out((row_count, STATE)), rows_of(tile, STATE)),
            (out((row_count, 128)), rows_of(tile, 128)),
            (out((16, INNER)), whole(16, INNER)),
        ],
        [pltpu.VMEM((tile, INNER), F32), pltpu.VMEM((tile, INNER), F32)],
    )

    final_left = both_cores(final_turned, core)
    d_z_theirs = swap(d_z, "core")
    back = {"acc": jnp.zeros(square, F32)}

    def out_sums(wait):
        back["out"] = Reduction(final_left, [out_grad, out_grad_theirs], 0, width // 2, width, [wait])
        back["out"].launch()
        return back["out"].made()

    def z_sums(wait):
        back["z"] = Reduction(normed_left, [d_z, d_z_theirs], 0, half, INNER, [wait])
        back["z"].launch()
        return back["z"].made()

    def within(index, wait):
        ends = [(out((row_count, bc_width)), whole(row_count, bc_width))] if index else []
        back[index], back["acc"], *back["bc"] = call(
            functools.partial(back_body, index * half_groups), half_groups, 18,
            [
                (act_x, pairs_at(index)),
                (d_y, pairs_at(index)),
                (steps, per_token),
                (scores_t, whole(*square)),
                (cumulative, per_token),
                (cum_rows, cums_at(index)),
                (act_bc, whole(row_count, bc_width)),
                (doc_rows, whole(8, row_count)),
                (masks, per_token),
                (back["acc"], whole(*square)),
            ],
            [
                (out((row_count, half)), lanes(row_count, PAIR_LANES)),
                (out(square), whole(*square)),
                *ends,
            ],
            waits=[wait],
        )
        return [back[index]]

    def first_within(wait):
        back["z"].second(wait)
        return within(0, wait)

    def second_within(wait):
        return within(1, wait)

    norm_block = 256

    def send_out(wait):
        back["out"].second(wait)
        back["z"].third(wait)
        return [back["z"].parts, *back["out"].next_x, *back["out"].next_y]

    returned = entering(
        returned_local, device_decay, True,
        [z_sums, out_sums, first_within, second_within, send_out],
    )

    blocks = half // BLOCK

    def carried(index, earlier, extra, extra_out, waits):
        steps_count = blocks + len(extra_out)
        own = pl.BlockSpec((row_count, BLOCK), lambda g: (0, jnp.minimum(g, blocks - 1)))

        def at(rows):
            return pl.BlockSpec((rows, BLOCK), lambda g: (0, jnp.minimum(g, blocks - 1) + index * blocks))

        state_at = pl.BlockSpec((1, STATE, BLOCK), lambda g: (index, 0, jnp.minimum(g, blocks - 1)))
        wide = half + len(extra_out) * (PROJ_X - INNER)
        return call(
            functools.partial(carry_body, index * blocks), steps_count, 14 + 4 * index,
            [
                (back[index], own),
                (act_x, at(row_count)),
                (d_y, at(row_count)),
                (pre_x, at(row_count)),
                (mixed_x, at(full_rows)),
                (full_conv[:, :INNER], at(8)),
                (masks, per_token),
                (act_bc, whole(row_count, bc_width)),
                (returned, state_at),
                (state_end, state_at),
                (to_end, per_token),
                (steps, per_token),
                (skip_wide, at(1)),
                *[(array, whole(*array.shape)) for array in earlier],
                *extra,
            ],
            [
                *extra_out,
                (out((row_count, wide), BF), lanes(row_count, BLOCK)),
                (out((2 * LEAD, wide)), lanes(2 * LEAD, BLOCK)),
                (out((8, wide)), lanes(8, BLOCK)),
                (out((row_count, STATE)), whole(row_count, STATE)),
                a_token,
                (out((8, 128)), whole(8, 128)),
            ],
            waits=waits,
        )

    none = jnp.zeros((row_count, 128), F32)
    d_xa, edge_a, conv_a, *so_far = carried(0, [none, none, none[:8]], [], [], [])
    back["out"].third(edge_a)
    d_xa_theirs = swap(d_xa, "core")
    halo_a = from_behind(edge_a[:LEAD], -1)
    last_a = (edge_a[LEAD:] + halo_a).astype(BF)
    last_a_theirs = swap(last_a, "core")
    sums_a = Reduction(normed_left, [d_xa, d_xa_theirs, last_a, last_a_theirs], 0, half // 2, half, [back["out"].parts, back["z"].got_z])
    sums_a.launch()
    heads, d_xb, edge_b, conv_b, *_ = carried(
        1, so_far,
        [
            (pre_bc, whole(row_count, bc_width)),
            (mixed_x, block_bc),
            (full_conv[:, INNER:], whole(8, bc_width)),
            (back["bc"][0], whole(row_count, bc_width)),
            (d_c_carry, whole(row_count, STATE)),
            (shifted, per_token),
            (rate, whole(1, 128)),
            (dy_y, per_token),
        ],
        [(out((16, 128)), whole(16, 128))],
        sums_a.made(),
    )
    d_xb_theirs = swap(d_xb, "core")
    halo_b = from_behind(edge_b[:LEAD], -1)
    sums_a.second(edge_b)
    sums_a.third()
    d_normed_z = call(
        back_z_body, width // norm_block, 10,
        [
            (d_z, whole(row_count, INNER)),
            (stacked, pl.BlockSpec((2, norm_block, half), lambda g: (0, g, 0))),
        ],
        [(out((row_count, width)), lanes(row_count, norm_block))],
        waits=[edge_b],
    )[0]
    last_b = (edge_b[LEAD:] + tie(halo_b, d_normed_z)).astype(BF)
    last_b_theirs = swap(last_b, "core")
    wide_b = d_xb.shape[1]
    sums_b = Reduction(
        normed_left, [d_xb, d_xb_theirs, last_b, last_b_theirs], 0, 1024, wide_b, [sums_a.parts]
    )
    sums_b.launch()

    d_xa = lax.dynamic_update_slice(d_xa, last_a, (row_count - LEAD, 0))
    d_xb = lax.dynamic_update_slice(d_xb, last_b, (row_count - LEAD, 0))
    d_normed = call(
        back_x_body, width // norm_block, 10,
        [
            (d_xa, whole(row_count, half)),
            (d_xb, whole(row_count, wide_b)),
            (weight_x, rows_of(norm_block, PROJ_X)),
            (d_normed_z, lanes(row_count, norm_block)),
        ],
        [(out((row_count, width)), lanes(row_count, norm_block))],
        waits=sums_b.made(),
    )[0]
    grad_tokens, gain_sums = call(
        back_norm_body, row_count // tile, 4,
        [
            (d_normed, rows_of(tile, width)),
            (tokens, rows_of(tile, width)),
            (out_grad, rows_of(tile, width)),
            (full_gain, whole(1, width)),
        ],
        [
            (out((row_count, width)), rows_of(tile, width)),
            (out((8, width)), whole(8, width)),
        ],
    )
    sums_b.second(grad_tokens)
    if direct:
        layer_out = call(
            functools.partial(layer_body, devices, rows_out), out_blocks, 13,
            [
                (final, lanes(row_count, out_block)),
                (stacked, weight_block),
                (tokens, whole(row_count, width)),
            ],
            [(out((row_count, width), BF), whole(row_count, width))],
            [pltpu.VMEM((row_count, width), F32)],
            waits=[*sums_b.next_x, *sums_b.next_y],
        )[0]
    else:
        layer_out = (tokens.astype(F32) + mm(final, kept["weight_o"])).astype(BF)

    conv_sums = jnp.concatenate([conv_a, conv_b[:, : CONVW - half]], axis=1)
    grad_skip = jnp.sum(jnp.sum(sums[8:], axis=0).reshape(HEADS, HEAD_DIM), axis=1)
    grad_gated = jnp.sum(sums[:8], axis=0)
    per_device = jnp.concatenate(
        [
            gain_sums[0].reshape(count, -1),
            jnp.moveaxis(conv_sums[:CONV_K].reshape(CONV_K, count, -1), 1, 0).reshape(count, -1),
            conv_sums[CONV_K].reshape(count, -1),
            grad_gated.reshape(count, -1),
            jnp.broadcast_to(
                jnp.concatenate([heads[0, :HEADS], heads[8, :HEADS], grad_skip])[None],
                (count, 3 * HEADS),
            ),
        ],
        axis=1,
    )
    sums_b.third(kind=BF)
    per_device = tie(per_device, *sums_b.next_x, *sums_b.next_y)
    arrived = lax.all_to_all(per_device, EVERY, 0, 0, tiled=True)
    done = [layer_out]
    sum_out, sum_in_z, sum_in_a = [each.last(*done) for each in (back["out"], back["z"], sums_a)]
    sum_in_b = sums_b.last()
    small_sums = jnp.sum(tie(arrived, layer_out), axis=0)
    cuts = [norm_gain.size, conv_weight.size, conv_bias.size, gated_gain.size, HEADS, HEADS]
    cuts = [sum(cuts[: i + 1]) for i in range(6)]
    sum_gain, sum_conv, sum_bias, sum_gated, sum_dt, sum_log, sum_skip = jnp.split(small_sums, cuts)
    sum_in = jnp.concatenate([sum_in_z, sum_in_a, sum_in_b[:, : in_weight.shape[1] - INNER - half]], axis=1)
    return (
        layer_out,
        grad_tokens,
        sum_gain,
        sum_in,
        sum_conv.reshape(conv_weight.shape),
        sum_bias,
        sum_dt,
        sum_log,
        sum_skip,
        sum_gated,
        sum_out,
    )


def solution(mesh):
    x = mesh.shape["dp"] // 2
    y = x
    z = mesh.shape["ctx"] // y
    fine = Mesh(mesh.devices.reshape(x, 2, z, y), EVERY)
    rows = P(EVERY, None)
    flat = P(EVERY)
    in_specs = (
        rows, rows, P(("x", "core"), None), flat, rows, P(None, EVERY), flat,
        P(), P(), P(), flat, rows,
    )
    out_specs = (rows, rows, flat, rows, P(None, EVERY), flat, P(), P(), P(), flat, rows)
    return jax.shard_map(shards, mesh=fine, in_specs=in_specs, out_specs=out_specs, check_vma=False)
```

```python
import functools

import jax
import jax.numpy as jnp
from jax import lax
from jax.experimental import pallas as pl
from jax.experimental.pallas import tpu as pltpu
from jax.sharding import Mesh, PartitionSpec as P

HEADS = 48
HEAD_DIM = 64
STATE = 128
CONV_K = 4
INNER = 3072
CONVW = 3328
LEAD = 16
PROJ_X = 3456
BLOCK = 512
BLOCK_HEADS = BLOCK // HEAD_DIM
PAIRS = 3
PAIR_LANES = 128 * PAIRS
VMEM = 56 * 1024 * 1024
F32 = jnp.float32
BF = jnp.bfloat16
EPS = 1e-05
highest = lax.Precision.HIGHEST
EVERY = ("x", "core", "z", "y")
CTX = ("z", "y")


def params():
    return pltpu.CompilerParams(vmem_limit_bytes=VMEM, dimension_semantics=("arbitrary",))


def call(body, grid, micros, ins, outs, scratch=(), waits=(), places=None):
    first = (places is not None) + len(ins)
    anywhere = pl.BlockSpec(memory_space=pl.ANY)

    def run(*refs):
        body(*refs[:first], *refs[first + len(waits) :])

    scalars = [] if places is None else [places]
    return pl.pallas_call(
        run,
        grid_spec=pltpu.PrefetchScalarGridSpec(
            num_scalar_prefetch=len(scalars),
            grid=(grid,),
            in_specs=[spec for _, spec in ins] + [anywhere] * len(waits),
            out_specs=[spec for _, spec in outs],
            scratch_shapes=list(scratch),
        ),
        out_shape=[shape for shape, _ in outs],
        compiler_params=params(),
        cost_estimate=pl.CostEstimate(
            flops=int(micros * 1e9), bytes_accessed=int(micros * 3e6), transcendentals=0
        ),
    )(*scalars, *[array for array, _ in ins], *waits)


def tie(value, *others):
    def body(*refs):
        pass

    anywhere = pl.BlockSpec(memory_space=pl.ANY)
    return pl.pallas_call(
        body,
        in_specs=[anywhere] * (1 + len(others)),
        out_specs=anywhere,
        out_shape=jax.ShapeDtypeStruct(value.shape, value.dtype),
        input_output_aliases={0: 0},
    )(value, *others)


def whole(*shape):
    return pl.BlockSpec(shape, lambda g: (0,) * len(shape))


def lanes(rows, width):
    return pl.BlockSpec((rows, width), lambda g: (0, g))


def rows_of(count, width):
    return pl.BlockSpec((count, width), lambda g: (g, 0))


def halves(rows, width):
    count = INNER // 2 // width
    return pl.BlockSpec((1, rows, width), lambda g: (g // count, 0, g % count))


def group(rows, width):
    return pl.BlockSpec((1, rows, width), lambda g: (g, 0, 0))


def out(shape, dtype=F32):
    return jax.ShapeDtypeStruct(shape, dtype)


def split(value):
    high = value.astype(BF)
    return high, (value - high.astype(F32)).astype(BF)


def mm(left, right):
    return jnp.dot(left, right, preferred_element_type=F32)


def mm_nt(left, right):
    return lax.dot_general(left, right, (((1,), (1,)), ((), ())), preferred_element_type=F32)


def mm_tn(left, right):
    return lax.dot_general(left, right, (((0,), (0,)), ((), ())), preferred_element_type=F32)


def three(product, left, right):
    left_high, left_low = left
    right_high, right_low = right
    return (
        product(left_high, right_high)
        + product(left_high, right_low)
        + product(left_low, right_high)
    )


def head_of_lane(first, count):
    lane = lax.broadcasted_iota(jnp.int32, (STATE, count), 1) // HEAD_DIM + first
    row = lax.broadcasted_iota(jnp.int32, (STATE, count), 0)
    return (lane == row).astype(BF)


def expand(value, places):
    high, low = split(value)
    return mm(high, places) + mm(low, places)


def fold(value, places):
    high, low = split(value)
    return mm_nt(high, places) + mm_nt(low, places)


def sigmoid(value):
    return 1.0 / (1.0 + jnp.exp(-value))


def conv_pre(extended, weight, bias, masks):
    running = jnp.zeros((masks.shape[0], extended.shape[1]), F32) + bias
    for tap in range(CONV_K):
        shifted = extended if tap == CONV_K - 1 else pltpu.roll(extended, CONV_K - 1 - tap, 0)
        running = running + shifted[LEAD:] * weight[tap : tap + 1] * masks[:, tap : tap + 1]
    return running


def conv_back(d_pre, extended, weight, masks):
    zeros = jnp.zeros((LEAD, d_pre.shape[1]), F32)
    total = LEAD + d_pre.shape[0]
    d_ext = jnp.zeros((total, d_pre.shape[1]), F32)
    weight_rows = []
    for tap in range(CONV_K):
        by = CONV_K - 1 - tap
        part = d_pre * masks[:, tap : tap + 1]
        padded = jnp.concatenate([zeros, part], axis=0)
        shifted = extended
        if by:
            padded = pltpu.roll(padded, total - by, 0)
            shifted = pltpu.roll(extended, by, 0)
        d_ext = d_ext + padded * weight[tap : tap + 1]
        weight_rows.append(jnp.sum(shifted[LEAD:] * part, axis=0, keepdims=True))
    weight_rows.append(jnp.sum(d_pre, axis=0, keepdims=True))
    weight_rows.append(jnp.zeros((8 - len(weight_rows), d_pre.shape[1]), F32))
    return d_ext, jnp.concatenate(weight_rows, axis=0)


def same_mask(doc_row, doc_col, transposed):
    count = doc_row.shape[1]
    rows = lax.broadcasted_iota(jnp.int32, (count, count), 0)
    cols = lax.broadcasted_iota(jnp.int32, (count, count), 1)
    order = rows <= cols if transposed else rows >= cols
    return jnp.where((doc_row == doc_col) & order, 1.0, 0.0)


def norm_body(lead_ref, x_ref, gain_ref, normed_ref, turned_ref):
    def normed(value):
        scale = lax.rsqrt(jnp.mean(value * value, axis=-1, keepdims=True) + EPS)
        return value * scale * gain_ref[...]

    normed_ref[:LEAD] = normed(lead_ref[...].astype(F32)).astype(BF)
    for tile in range(x_ref.shape[0] // 128):
        here = slice(tile * 128, tile * 128 + 128)
        value = normed(x_ref[here].astype(F32))
        normed_ref[LEAD + tile * 128 : LEAD + tile * 128 + 128] = value.astype(BF)
        turned_ref[:, here] = value.T.astype(BF)


def parts_of(value):
    high, low = split(value)
    return high, low, (value - high.astype(F32) - low.astype(F32)).astype(BF)


def running_sum(value, transposed):
    count = value.shape[0]
    rows = lax.broadcasted_iota(jnp.int32, (count, count), 0)
    cols = lax.broadcasted_iota(jnp.int32, (count, count), 1)
    side = ((rows <= cols) if transposed else (rows >= cols)).astype(BF)
    high, middle, low = parts_of(value)
    return mm(side, high) + mm(side, middle) + mm(side, low)


def softplus(value):
    return jnp.maximum(value, 0.0) + jnp.log1p(jnp.exp(-jnp.abs(value)))


def prep_bc_body(
    x_ref, dr_ref, w_ref, b_ref, m_ref, doc_ref, shift_ref, rate_ref,
    pre_ref, act_ref, t_ref, s_ref, st_ref, steps_ref, enter_ref, to_end_ref, cum_ref, turned_ref, dt_ref,
):
    masks = m_ref[...]
    pre = conv_pre(x_ref[...].astype(F32), w_ref[...], b_ref[...], masks)
    act = pre * sigmoid(pre)
    pre_ref[...] = pre
    act_ref[...] = act
    t_ref[...] = act.T
    b_rows, c_rows = split(act[:, :STATE]), split(act[:, STATE:])
    doc_row, doc_col = doc_ref[0:1], masks[:, CONV_K : CONV_K + 1]
    s_ref[...] = three(mm_nt, c_rows, b_rows) * same_mask(doc_row, doc_col, False)
    st_ref[...] = three(mm_nt, b_rows, c_rows) * same_mask(doc_row, doc_col, True)
    shifted = dr_ref[LEAD:, :].astype(F32) + shift_ref[...]
    steps = softplus(shifted)
    cumulative = running_sum(-steps * rate_ref[...], False)
    last = cumulative[cumulative.shape[0] - 1 :]
    dt_ref[...] = shifted
    steps_ref[...] = steps
    enter_ref[...] = jnp.exp(cumulative) * masks[:, CONV_K + 1 : CONV_K + 2]
    to_end_ref[...] = jnp.exp(last - cumulative) * masks[:, CONV_K + 2 : CONV_K + 3]
    cum_ref[...] = cumulative
    turned_ref[...] = cumulative.T


def prep_x_body(
    x_ref, w_ref, b_ref, m_ref, wl_ref, dt_ref, e_ref, t_ref, pre_ref, act_ref, state_ref, decay_ref
):
    pre = conv_pre(x_ref[...].astype(F32), w_ref[...], b_ref[...], m_ref[...])
    act = pre * sigmoid(pre)
    pre_ref[...] = pre
    act_ref[...] = act
    places = head_of_lane(pl.program_id(0) * BLOCK_HEADS, BLOCK)
    weighted = split(act * expand(wl_ref[...] * dt_ref[...], places))
    state_ref[0] = three(mm, split(t_ref[:STATE]), weighted)
    last = e_ref[e_ref.shape[0] - 8 :]
    high, middle, low = parts_of(last)
    spread = mm(high, places) + mm(middle, places) + mm(low, places)
    decay_ref[0] = jnp.broadcast_to(spread[7:8], spread.shape)


def heads_here(cum_ref, first):
    back = STATE - (pl.program_id(0) + first) * 2 * PAIRS
    return pltpu.roll(cum_ref[...], jnp.where(back == STATE, 0, back), 1)


def intra_body(first, x_ref, dt_ref, skip_ref, s_ref, cum_ref, row_ref, y_ref):
    half = s_ref.shape[0] // 2
    places = head_of_lane((pl.program_id(0) + first) * 2 * PAIRS, PAIR_LANES)
    scaled = x_ref[...] * expand(dt_ref[...], places)
    cols = heads_here(cum_ref, first)
    lane = lax.broadcasted_iota(jnp.int32, (2 * half, 128), 1)
    for pair in range(PAIRS):
        here = slice(pair * 128, pair * 128 + 128)
        high, low = split(scaled[:, here])
        right = jnp.concatenate([high, low], axis=1)
        both = []
        for side in range(2):
            head = 2 * pair + side
            col = cols[:, head : head + 1]
            row = row_ref[0, head : head + 1, :]
            top = s_ref[:half, :half] * jnp.exp(jnp.minimum(col[:half] - row[:, :half], 0.0))
            low_part = s_ref[half:, :] * jnp.exp(jnp.minimum(col[half:] - row, 0.0))
            done = []
            for part, count in ((top, half), (low_part, 2 * half)):
                p_high, p_low = split(part)
                first = mm(p_high, right[:count])
                done.append(first[:, :128] + first[:, 128:] + mm(p_low, high[:count]))
            both.append(jnp.concatenate(done, axis=0))
        y_ref[:, here] = (
            jnp.where(lane < HEAD_DIM, both[0], both[1]) + skip_ref[:, here] * x_ref[:, here]
        )


def gate_body(
    ya_ref, yb_ref, za_ref, zb_ref, df_ref, x_ref, c_ref, ct_ref, state_ref, e_ref, gain_ref, skip_ref,
    final_ref, turned_ref, dz_ref, dy_ref, r_ref, dc_ref, q_ref, sums_ref, carry, scaled,
):
    @pl.when(pl.program_id(0) == 0)
    def _():
        r_ref[...] = jnp.zeros_like(r_ref)
        sums_ref[...] = jnp.zeros_like(sums_ref)

    e_high, e_low = split(e_ref[...])
    c_rows = split(c_ref[...])
    for block in range(INNER // BLOCK):
        here = slice(block * BLOCK, block * BLOCK + BLOCK)
        places = head_of_lane(block * BLOCK_HEADS, BLOCK)
        spread = mm(e_high, places) + mm(e_low, places)
        there = slice(block % 3 * BLOCK, block % 3 * BLOCK + BLOCK)
        carry[:, here] = three(mm, c_rows, split(state_ref[block // 3, :, there])) * spread
        scaled[:, here] = spread
    gain, skip = gain_ref[...], skip_ref[...]

    def some(lap, sums):
        at = pl.ds(pl.multiple_of(lap * 16, 16), 16)
        y = jnp.concatenate([ya_ref[at, :], yb_ref[at, :]], axis=1) + carry[at, :]
        z = jnp.concatenate([za_ref[at, :], zb_ref[at, :]], axis=1).astype(F32)
        sig = sigmoid(z)
        gate = z * sig
        gated = y * gate
        scale = lax.rsqrt(jnp.mean(gated * gated, axis=-1, keepdims=True) + EPS)
        unit = gated * scale
        final_ref[at, :] = (unit * gain).astype(BF)
        d_final = df_ref[at, :]
        q = d_final * gain
        inner = jnp.mean(q * unit, axis=-1, keepdims=True)
        d_gated = scale * (q - unit * inner)
        d_y = d_gated * gate
        dz_ref[at, :] = (d_gated * y * (sig * (1.0 + z * (1.0 - sig)))).astype(BF)
        dy_ref[at, :] = d_y
        x = x_ref[at, :]
        scaled[at, :] = scaled[at, :] * d_y
        carry[at, :] = d_y * (y - skip * x)
        d_gain, d_skip = d_final * unit, d_y * x
        return (
            sums[0] + d_gain[:8] + d_gain[8:],
            sums[1] + d_skip[:8] + d_skip[8:],
        )

    zero = jnp.zeros((8, INNER), F32)
    d_gain, d_skip = lax.fori_loop(0, za_ref.shape[0] // 16, some, (zero, zero))
    sums_ref[0:8] += d_gain
    sums_ref[8:16] += d_skip
    ct_rows = split(ct_ref[...])
    d_c = jnp.zeros(dc_ref.shape, F32)
    q_sum = jnp.zeros(q_ref.shape, F32)
    for block in range(INNER // BLOCK):
        here = slice(block * BLOCK, block * BLOCK + BLOCK)
        there = slice(block % 3 * BLOCK, block % 3 * BLOCK + BLOCK)
        piece = split(scaled[:, here])
        r_ref[block // 3, :, there] += three(mm, ct_rows, piece)
        d_c = d_c + three(mm_nt, piece, split(state_ref[block // 3, :, there]))
        turned_ref[here, :] = final_ref[:, here].T
        q_sum = q_sum + fold(carry[:, here], head_of_lane(block * BLOCK_HEADS, BLOCK))
    dc_ref[...] = d_c
    q_ref[...] = q_sum


def back_body(first, x_ref, dy_ref, dt_ref, st_ref, cum_ref, row_ref, bc_ref, doc_ref, m_ref, in_ref, dx_ref, acc, *ends):
    step = pl.program_id(0)
    half = st_ref.shape[0] // 2

    @pl.when(step == 0)
    def _():
        acc[...] = in_ref[...]

    places = head_of_lane((step + first) * 2 * PAIRS, PAIR_LANES)
    scaled = x_ref[...] * expand(dt_ref[...], places)
    cols = heads_here(cum_ref, first)
    lane = lax.broadcasted_iota(jnp.int32, (2 * half, 128), 1)
    for pair in range(PAIRS):
        here = slice(pair * 128, pair * 128 + 128)
        dy_high, dy_low = split(dy_ref[:, here])
        right = jnp.concatenate([dy_high, dy_low], axis=1)
        twice = jnp.concatenate([dy_high, dy_high], axis=1)
        both = []
        for side in range(2):
            head = 2 * pair + side
            mine = (lane < HEAD_DIM) if side == 0 else (lane >= HEAD_DIM)
            x_high, x_low = split(jnp.where(mine, scaled[:, here], 0.0))
            x_both = jnp.concatenate([x_high, x_low], axis=1)
            col = cols[:, head : head + 1]
            row = row_ref[0, head : head + 1, :]
            done = []
            for at, over in ((slice(0, half), slice(0, 2 * half)), (slice(half, 2 * half), slice(half, 2 * half))):
                decay = jnp.exp(jnp.minimum(row[:, over] - col[at], 0.0))
                p_high, p_low = split(st_ref[at, over] * decay)
                first = mm(p_high, right[over])
                done.append(first[:, :128] + first[:, 128:] + mm(p_low, dy_high[over]))
                outer = mm_nt(x_both[at], twice[over]) + mm_nt(x_high[at], dy_low[over])
                acc[at, over] += outer * decay
            both.append(jnp.concatenate(done, axis=0))
        dx_ref[:, here] = jnp.where(lane < HEAD_DIM, both[0], both[1])

    if not ends:
        return

    @pl.when(step == pl.num_programs(0) - 1)
    def _():
        dbc_ref = ends[0]
        doc_col = m_ref[:, CONV_K : CONV_K + 1]
        ds = split(acc[...] * same_mask(doc_ref[0:1], doc_col, True))
        dbc_ref[:, :STATE] = three(mm, ds, split(bc_ref[:, STATE:]))
        dbc_ref[:, STATE:] = three(mm_tn, ds, split(bc_ref[:, :STATE]))


def carry_body(
    first, dx_ref, x_ref, dy_ref, pre_ref, in_ref, w_ref, m_ref, bc_ref, r_ref, end_ref, wl_ref, dt_ref,
    skip_ref, db_in, g_in, flow_in, *refs,
):
    extra = refs[:-6]
    d_ref, edge_ref, conv_ref, db_ref, g_ref, flow_ref = refs[-6:]
    if extra:
        pre_bc, in_bc, w_bc, dbc_ref, dc_ref, shifted_ref, rate_ref, q_ref, heads_ref = extra
    step = pl.program_id(0)
    count = INNER // 2 // BLOCK

    @pl.when(step == 0)
    def _():
        db_ref[...] = db_in[...]
        g_ref[...] = g_in[...]
        flow_ref[...] = flow_in[...]

    def conv(d_act, pre, inputs, weight, width):
        sig = sigmoid(pre)
        d_pre = d_act * (sig * (1.0 + pre * (1.0 - sig)))
        d_ext, sums = conv_back(d_pre, inputs, weight, m_ref[...])
        d_ref[:, :width] = d_ext[LEAD:].astype(BF)
        edge_ref[:LEAD, :width] = d_ext[:LEAD]
        edge_ref[LEAD:, :width] = d_ext[d_ext.shape[0] - LEAD :]
        conv_ref[:, :width] = sums

    @pl.when(step < count)
    def _():
        places = head_of_lane((step + first) * BLOCK_HEADS, BLOCK)
        returned = r_ref[0]
        r_parts = split(returned)
        to_end = expand(wl_ref[...], places)
        steps = expand(dt_ref[...], places)
        x = x_ref[...]
        d_scaled = dx_ref[...] + to_end * three(mm, split(bc_ref[:, :STATE]), r_parts)
        g_ref[...] += fold(x * d_scaled, places)
        db_ref[...] += three(mm_nt, split(to_end * steps * x), r_parts)
        flow = jnp.sum(returned * end_ref[0], axis=0, keepdims=True)
        high, middle, low = parts_of(jnp.broadcast_to(flow, (8, BLOCK)))
        flow_ref[...] += mm_nt(high, places) + mm_nt(middle, places) + mm_nt(low, places)
        d_x = steps * d_scaled + skip_ref[...] * dy_ref[...]
        conv(d_x, pre_ref[...], in_ref[...].astype(F32), w_ref[...], BLOCK)

    if not extra:
        return

    @pl.when(step == count)
    def _():
        width = 2 * STATE
        d_bc = jnp.concatenate([dbc_ref[:, :STATE] + db_ref[...], dbc_ref[:, STATE:] + dc_ref[...]], axis=1)
        conv(d_bc, pre_bc[...], in_bc[...].astype(F32), w_bc[...], width)
        masks = m_ref[...]
        steps, rate, shifted = dt_ref[...], rate_ref[...], shifted_ref[...]
        difference = q_ref[...] - steps * g_ref[...]
        d_log = (flow_ref[0:1] + running_sum(difference, True)) * masks[:, CONV_K - 2 : CONV_K - 1]
        d_steps = g_ref[...] - rate * d_log
        d_dt = d_steps * sigmoid(shifted)
        head = lax.broadcasted_iota(jnp.int32, d_dt.shape, 1) < HEADS
        d_dt = jnp.where(head, d_dt, 0.0)
        d_ref[:, width : width + STATE] = d_dt.astype(BF)
        edge_ref[:LEAD, width : width + STATE] = jnp.zeros((LEAD, STATE), F32)
        edge_ref[LEAD:, width : width + STATE] = d_dt[d_dt.shape[0] - LEAD :]
        conv_ref[:, width : width + STATE] = jnp.zeros((8, STATE), F32)
        heads_ref[0:8] = jnp.broadcast_to(jnp.sum(d_dt, axis=0, keepdims=True), (8, STATE))
        log_sum = -jnp.sum(steps * rate * d_log, axis=0, keepdims=True)
        heads_ref[8:16] = jnp.broadcast_to(log_sum, (8, STATE))


def woven(ref, devices, rows):
    pieces = [ref[side, d * rows : d * rows + rows, :] for d in range(devices) for side in range(2)]
    return jnp.concatenate(pieces, axis=0)


def d_final_body(devices, rows, g_ref, w_ref, o_ref):
    o_ref[...] = mm_nt(g_ref[...], woven(w_ref, devices, rows))


def layer_body(devices, rows, f_ref, w_ref, t_ref, o_ref, total):
    @pl.when(pl.program_id(0) == 0)
    def _():
        total[...] = t_ref[...].astype(F32)

    total[...] += mm(f_ref[...], woven(w_ref, devices, rows))

    @pl.when(pl.program_id(0) == pl.num_programs(0) - 1)
    def _():
        o_ref[...] = total[...].astype(BF)


def back_z_body(d_ref, w_ref, o_ref):
    half = w_ref.shape[2]
    o_ref[...] = mm_nt(d_ref[:, :half], w_ref[0]) + mm_nt(d_ref[:, half:], w_ref[1])


def back_x_body(da_ref, db_ref, w_ref, part_ref, o_ref):
    half = da_ref.shape[1]
    o_ref[...] = part_ref[...] + mm_nt(da_ref[...], w_ref[:, :half]) + mm_nt(db_ref[...], w_ref[:, half:])


def back_norm_body(d_ref, x_ref, og_ref, gain_ref, o_ref, sum_ref):
    @pl.when(pl.program_id(0) == 0)
    def _():
        sum_ref[...] = jnp.zeros_like(sum_ref)

    d_normed = d_ref[...]
    x = x_ref[...].astype(F32)
    scale = lax.rsqrt(jnp.mean(x * x, axis=-1, keepdims=True) + EPS)
    unit = x * scale
    pulled = d_normed * gain_ref[...]
    inner = jnp.mean(pulled * unit, axis=-1, keepdims=True)
    o_ref[...] = og_ref[...].astype(F32) + scale * (pulled - unit * inner)
    total = jnp.sum(d_normed * unit, axis=0, keepdims=True)
    sum_ref[...] += jnp.broadcast_to(total, sum_ref.shape)


def swap(array, axis):
    return lax.ppermute(array, axis, [(0, 1), (1, 0)])


def from_behind(array, by):
    peers = lax.axis_size(CTX[0]) * lax.axis_size(CTX[1])
    pairs = [(i, i + by) for i in range(peers) if 0 <= i + by < peers]
    return lax.ppermute(array, CTX, pairs)


def entering(state, decay, reverse, fills):
    fills = list(fills)

    def meanwhile(sent, arrived):
        return tie(arrived, *fills.pop(0)(sent)) if fills else arrived

    depth, width = lax.axis_size("z"), lax.axis_size("y")
    place_z, place_y = lax.axis_index("z"), lax.axis_index("y")
    if width != 2:
        gathered = lax.all_gather(jnp.concatenate([state, decay], axis=1), CTX)
        while fills:
            gathered = meanwhile(state, gathered)
        count = depth * width
        place = place_z * width + place_y
        ahead = count - 1 - place if reverse else place

        def one(lap, running):
            source = count - 1 - lap if reverse else lap
            item = lax.dynamic_index_in_dim(gathered, source, 0, False)
            return item[:, STATE : STATE + 1] * running + item[:, :STATE]

        return lax.fori_loop(0, ahead, one, jnp.zeros_like(state))
    second = place_y == (0 if reverse else 1)
    sent = pick(state, 1 - place_y)
    got = meanwhile(sent, swap(sent, "y"))
    own = pick(state, place_y)
    decay_own = pick(decay, place_y)[:1]
    decay_got = swap(pick(decay, 1 - place_y), "y")[:1]
    early = jnp.where(second, got, own)
    late = jnp.where(second, own, got)
    decay_early = jnp.where(second, decay_got, decay_own)
    decay_late = jnp.where(second, decay_own, decay_got)
    total = decay_late * early + late
    decay_total = decay_early * decay_late
    before = jnp.zeros_like(total)
    sent = total
    turn = depth - 1 - place_z if reverse else place_z
    for hop in range(1, depth):
        pairs = [(depth - hop, depth - 1 - hop)] if reverse else [(hop - 1, hop)]
        arrived = meanwhile(sent, lax.ppermute(sent, "z", pairs))
        before = jnp.where(turn == hop, arrived, before)
        sent = decay_total * before + total
    middle = decay_early * before + early
    mine = jnp.where(second, middle, before)
    sent = jnp.where(second, before, middle)
    theirs = swap(sent, "y")
    while fills:
        theirs = meanwhile(sent, theirs)
    return in_order(mine, theirs, "y")


def pick(parts, index, dim=0):
    return lax.dynamic_index_in_dim(parts, index, dim, False)


def in_order(mine, theirs, axis):
    first = lax.axis_index(axis) == 0
    return jnp.where(first, jnp.stack([mine, theirs]), jnp.stack([theirs, mine]))


def across(array, axis, by):
    return lax.ppermute(array, axis, [(i, i ^ by) for i in range(lax.axis_size(axis))])


def products_body(
    patched, place_ref, sent_own, kept_own, sent_other, kept_other, own_ref, other_ref, *refs
):
    sent_ref, kept_ref = refs[-2:]
    own, other = own_ref[...], other_ref[...]
    if patched:
        upto = own.shape[0] - LEAD
        own = jnp.concatenate([own[:upto], refs[0][...]], axis=0)
        other = jnp.concatenate([other[:upto], refs[1][...]], axis=0)

    def product(first, second):
        first, second = first[...], second[...]
        first = first.reshape(-1, first.shape[-1])
        second = second.reshape(-1, second.shape[-1])
        return mm(first, own) + mm(second, other)

    sent_ref[...] = product(sent_own, sent_other).astype(BF)
    kept_ref[...] = product(kept_own, kept_other)


def products(left, right, start, count, axis, waits):
    own, other = left
    sizes = [lax.axis_size(a) for a in ("x", "z", "y")]
    tokens = own.shape[1]
    rows = other.shape[0] // sizes[0] // sizes[1] // sizes[2]
    out_rows = other.shape[0] // 2
    places = jnp.stack([lax.axis_index(a) for a in ("core", "x", "y")])
    if axis == "x":
        own = own.reshape(2, 2, out_rows, tokens)
        other = other.reshape(2, out_rows, tokens)
        own_block, other_block = (1, 1, out_rows, tokens), (1, out_rows, tokens)

        def spec(mine, flip):
            if mine:
                return pl.BlockSpec(own_block, lambda g, p: (p[1] ^ flip, p[0], 0, 0))
            return pl.BlockSpec(other_block, lambda g, p: (p[1] ^ flip, 0, 0))
    else:
        own = own.reshape(2, 2, sizes[1], 2, rows, tokens)
        other = other.reshape(2 * sizes[1], 2, rows, tokens)
        own_block = (2, 1, sizes[1], 1, rows, tokens)
        other_block = (2 * sizes[1], 1, rows, tokens)

        def spec(mine, flip):
            if mine:
                return pl.BlockSpec(own_block, lambda g, p: (0, p[0], 0, p[2] ^ flip, 0, 0))
            return pl.BlockSpec(other_block, lambda g, p: (0, p[2] ^ flip, 0, 0))

    block = 384 if count % 384 == 0 else 512
    first = start // block
    columns_of = pl.BlockSpec((tokens, block), lambda g, p: (0, g + first))
    edge_of = pl.BlockSpec((LEAD, block), lambda g, p: (0, g + first))
    result = pl.BlockSpec((out_rows, block), lambda g, p: (0, g))
    return call(
        functools.partial(products_body, len(right) > 2), -(-count // block), count * out_rows / 2.0e5,
        [
            (own, spec(True, 1)), (own, spec(True, 0)), (other, spec(False, 1)), (other, spec(False, 0)),
            (right[0], columns_of), (right[1], columns_of),
            *[(edge, edge_of) for edge in right[2:]],
        ],
        [(out((out_rows, count), BF), result), (out((out_rows, count)), result)],
        waits=waits,
        places=places,
    )


def products_any(left, right, start, count, axis):
    core, place = lax.axis_index("core"), lax.axis_index(axis)
    sizes = [lax.axis_size(a) for a in ("x", "z", "y")]
    own = core_rows(left[0], core).reshape(left[1].shape)
    both = jnp.concatenate([own, left[1]], axis=1)
    view = both.reshape(*sizes, -1, both.shape[1])
    if axis == "y":
        view = jnp.moveaxis(view, 2, 0)
    view = view.reshape(view.shape[0], -1, both.shape[1])
    if len(right) > 2:
        upto = right[0].shape[0] - LEAD
        right = [right[0][:upto], right[2], right[1][:upto], right[3]]
    right = jnp.concatenate(right, axis=0)[:, start : start + count]
    sent = [mm(pick(view, place ^ by), right).astype(BF) for by in range(1, view.shape[0])]
    return sent, mm(pick(view, place), right)


def total_of(kept, got):
    for piece in got:
        kept = kept + piece.astype(F32)
    return kept


def tied(value, others):
    return tie(value, *others) if others else value


def xor_parts(parts, axis):
    count, place = lax.axis_size(axis), lax.axis_index(axis)
    return pick(parts, place), [pick(parts, place ^ by).astype(BF) for by in range(1, count)]


def travel(sent, axis, others):
    return [across(tied(piece, others), axis, by + 1) for by, piece in enumerate(sent)]


def places_here():
    return jnp.stack([lax.axis_index(a) for a in ("core", "x", "y")])


def second_body(place_ref, *refs):
    for side in range(2):
        kept_own, got_own, kept_next, got_next = refs[4 * side : 4 * side + 4]
        own_ref, next_ref = refs[8 + 2 * side : 10 + 2 * side]
        own_ref[...] = (kept_own[...] + got_own[...].astype(F32)).reshape(own_ref.shape)
        next_ref[...] = (kept_next[...] + got_next[...].astype(F32)).reshape(next_ref.shape).astype(BF)


def second_stage(kept_x, got_x, kept_y, got_y, depth, waits):
    rows = kept_x.shape[0] // (2 * depth)
    ins, outs = [], []
    for kept, got, by_y in ((kept_x, got_x, True), (kept_y, got_y, False)):
        width = kept.shape[1]
        shape = (depth, 2, rows, width) if by_y else (2, depth, rows, width)

        def spec(flip, by_y=by_y, width=width):
            if by_y:
                return pl.BlockSpec((1, 1, rows, width), lambda g, p: (g, p[2] ^ flip, 0, 0))
            return pl.BlockSpec((1, 1, rows, width), lambda g, p: (p[1] ^ flip, g, 0, 0))

        for flip in (0, 1):
            ins += [(kept.reshape(shape), spec(flip)), (got.reshape(shape), spec(flip))]
        result = pl.BlockSpec((1, rows, width), lambda g, p: (g, 0, 0))
        outs += [(out((depth, rows, width)), result), (out((depth, rows, width), BF), result)]
    return call(second_body, depth, 3, ins, outs, waits=waits, places=places_here())


def third_body(own_x, came_x, own_y, came_y, o_ref):
    width = own_x.shape[2]
    o_ref[:, :, :width] = (own_x[...] + came_x[...].astype(F32)).astype(o_ref.dtype)
    o_ref[:, :, width:] = (own_y[...] + came_y[...].astype(F32)).astype(o_ref.dtype)


def third_stage(own_x, came_x, own_y, came_y, kind, waits):
    depth, rows, wide_x = own_x.shape
    wide_y = own_y.shape[2]

    def spec(width):
        return pl.BlockSpec((1, rows, width), lambda g: (g, 0, 0))

    return call(
        third_body, depth, 2,
        [(own_x, spec(wide_x)), (came_x, spec(wide_x)), (own_y, spec(wide_y)), (came_y, spec(wide_y))],
        [(out((depth, rows, wide_x + wide_y), kind), spec(wide_x + wide_y))],
        waits=waits,
    )[0]


class Reduction:
    def __init__(self, left, right, start, middle, end, waits=()):
        if lax.axis_size("x") == 2 and lax.axis_size("y") == 2:
            sent_x, self.kept_x = products(left, right, start, middle - start, "x", waits)
            sent_y, self.kept_y = products(left, right, middle, end - middle, "y", waits)
            self.sent_x, self.sent_y = [sent_x], [sent_y]
        else:
            self.sent_x, self.kept_x = products_any(left, right, start, middle - start, "x")
            self.sent_y, self.kept_y = products_any(left, right, middle, end - middle, "y")

    def made(self):
        return [self.kept_x, self.kept_y, *self.sent_x, *self.sent_y]

    def launch(self, *others):
        self.got_x = travel(self.sent_x, "x", others)
        self.got_y = travel(self.sent_y, "y", others)

    def second(self, *others):
        sizes = [lax.axis_size(a) for a in ("x", "z", "y")]
        self.pairs = sizes[0] == 2 and sizes[2] == 2
        if self.pairs:
            self.own_x, next_x, self.own_y, next_y = second_stage(
                self.kept_x, self.got_x[0], self.kept_y, self.got_y[0], sizes[1], others
            )
            self.next_x, self.next_y = [next_x], [next_y]
            self.came_x = travel(self.next_x, "y", ())
            self.came_y = travel(self.next_y, "x", ())
            return
        part_x = total_of(tied(self.kept_x, others), self.got_x)
        part_y = total_of(tied(self.kept_y, others), self.got_y)
        view_x = part_x.reshape(sizes[1], sizes[2], -1, part_x.shape[1])
        view_y = part_y.reshape(sizes[0], sizes[1], -1, part_y.shape[1])
        self.own_x, self.next_x = xor_parts(jnp.moveaxis(view_x, 1, 0), "y")
        self.own_y, self.next_y = xor_parts(view_y, "x")
        self.came_x = travel(self.next_x, "y", ())
        self.came_y = travel(self.next_y, "x", ())

    def third(self, *others, kind=F32):
        place = lax.axis_index("z")
        if self.pairs:
            self.parts = third_stage(
                self.own_x, self.came_x[0], self.own_y, self.came_y[0], kind, others
            )
        else:
            done_x = total_of(tied(self.own_x, others), self.came_x)
            done_y = total_of(tied(self.own_y, others), self.came_y)
            self.parts = jnp.concatenate([done_x, done_y], axis=2).astype(kind)
        self.mine = None
        if kind == BF:
            sides = ((self.own_x, self.came_x), (self.own_y, self.came_y))
            self.mine = jnp.concatenate(
                [total_of(pick(own, place), [pick(c, place) for c in came]) for own, came in sides], axis=1
            )
        self.got_z = lax.all_to_all(self.parts, "z", 0, 0, tiled=True)

    def last(self, *others):
        got = tied(self.got_z, others)
        if self.mine is None:
            return jnp.sum(got, axis=0)
        others_only = lax.broadcasted_iota(jnp.int32, got.shape, 0) != lax.axis_index("z")
        return self.mine + jnp.sum(jnp.where(others_only, got.astype(F32), 0.0), axis=0)


def core_rows(turned, core):
    view = turned.reshape(lax.axis_size("x"), 2, -1, turned.shape[1])
    return pick(view, core, 1)


def both_cores(turned, core):
    theirs = core_rows(turned, 1 - core)
    return turned, swap(theirs.reshape(-1, turned.shape[1]), "core")


def document_ids(lengths, positions):
    first_end = lengths[0]
    second_end = lengths[0] + lengths[1]
    inside = (positions >= first_end).astype(jnp.int32) + (positions >= second_end).astype(jnp.int32)
    return jnp.where(positions < 0, -1, inside)


def gather_small(pieces, count):
    flat = jnp.concatenate([piece.reshape(-1) for piece in pieces])
    spread = jnp.broadcast_to(flat[None], (count, flat.shape[0]))
    return lax.all_to_all(spread, EVERY, 0, 0, tiled=True)


def columns(array, width):
    return jnp.pad(array, ((0, 0), (0, width - array.shape[1])))


def shards(
    tokens, out_grad, seq_lengths, norm_gain, in_weight, conv_weight, conv_bias,
    dt_bias, a_log, skip_gain, gated_gain, out_weight,
):
    count = 1
    for axis in EVERY:
        count *= lax.axis_size(axis)
    core = lax.axis_index("core")
    place = lax.axis_index("z") * lax.axis_size("y") + lax.axis_index("y")
    row_count, width = tokens.shape
    first_row = place * row_count
    full_rows = LEAD + row_count
    half = INNER // 2
    bc_width = CONVW - INNER
    square = (row_count, row_count)

    lead_tokens = from_behind(tokens[row_count - LEAD :], 1)
    small = gather_small([norm_gain, conv_weight, conv_bias, gated_gain], count)
    weight_x = lax.all_gather(columns(in_weight[:, INNER:], PROJ_X), EVERY, axis=0, tiled=True)
    rows_out = out_weight.shape[0] // 2
    stacked = jnp.stack(
        [in_weight[:, :half], in_weight[:, half:INNER], out_weight[:rows_out], out_weight[rows_out:]]
    )
    stacked = lax.all_gather(stacked, EVERY, axis=1, tiled=True)
    cuts = [norm_gain.size, conv_weight.size, conv_bias.size]
    cuts = [sum(cuts[: i + 1]) for i in range(3)]
    gain_piece, conv_piece, bias_piece, gated_piece = jnp.split(small, cuts, axis=1)
    full_gain = gain_piece.reshape(1, -1).astype(F32)
    full_conv = jnp.moveaxis(conv_piece.reshape(count, CONV_K, -1), 1, 0).reshape(CONV_K, -1)
    full_conv = jnp.pad(full_conv.astype(F32), ((0, 4), (0, 0)))
    full_bias = bias_piece.reshape(1, -1).astype(F32)
    full_gated = gated_piece.reshape(1, -1).astype(F32)

    normed_ext, turned = call(
        norm_body, 1, 4,
        [
            (lead_tokens, whole(LEAD, width)),
            (tokens, whole(row_count, width)),
            (full_gain, whole(1, width)),
        ],
        [
            (out((full_rows, width), BF), whole(full_rows, width)),
            (out((width, row_count), BF), whole(width, row_count)),
        ],
    )
    normed = normed_ext[LEAD:]
    normed_left = both_cores(turned, core)
    out_grad_theirs = swap(out_grad, "core")

    lengths = seq_lengths[0]
    ordinal = jnp.arange(row_count, dtype=jnp.int32)
    doc_ids = document_ids(lengths, first_row + ordinal)
    doc_before = document_ids(lengths, first_row - 1 + jnp.zeros((1,), jnp.int32))
    marks = [
        document_ids(lengths, first_row + ordinal - (CONV_K - 1 - tap)) == doc_ids
        for tap in range(CONV_K)
    ]
    marks = marks + [doc_ids, doc_ids == doc_before[0], doc_ids == doc_ids[row_count - 1]]
    masks = columns(jnp.stack([mark.astype(F32) for mark in marks], axis=1), 128)
    doc_rows = jnp.broadcast_to(doc_ids.astype(F32)[None], (8, row_count))
    rate = columns(jnp.exp(a_log)[None], 128)
    shift = columns(dt_bias[None], 128)
    skip_wide = jnp.repeat(skip_gain, HEAD_DIM)[None]
    mixed_x = mm(normed_ext, weight_x).astype(BF)

    block_bc = pl.BlockSpec((full_rows, bc_width), lambda g: (0, INNER // bc_width))
    block_dr = pl.BlockSpec((full_rows, 128), lambda g: (0, CONVW // 128))
    per_token = whole(row_count, 128)
    a_token = (out((row_count, 128)), per_token)
    pre_bc, act_bc, act_t, scores, scores_t, steps, enter, to_end, cumulative, cum_turned, shifted = call(
        prep_bc_body, 1, 6,
        [
            (mixed_x, block_bc),
            (mixed_x, block_dr),
            (full_conv[:, INNER:], whole(8, bc_width)),
            (full_bias[:, INNER:], whole(1, bc_width)),
            (masks, per_token),
            (doc_rows, whole(8, row_count)),
            (shift, whole(1, 128)),
            (rate, whole(1, 128)),
        ],
        [
            (out((row_count, bc_width)), whole(row_count, bc_width)),
            (out((row_count, bc_width)), whole(row_count, bc_width)),
            (out((bc_width, row_count)), whole(bc_width, row_count)),
            (out(square), whole(*square)),
            (out(square), whole(*square)),
            a_token, a_token, a_token, a_token,
            (out((128, row_count)), whole(128, row_count)),
            a_token,
        ],
    )
    pre_x, act_x, state_local, device_decay = call(
        prep_x_body, INNER // BLOCK, 12,
        [
            (mixed_x, lanes(full_rows, BLOCK)),
            (full_conv[:, :INNER], lanes(8, BLOCK)),
            (full_bias[:, :INNER], lanes(1, BLOCK)),
            (masks, per_token),
            (to_end, per_token),
            (steps, per_token),
            (enter, per_token),
            (act_t, whole(bc_width, row_count)),
        ],
        [
            (out((row_count, INNER)), lanes(row_count, BLOCK)),
            (out((row_count, INNER)), lanes(row_count, BLOCK)),
            (out((2, STATE, half)), halves(STATE, BLOCK)),
            (out((2, 8, half)), halves(8, BLOCK)),
        ],
    )

    heads_block = 2 * PAIRS
    groups = HEADS // heads_block
    half_groups = groups // 2
    cum_rows = cum_turned[:HEADS].reshape(groups, heads_block, row_count)
    kept = {}

    def pairs_at(index):
        return pl.BlockSpec((row_count, PAIR_LANES), lambda g: (0, g + index * half_groups))

    def cums_at(index):
        return pl.BlockSpec((1, heads_block, row_count), lambda g: (g + index * half_groups, 0, 0))

    def intra(index, wait):
        kept[index] = call(
            functools.partial(intra_body, index * half_groups), half_groups, 12,
            [
                (act_x, pairs_at(index)),
                (steps, per_token),
                (skip_wide, pl.BlockSpec((1, PAIR_LANES), lambda g: (0, g + index * half_groups))),
                (scores, whole(*square)),
                (cumulative, per_token),
                (cum_rows, cums_at(index)),
            ],
            [(out((row_count, half)), lanes(row_count, PAIR_LANES))],
            waits=[wait],
        )[0]
        return [kept[index]]

    devices = 4
    out_block = 2 * devices * rows_out
    out_blocks = count // devices
    weight_block = pl.BlockSpec((2, devices * rows_out, width), lambda g: (1, g, 0))
    direct = rows_out % 16 == 0

    def project_z(wait):
        kept["mixed_z"] = [mm(normed, stacked[side]).astype(BF) for side in range(2)]
        return kept["mixed_z"]

    def project(wait):
        if direct:
            kept["d_final"] = call(
                functools.partial(d_final_body, devices, rows_out), out_blocks, 7,
                [(out_grad, whole(row_count, width)), (stacked, weight_block)],
                [(out((row_count, INNER)), lanes(row_count, out_block))],
                waits=[wait],
            )[0]
        else:
            weight_o = jnp.moveaxis(stacked[2:].reshape(2, count, rows_out, width), 0, 1)
            kept["weight_o"] = weight_o.reshape(-1, width)
            kept["d_final"] = mm_nt(out_grad, kept["weight_o"])
        return [kept["d_final"]]

    state_in = entering(
        state_local, device_decay, False,
        [
            lambda wait: intra(0, wait), lambda wait: intra(1, wait), lambda wait: [], project_z,
            project,
        ],
    )
    state_end = device_decay[:, :1] * state_in + state_local

    tile = 128
    final, final_turned, d_z, d_y, returned_local, d_c_carry, dy_y, sums = call(
        gate_body, row_count // tile, 31,
        [
            (kept[0], rows_of(tile, half)),
            (kept[1], rows_of(tile, half)),
            (kept["mixed_z"][0], rows_of(tile, half)),
            (kept["mixed_z"][1], rows_of(tile, half)),
            (kept["d_final"], rows_of(tile, INNER)),
            (act_x, rows_of(tile, INNER)),
            (act_bc[:, STATE:], rows_of(tile, STATE)),
            (act_t[STATE:], lanes(STATE, tile)),
            (state_in, whole(2, STATE, half)),
            (enter, rows_of(tile, 128)),
            (full_gated, whole(1, INNER)),
            (skip_wide, whole(1, INNER)),
        ],
        [
            (out((row_count, INNER), BF), rows_of(tile, INNER)),
            (out((INNER, row_count), BF), lanes(INNER, tile)),
            (out((row_count, INNER), BF), rows_of(tile, INNER)),
            (out((row_count, INNER)), rows_of(tile, INNER)),
            (out((2, STATE, half)), whole(2, STATE, half)),
            (out((row_count, STATE)), rows_of(tile, STATE)),
            (out((row_count, 128)), rows_of(tile, 128)),
            (out((16, INNER)), whole(16, INNER)),
        ],
        [pltpu.VMEM((tile, INNER), F32), pltpu.VMEM((tile, INNER), F32)],
    )

    final_left = both_cores(final_turned, core)
    d_z_theirs = swap(d_z, "core")
    back = {"acc": jnp.zeros(square, F32)}

    def out_sums(wait):
        back["out"] = Reduction(final_left, [out_grad, out_grad_theirs], 0, width // 2, width, [wait])
        back["out"].launch()
        return back["out"].made()

    def z_sums(wait):
        back["z"] = Reduction(normed_left, [d_z, d_z_theirs], 0, half, INNER, [wait])
        back["z"].launch()
        return back["z"].made()

    def within(index, wait):
        ends = [(out((row_count, bc_width)), whole(row_count, bc_width))] if index else []
        back[index], back["acc"], *back["bc"] = call(
            functools.partial(back_body, index * half_groups), half_groups, 18,
            [
                (act_x, pairs_at(index)),
                (d_y, pairs_at(index)),
                (steps, per_token),
                (scores_t, whole(*square)),
                (cumulative, per_token),
                (cum_rows, cums_at(index)),
                (act_bc, whole(row_count, bc_width)),
                (doc_rows, whole(8, row_count)),
                (masks, per_token),
                (back["acc"], whole(*square)),
            ],
            [
                (out((row_count, half)), lanes(row_count, PAIR_LANES)),
                (out(square), whole(*square)),
                *ends,
            ],
            waits=[wait],
        )
        return [back[index]]

    def first_within(wait):
        back["z"].second(wait)
        return within(0, wait)

    def second_within(wait):
        return within(1, wait)

    norm_block = 256

    def send_out(wait):
        back["out"].second(wait)
        back["z"].third(wait)
        return [back["z"].parts, *back["out"].next_x, *back["out"].next_y]

    returned = entering(
        returned_local, device_decay, True,
        [z_sums, out_sums, first_within, second_within, send_out],
    )

    blocks = half // BLOCK

    def carried(index, earlier, extra, extra_out, waits):
        steps_count = blocks + len(extra_out)
        own = pl.BlockSpec((row_count, BLOCK), lambda g: (0, jnp.minimum(g, blocks - 1)))

        def at(rows):
            return pl.BlockSpec((rows, BLOCK), lambda g: (0, jnp.minimum(g, blocks - 1) + index * blocks))

        state_at = pl.BlockSpec((1, STATE, BLOCK), lambda g: (index, 0, jnp.minimum(g, blocks - 1)))
        wide = half + len(extra_out) * (PROJ_X - INNER)
        return call(
            functools.partial(carry_body, index * blocks), steps_count, 14 + 4 * index,
            [
                (back[index], own),
                (act_x, at(row_count)),
                (d_y, at(row_count)),
                (pre_x, at(row_count)),
                (mixed_x, at(full_rows)),
                (full_conv[:, :INNER], at(8)),
                (masks, per_token),
                (act_bc, whole(row_count, bc_width)),
                (returned, state_at),
                (state_end, state_at),
                (to_end, per_token),
                (steps, per_token),
                (skip_wide, at(1)),
                *[(array, whole(*array.shape)) for array in earlier],
                *extra,
            ],
            [
                *extra_out,
                (out((row_count, wide), BF), lanes(row_count, BLOCK)),
                (out((2 * LEAD, wide)), lanes(2 * LEAD, BLOCK)),
                (out((8, wide)), lanes(8, BLOCK)),
                (out((row_count, STATE)), whole(row_count, STATE)),
                a_token,
                (out((8, 128)), whole(8, 128)),
            ],
            waits=waits,
        )

    none = jnp.zeros((row_count, 128), F32)
    d_xa, edge_a, conv_a, *so_far = carried(0, [none, none, none[:8]], [], [], [])
    back["out"].third(edge_a)
    d_xa_theirs = swap(d_xa, "core")
    halo_a = from_behind(edge_a[:LEAD], -1)
    last_a = (edge_a[LEAD:] + halo_a).astype(BF)
    last_a_theirs = swap(last_a, "core")
    sums_a = Reduction(normed_left, [d_xa, d_xa_theirs, last_a, last_a_theirs], 0, half // 2, half, [back["out"].parts, back["z"].got_z])
    sums_a.launch()
    heads, d_xb, edge_b, conv_b, *_ = carried(
        1, so_far,
        [
            (pre_bc, whole(row_count, bc_width)),
            (mixed_x, block_bc),
            (full_conv[:, INNER:], whole(8, bc_width)),
            (back["bc"][0], whole(row_count, bc_width)),
            (d_c_carry, whole(row_count, STATE)),
            (shifted, per_token),
            (rate, whole(1, 128)),
            (dy_y, per_token),
        ],
        [(out((16, 128)), whole(16, 128))],
        sums_a.made(),
    )
    d_xb_theirs = swap(d_xb, "core")
    halo_b = from_behind(edge_b[:LEAD], -1)
    sums_a.second(edge_b)
    sums_a.third()
    d_normed_z = call(
        back_z_body, width // norm_block, 10,
        [
            (d_z, whole(row_count, INNER)),
            (stacked, pl.BlockSpec((2, norm_block, half), lambda g: (0, g, 0))),
        ],
        [(out((row_count, width)), lanes(row_count, norm_block))],
        waits=[edge_b],
    )[0]
    last_b = (edge_b[LEAD:] + tie(halo_b, d_normed_z)).astype(BF)
    last_b_theirs = swap(last_b, "core")
    wide_b = d_xb.shape[1]
    sums_b = Reduction(
        normed_left, [d_xb, d_xb_theirs, last_b, last_b_theirs], 0, 1024, wide_b, [sums_a.parts]
    )
    sums_b.launch()

    d_xa = lax.dynamic_update_slice(d_xa, last_a, (row_count - LEAD, 0))
    d_xb = lax.dynamic_update_slice(d_xb, last_b, (row_count - LEAD, 0))
    d_normed = call(
        back_x_body, width // norm_block, 10,
        [
            (d_xa, whole(row_count, half)),
            (d_xb, whole(row_count, wide_b)),
            (weight_x, rows_of(norm_block, PROJ_X)),
            (d_normed_z, lanes(row_count, norm_block)),
        ],
        [(out((row_count, width)), lanes(row_count, norm_block))],
        waits=sums_b.made(),
    )[0]
    grad_tokens, gain_sums = call(
        back_norm_body, row_count // tile, 4,
        [
            (d_normed, rows_of(tile, width)),
            (tokens, rows_of(tile, width)),
            (out_grad, rows_of(tile, width)),
            (full_gain, whole(1, width)),
        ],
        [
            (out((row_count, width)), rows_of(tile, width)),
            (out((8, width)), whole(8, width)),
        ],
    )
    sums_b.second(grad_tokens)
    if direct:
        layer_out = call(
            functools.partial(layer_body, devices, rows_out), out_blocks, 13,
            [
                (final, lanes(row_count, out_block)),
                (stacked, weight_block),
                (tokens, whole(row_count, width)),
            ],
            [(out((row_count, width), BF), whole(row_count, width))],
            [pltpu.VMEM((row_count, width), F32)],
            waits=[*sums_b.next_x, *sums_b.next_y],
        )[0]
    else:
        layer_out = (tokens.astype(F32) + mm(final, kept["weight_o"])).astype(BF)

    conv_sums = jnp.concatenate([conv_a, conv_b[:, : CONVW - half]], axis=1)
    grad_skip = jnp.sum(jnp.sum(sums[8:], axis=0).reshape(HEADS, HEAD_DIM), axis=1)
    grad_gated = jnp.sum(sums[:8], axis=0)
    per_device = jnp.concatenate(
        [
            gain_sums[0].reshape(count, -1),
            jnp.moveaxis(conv_sums[:CONV_K].reshape(CONV_K, count, -1), 1, 0).reshape(count, -1),
            conv_sums[CONV_K].reshape(count, -1),
            grad_gated.reshape(count, -1),
            jnp.broadcast_to(
                jnp.concatenate([heads[0, :HEADS], heads[8, :HEADS], grad_skip])[None],
                (count, 3 * HEADS),
            ),
        ],
        axis=1,
    )
    sums_b.third(kind=BF)
    per_device = tie(per_device, *sums_b.next_x, *sums_b.next_y)
    arrived = lax.all_to_all(per_device, EVERY, 0, 0, tiled=True)
    done = [layer_out]
    sum_out, sum_in_z, sum_in_a = [each.last(*done) for each in (back["out"], back["z"], sums_a)]
    sum_in_b = sums_b.last()
    small_sums = jnp.sum(tie(arrived, layer_out), axis=0)
    cuts = [norm_gain.size, conv_weight.size, conv_bias.size, gated_gain.size, HEADS, HEADS]
    cuts = [sum(cuts[: i + 1]) for i in range(6)]
    sum_gain, sum_conv, sum_bias, sum_gated, sum_dt, sum_log, sum_skip = jnp.split(small_sums, cuts)
    sum_in = jnp.concatenate([sum_in_z, sum_in_a, sum_in_b[:, : in_weight.shape[1] - INNER - half]], axis=1)
    return (
        layer_out,
        grad_tokens,
        sum_gain,
        sum_in,
        sum_conv.reshape(conv_weight.shape),
        sum_bias,
        sum_dt,
        sum_log,
        sum_skip,
        sum_gated,
        sum_out,
    )


def solution(mesh):
    x = mesh.shape["dp"] // 2
    y = x
    z = mesh.shape["ctx"] // y
    fine = Mesh(mesh.devices.reshape(x, 2, z, y), EVERY)
    rows = P(EVERY, None)
    flat = P(EVERY)
    in_specs = (
        rows, rows, P(("x", "core"), None), flat, rows, P(None, EVERY), flat,
        P(), P(), P(), flat, rows,
    )
    out_specs = (rows, rows, flat, rows, P(None, EVERY), flat, P(), P(), P(), flat, rows)
    return jax.shard_map(shards, mesh=fine, in_specs=in_specs, out_specs=out_specs, check_vma=False)
```
